32 devices in a mesh: wide: 8 (over z, y), narrow: 4 (over x, core).
Axes of the slice: x: 2, y: 2, z: 4, core: 2. Of those that a mesh axis runs over, the one named last changes fastest.
Arguments:
- slab: bfloat16 [6144, 2048], P('wide', 'narrow'), may hold values from -1.1953125 to 1.1953125
- occupation: float32 [4096], replicated, may hold values from 0.02 to 2
- column_band: int32 [2048], P('narrow'), may hold values from 0 to 4095
- pattern: int32 [48, 12], P('wide'), may hold values from 0 to 47, as said below
Outputs:
- density: bfloat16 [48, 12, 128, 128], P('wide', 'narrow')
The draws below stay inside these ranges and needn't reach their ends.
Inputs may be any that keep to these rules, and one draw needn't show every extreme that they name: `pattern`: each row c lists 12 different clusters, each equal to (c + d) mod 48 with -8 <= d <= 8; d = -8 and d = 8 appear in every row.
All inputs are finite; a program needn't handle non-finite values.
Results may differ from the reference program's by a relative error of at most 0.015.
Values may be sent and summed in bfloat16 or wider, within the bound.
No kernel may reach another device: no remote copies, remote signals or barrier semaphores. Data moves between devices by JAX's collectives and lax.ppermute only.
A program may use at most 64 MiB of HBM per device.

```python
import math
import jax
import jax.numpy as jnp
from jax import lax

B = 128
K = 2048
NBAND = 4096
NNB = 12
REACH = 8
NCL = 48
ORB = 6144
N_NARROW = 4


def draw_pattern(key, part):
    key = jax.random.fold_in(key, 7)
    keys = jax.random.split(key, NCL)
    inner = jax.vmap(lambda k: jax.random.permutation(k, 2 * REACH - 1))(keys)
    inner = inner[:, :NNB - 2] - (REACH - 1)
    edges = jnp.broadcast_to(jnp.array([-REACH, REACH], dtype=jnp.int32), (NCL, 2))
    offsets = jnp.concatenate([edges, inner.astype(jnp.int32)], axis=1)
    rows = jnp.arange(NCL, dtype=jnp.int32)[:, None]
    return ((rows + offsets) % NCL).astype(jnp.int32)


def with_ends(values, stream_key, least, top_value):
    spot = [jax.random.randint(jax.random.fold_in(stream_key, axis), (), 0, length) for axis, length in enumerate(values.shape)]
    main_axis = values.shape.index(max(values.shape))
    beside = spot[:main_axis] + [(spot[main_axis] + 1) % values.shape[main_axis]] + spot[main_axis + 1:]
    return values.at[tuple(spot)].set(least).at[tuple(beside)].set(top_value)


def level_of(key, shape, cuts, least, high):
    def one(axis_at, shards_of):
        steps = jax.random.uniform(jax.random.fold_in(jax.random.fold_in(key, 6), axis_at), (shards_of,), jnp.float32, least / len(cuts), high / len(cuts))
        return jnp.repeat(jnp.exp(steps), shape[axis_at] // shards_of).reshape((-1,) + (1,) * (len(shape) - axis_at - 1))

    gain = one(*cuts[0])
    for cut in cuts[1:]:
        gain = gain * one(*cut)
    return gain


def gaussian(key, shape, spread, most, shards=(), kind=jnp.bfloat16):
    drawn = jax.random.normal(key, shape, jnp.float32) * spread
    if len(shards) > 0:
        drawn = level_of(key, shape, shards, -0.22, 0.18) * drawn
    return jnp.clip(drawn, min=-most, max=most).astype(kind)


def setup_inputs(seed: int = 0) -> dict:
    splits = jax.random.split(jax.random.key(seed), 5)
    slab = gaussian(splits[0], (ORB, K), 0.2, 1.1953125, ((0, 8), (1, 4)))
    occupation = jnp.clip(jnp.exp(jax.random.uniform(splits[1], (NBAND,), jnp.float32, math.log(0.02), math.log(2.0))), 0.02, 2.0)
    column_band = with_ends(jax.random.randint(splits[2], (K,), 0, NBAND), jax.random.fold_in(splits[2], 1), 0, NBAND - 1).astype(jnp.int32)
    pattern = draw_pattern(jax.random.fold_in(splits[4], 71), 0)
    return {"slab": slab, "occupation": occupation, "column_band": column_band, "pattern": pattern}


def reference(slab, occupation, column_band, pattern):
    picks = column_band[:, None] == jnp.arange(NBAND, dtype=jnp.int32)[None, :]
    weight = jnp.sum(jnp.where(picks, occupation[None, :], jnp.float32(0.0)), axis=1)
    scaled = (slab.astype(jnp.float32) * weight[None, :]).astype(jnp.bfloat16)
    quarter = K // N_NARROW
    left_all = scaled.reshape(NCL, B, N_NARROW, quarter)
    right_all = slab.reshape(NCL, B, N_NARROW, quarter)

    def one_cluster(c):
        left = left_all[c].astype(jnp.float32)
        right = jnp.take(right_all, pattern[c], axis=0).astype(jnp.float32)
        parts = jnp.einsum("iqk,njqk->qnij", left, right).astype(jnp.bfloat16)
        return jnp.sum(parts.astype(jnp.float32), axis=0).astype(jnp.bfloat16)

    return lax.map(one_cluster, jnp.arange(NCL, dtype=jnp.int32))
```

```python
import functools

import jax
import jax.numpy as jnp
from jax import lax
from jax.experimental import pallas as pl
from jax.experimental.pallas import tpu as pltpu
from jax.sharding import PartitionSpec as P

B = 128
REACH = 8


def from_behind(value, axis, steps):
    count = lax.axis_size(axis)
    pairs = [(source, (source + steps) % count) for source in range(count)]
    return lax.ppermute(value, axis, pairs)


def swap(value, axis, mask):
    count = lax.axis_size(axis)
    return lax.ppermute(value, axis, [(source, source ^ mask) for source in range(count)])


def blocks_kernel(cl, clusters, share, sizes, pattern, left, *refs):
    pieces = refs[: len(sizes)]
    outs = refs[len(sizes) : len(sizes) + 4]
    window, dense = refs[len(sizes) + 4 :]
    at = 0
    for piece, rows in zip(pieces, sizes):
        window[at : at + rows, :] = piece[...]
        at += rows
    span = at // B
    for pair in range(span // 2):
        low, high = 2 * pair, 2 * pair + 1
        c0, c1 = max(0, low - 2 * REACH), min(cl - 1, high)
        product = lax.dot_general(
            left[c0 * B : (c1 + 1) * B, :],
            window[low * B : (high + 1) * B, :],
            (((1,), (1,)), ((), ())),
            preferred_element_type=jnp.float32,
        ).astype(jnp.bfloat16)
        for c in range(c0, c1 + 1):
            part = product[(c - c0) * B : (c - c0 + 1) * B, :]
            dense[c, low] = part[:, :B]
            dense[c, high] = part[:, B:]
    base = lax.axis_index("wide") * cl - REACH
    me = lax.axis_index("narrow")
    for out, mask in zip(outs, (3, 1, 2, 0)):
        slot0 = (me ^ mask) * share
        for c in range(cl):
            for s in range(share):
                where = lax.rem(pattern[c, slot0 + s] - base + clusters, clusters)
                out[c, s] = dense[c, where]


def per_device(slab, occupation, column_band, pattern):
    cl = slab.shape[0] // B
    cols = slab.shape[1]
    clusters = cl * lax.axis_size("wide")
    share = pattern.shape[1] // lax.axis_size("narrow")
    hops = -(-REACH // cl)
    takes = [min(cl, REACH - (s - 1) * cl) for s in range(1, hops + 1)]
    behind = [
        from_behind(slab[(cl - take) * B :], "wide", s + 1) for s, take in enumerate(takes)
    ]
    ahead = [from_behind(slab[: take * B], "wide", -s - 1) for s, take in enumerate(takes)]
    picks = column_band[:, None] == jnp.arange(occupation.shape[0], dtype=jnp.int32)[None, :]
    weight = jnp.sum(jnp.where(picks, occupation[None, :], jnp.float32(0.0)), axis=1)
    scaled = (slab.astype(jnp.float32) * weight[None, :]).astype(jnp.bfloat16)

    pieces = behind[::-1] + [slab] + ahead
    sizes = [piece.shape[0] for piece in pieces]
    span = sum(sizes) // B
    vmem = pl.BlockSpec(memory_space=pltpu.VMEM)
    share_shape = jax.ShapeDtypeStruct((cl, share, B, B), jnp.bfloat16)
    send_far, send_near, keep_far, keep_near = pl.pallas_call(
        functools.partial(blocks_kernel, cl, clusters, share, sizes),
        out_shape=[share_shape] * 4,
        in_specs=[pl.BlockSpec(memory_space=pltpu.SMEM)] + [vmem] * (1 + len(pieces)),
        out_specs=[vmem] * 4,
        scratch_shapes=[
            pltpu.VMEM((span * B, cols), jnp.bfloat16),
            pltpu.VMEM((cl, span, B, B), jnp.bfloat16),
        ],
        compiler_params=pltpu.CompilerParams(vmem_limit_bytes=40 * 1024 * 1024),
        name="blocks",
    )(pattern, scaled, *pieces)
    got_far = swap(send_far, "narrow", 1)
    got_near = swap(send_near, "narrow", 1)
    far = (keep_far.astype(jnp.float32) + got_far.astype(jnp.float32)).astype(jnp.bfloat16)
    got = swap(far, "narrow", 2)
    near = keep_near.astype(jnp.float32) + got_near.astype(jnp.float32)
    return (near + got.astype(jnp.float32)).astype(jnp.bfloat16)


def solution(mesh):
    placed = (P("wide", "narrow"), P(), P("narrow"), P("wide", None))
    return jax.shard_map(
        per_device,
        mesh=mesh,
        in_specs=placed,
        out_specs=P("wide", "narrow", None, None),
        check_vma=False,
    )
```

```python
import functools

import jax
import jax.numpy as jnp
from jax import lax
from jax.experimental import pallas as pl
from jax.experimental.pallas import tpu as pltpu
from jax.sharding import PartitionSpec as P

B = 128
REACH = 8
CL = 6
PAIR = 2
VMEM = pl.BlockSpec(memory_space=pltpu.VMEM)
SMEM = pl.BlockSpec(memory_space=pltpu.SMEM)
LIMIT = 40 * 1024 * 1024
SHORT = pl.CostEstimate(flops=1, bytes_accessed=1, transcendentals=0)


def move(value, axis, target):
    count = lax.axis_size(axis)
    return lax.ppermute(value, axis, [(s, target(s) % count) for s in range(count)])


def outward(w):
    return w + 2 if w % 2 == 0 else w - 2


def inward(w):
    return w - 2 if w % 2 == 0 else w + 2


def blocks_kernel(clusters, share, marks, first, last, pattern, left, own, after, *refs):
    pieces = refs[: len(marks)]
    outs = refs[len(marks) : len(marks) + 4]
    dense = refs[len(marks) + 4]
    wide = lax.axis_index("wide")
    me = lax.axis_index("narrow")
    odd = lax.rem(wide, 2)

    def natural(low, high):
        return jnp.where(odd == 1, low, CL - 1 - high)

    def multiply(rows, offset, c0, c1):
        count = c1 - c0 + 1
        start = natural(c0, c1)
        product = lax.dot_general(
            left[pl.ds(pl.multiple_of(start * B, B), count * B), :],
            rows,
            (((1,), (1,)), ((), ())),
            preferred_element_type=jnp.float32,
        ).astype(jnp.bfloat16)
        for r in range(count):
            for h in range(PAIR):
                dense[start + r, offset + REACH + h] = product[r * B : (r + 1) * B, h * B : (h + 1) * B]

    for offset in range(0, CL, PAIR):
        multiply(own[offset * B : (offset + PAIR) * B, :], offset, first, last)
    for piece, mark in zip(pieces, marks):
        c0, c1 = max(first, mark - REACH), min(last, mark + PAIR - 1 + REACH)
        multiply(piece[...], natural(mark, mark + PAIR - 1), c0, c1)

    base = wide * CL - REACH
    start = natural(first, last)
    for out, mask in zip(outs, (3, 1, 2, 0)):
        slot0 = (me ^ mask) * share
        for r in range(last - first + 1):
            for s in range(share):
                where = lax.rem(pattern[start + r, slot0 + s] - base + clusters, clusters)
                out[r, s] = dense[start + r, where]


def blocks(clusters, share, first, last, pattern, left, own, window, after):
    marks = [m for m in window if m + PAIR - 1 >= first - REACH and m <= last + REACH]
    shape = jax.ShapeDtypeStruct((last - first + 1, share, B, B), jnp.bfloat16)
    return pl.pallas_call(
        functools.partial(blocks_kernel, clusters, share, marks, first, last),
        out_shape=[shape] * 4,
        in_specs=[SMEM, VMEM, VMEM, pl.BlockSpec(memory_space=pl.ANY)] + [VMEM] * len(marks),
        out_specs=[VMEM] * 4,
        scratch_shapes=[pltpu.VMEM((CL, CL + 2 * REACH, B, B), jnp.bfloat16)],
        compiler_params=pltpu.CompilerParams(vmem_limit_bytes=LIMIT),
        cost_estimate=SHORT,
        name=f"blocks_{first}_{last}",
    )(pattern, left, own, after, *[window[m] for m in marks])


def finish_kernel(chunks, *refs):
    out = refs[-1]
    odd = lax.rem(lax.axis_index("wide"), 2)
    for at, (first, last) in enumerate(chunks):
        near, got_near, got = refs[3 * at : 3 * at + 3]
        start = jnp.where(odd == 1, first, CL - 1 - last)
        for r in range(last - first + 1):
            total = near[r].astype(jnp.float32) + got_near[r].astype(jnp.float32) + got[r].astype(jnp.float32)
            out[start + r] = total.astype(jnp.bfloat16)


def per_device(slab, occupation, column_band, pattern):
    clusters = CL * lax.axis_size("wide")
    share = pattern.shape[1] // lax.axis_size("narrow")
    odd = lax.axis_index("wide") % 2
    rows = PAIR * B
    partner = lambda w: w ^ 1

    far_rows = lax.dynamic_slice_in_dim(slab, odd * 2 * rows, rows, 0)
    near_rows = lax.dynamic_slice_in_dim(slab, (1 - odd) * 2 * rows, rows, 0)
    middle_rows = slab[rows : 2 * rows]
    window = {}
    window[-6] = move(far_rows, "wide", partner)
    window[-4] = move(middle_rows, "wide", partner)
    window[-2] = move(near_rows, "wide", partner)
    window[-8] = move(far_rows, "wide", inward)
    window[12] = move(near_rows, "wide", outward)
    window[6] = move(window[-6], "wide", outward)
    window[8] = move(window[-4], "wide", outward)
    window[10] = move(window[-2], "wide", outward)

    picks = column_band[:, None] == jnp.arange(occupation.shape[0], dtype=jnp.int32)[None, :]
    weight = jnp.sum(jnp.where(picks, occupation[None, :], jnp.float32(0.0)), axis=1)
    scaled = (slab.astype(jnp.float32) * weight[None, :]).astype(jnp.bfloat16)

    chunks = ((0, 1), (2, 5))
    parts = []
    far = pattern
    for first, last in chunks:
        send_far, send_near, keep_far, keep_near = blocks(
            clusters, share, first, last, pattern, scaled, slab, window, far
        )
        got_far = move(send_far, "narrow", lambda n: n ^ 1)
        got_near = move(send_near, "narrow", lambda n: n ^ 1)
        far = (keep_far.astype(jnp.float32) + got_far.astype(jnp.float32)).astype(jnp.bfloat16)
        parts += [keep_near, got_near, move(far, "narrow", lambda n: n ^ 2)]
    return pl.pallas_call(
        functools.partial(finish_kernel, chunks),
        out_shape=jax.ShapeDtypeStruct((CL, share, B, B), jnp.bfloat16),
        in_specs=[VMEM] * len(parts),
        out_specs=VMEM,
        compiler_params=pltpu.CompilerParams(vmem_limit_bytes=LIMIT),
        cost_estimate=SHORT,
        name="finish",
    )(*parts)


def solution(mesh):
    placed = (P("wide", "narrow"), P(), P("narrow"), P("wide", None))
    return jax.shard_map(
        per_device,
        mesh=mesh,
        in_specs=placed,
        out_specs=P("wide", "narrow", None, None),
        check_vma=False,
    )
```

```python
import functools

import jax
import jax.numpy as jnp
from jax import lax
from jax.experimental import pallas as pl
from jax.experimental.pallas import tpu as pltpu
from jax.sharding import PartitionSpec as P

B = 128
REACH = 8
CL = 6
PAIR = 2
VMEM = pl.BlockSpec(memory_space=pltpu.VMEM)
SMEM = pl.BlockSpec(memory_space=pltpu.SMEM)
LIMIT = 40 * 1024 * 1024
SHORT = pl.CostEstimate(flops=1, bytes_accessed=1, transcendentals=0)


def move(value, axis, target):
    count = lax.axis_size(axis)
    return lax.ppermute(value, axis, [(s, target(s) % count) for s in range(count)])


def outward(w):
    return w + 2 if w % 2 == 0 else w - 2


def inward(w):
    return w - 2 if w % 2 == 0 else w + 2


def gate_kernel(*refs):
    pass


def gate(value, *earlier, micros=0):
    hbm = pl.BlockSpec(memory_space=pl.ANY)
    return pl.pallas_call(
        gate_kernel,
        out_shape=jax.ShapeDtypeStruct(value.shape, value.dtype),
        in_specs=[hbm] * (1 + len(earlier)),
        out_specs=hbm,
        input_output_aliases={0: 0},
        cost_estimate=pl.CostEstimate(flops=micros * 10**9, bytes_accessed=micros * 3_000_000, transcendentals=0),
        name="gate",
    )(value, *earlier)


def blocks_kernel(clusters, share, marks, first, last, pattern, left, own, after, *refs):
    pieces = refs[: len(marks)]
    outs = refs[len(marks) : len(marks) + 4]
    dense = refs[len(marks) + 4]
    wide = lax.axis_index("wide")
    me = lax.axis_index("narrow")
    odd = lax.rem(wide, 2)

    def natural(low, high):
        return jnp.where(odd == 1, low, CL - 1 - high)

    def multiply(rows, offset, c0, c1):
        count = c1 - c0 + 1
        start = natural(c0, c1)
        product = lax.dot_general(
            left[pl.ds(pl.multiple_of(start * B, B), count * B), :],
            rows,
            (((1,), (1,)), ((), ())),
            preferred_element_type=jnp.float32,
        ).astype(jnp.bfloat16)
        for r in range(count):
            for h in range(PAIR):
                dense[start + r, offset + REACH + h] = product[r * B : (r + 1) * B, h * B : (h + 1) * B]

    for offset in range(0, CL, PAIR):
        multiply(own[offset * B : (offset + PAIR) * B, :], offset, first, last)
    for piece, mark in zip(pieces, marks):
        c0, c1 = max(first, mark - REACH), min(last, mark + PAIR - 1 + REACH)
        multiply(piece[...], natural(mark, mark + PAIR - 1), c0, c1)

    base = wide * CL - REACH
    start = natural(first, last)
    for out, mask in zip(outs, (3, 1, 2, 0)):
        slot0 = (me ^ mask) * share
        for r in range(last - first + 1):
            for s in range(share):
                where = lax.rem(pattern[start + r, slot0 + s] - base + clusters, clusters)
                out[r, s] = dense[start + r, where]


def blocks(clusters, share, first, last, pattern, left, own, window, after):
    marks = [m for m in window if m + PAIR - 1 >= first - REACH and m <= last + REACH]
    shape = jax.ShapeDtypeStruct((last - first + 1, share, B, B), jnp.bfloat16)
    return pl.pallas_call(
        functools.partial(blocks_kernel, clusters, share, marks, first, last),
        out_shape=[shape] * 4,
        in_specs=[SMEM, VMEM, VMEM, pl.BlockSpec(memory_space=pl.ANY)] + [VMEM] * len(marks),
        out_specs=[VMEM] * 4,
        scratch_shapes=[pltpu.VMEM((CL, CL + 2 * REACH, B, B), jnp.bfloat16)],
        compiler_params=pltpu.CompilerParams(vmem_limit_bytes=LIMIT),
        cost_estimate=SHORT,
        name=f"blocks_{first}_{last}",
    )(pattern, left, own, after, *[window[m] for m in marks])


def add_kernel(x, y, after, out):
    out[...] = (x[...].astype(jnp.float32) + y[...].astype(jnp.float32)).astype(jnp.bfloat16)


def add(x, y, after):
    return pl.pallas_call(
        add_kernel,
        out_shape=jax.ShapeDtypeStruct(x.shape, x.dtype),
        in_specs=[VMEM, VMEM, pl.BlockSpec(memory_space=pl.ANY)],
        out_specs=VMEM,
        compiler_params=pltpu.CompilerParams(vmem_limit_bytes=LIMIT),
        cost_estimate=SHORT,
        name="add",
    )(x, y, after)


def finish_kernel(chunks, *refs):
    out = refs[-1]
    odd = lax.rem(lax.axis_index("wide"), 2)
    for at, (first, last) in enumerate(chunks):
        near, got_near, got = refs[3 * at : 3 * at + 3]
        start = jnp.where(odd == 1, first, CL - 1 - last)
        for r in range(last - first + 1):
            total = near[r].astype(jnp.float32) + got_near[r].astype(jnp.float32) + got[r].astype(jnp.float32)
            out[start + r] = total.astype(jnp.bfloat16)


def per_device(slab, occupation, column_band, pattern):
    clusters = CL * lax.axis_size("wide")
    share = pattern.shape[1] // lax.axis_size("narrow")
    odd = lax.axis_index("wide") % 2
    rows = PAIR * B
    partner = lambda w: w ^ 1

    far_rows = lax.dynamic_slice_in_dim(slab, odd * 2 * rows, rows, 0)
    near_rows = lax.dynamic_slice_in_dim(slab, (1 - odd) * 2 * rows, rows, 0)
    middle_rows = slab[rows : 2 * rows]
    window = {}
    window[-8] = gate(move(far_rows, "wide", inward), micros=20)
    window[12] = gate(move(near_rows, "wide", outward), micros=20)
    window[-6] = move(far_rows, "wide", partner)
    window[6] = gate(move(window[-6], "wide", outward), micros=8)
    window[-4] = move(gate(middle_rows, window[-6]), "wide", partner)
    window[8] = move(window[-4], "wide", outward)
    window[-2] = move(gate(near_rows, window[-4]), "wide", partner)
    window[10] = move(window[-2], "wide", outward)

    picks = column_band[:, None] == jnp.arange(occupation.shape[0], dtype=jnp.int32)[None, :]
    weight = jnp.sum(jnp.where(picks, occupation[None, :], jnp.float32(0.0)), axis=1)
    scaled = (slab.astype(jnp.float32) * weight[None, :]).astype(jnp.bfloat16)

    chunks = ((0, 1), (2, 5))
    parts = []
    after = window[12]
    got = None
    for first, last in chunks:
        send_far, send_near, keep_far, keep_near = blocks(
            clusters, share, first, last, pattern, scaled, slab, window, after
        )
        got_far = move(send_far, "narrow", lambda n: n ^ 1)
        got_near = move(send_near, "narrow", lambda n: n ^ 1)
        after = add(keep_far, got_far, keep_far if got is None else got)
        got = move(after, "narrow", lambda n: n ^ 2)
        if last != CL - 1:
            got = gate(got, micros=20)
        parts += [keep_near, got_near, got]
    return pl.pallas_call(
        functools.partial(finish_kernel, chunks),
        out_shape=jax.ShapeDtypeStruct((CL, share, B, B), jnp.bfloat16),
        in_specs=[VMEM] * len(parts),
        out_specs=VMEM,
        compiler_params=pltpu.CompilerParams(vmem_limit_bytes=LIMIT),
        cost_estimate=SHORT,
        name="finish",
    )(*parts)


def solution(mesh):
    placed = (P("wide", "narrow"), P(), P("narrow"), P("wide", None))
    return jax.shard_map(
        per_device,
        mesh=mesh,
        in_specs=placed,
        out_specs=P("wide", "narrow", None, None),
        check_vma=False,
    )
```

```python
import functools

import jax
import jax.numpy as jnp
from jax import lax
from jax.experimental import pallas as pl
from jax.experimental.pallas import tpu as pltpu
from jax.sharding import PartitionSpec as P

B = 128
REACH = 8
CL = 6
PAIR = 2
VMEM = pl.BlockSpec(memory_space=pltpu.VMEM)
SMEM = pl.BlockSpec(memory_space=pltpu.SMEM)
LIMIT = 40 * 1024 * 1024


def move(value, axis, target):
    count = lax.axis_size(axis)
    return lax.ppermute(value, axis, [(s, target(s) % count) for s in range(count)])


def outward(w):
    return w + 2 if w % 2 == 0 else w - 2


def across(w):
    return w - 1 if w % 2 == 0 else w + 1


def inward(w):
    return w - 2 if w % 2 == 0 else w + 2


def blocks_kernel(clusters, share, marks, first, last, pattern, left, own, *refs):
    pieces = refs[: len(marks)]
    outs = refs[len(marks) : len(marks) + 4]
    dense = refs[len(marks) + 4]
    wide = lax.axis_index("wide")
    me = lax.axis_index("narrow")
    odd = lax.rem(wide, 2)

    def natural(low, high):
        return jnp.where(odd == 1, low, CL - 1 - high)

    def multiply(rows, offset, c0, c1):
        count = c1 - c0 + 1
        start = natural(c0, c1)
        product = lax.dot_general(
            left[pl.ds(pl.multiple_of(start * B, B), count * B), :],
            rows,
            (((1,), (1,)), ((), ())),
            preferred_element_type=jnp.float32,
        ).astype(jnp.bfloat16)
        for r in range(count):
            for h in range(PAIR):
                dense[start + r, offset + REACH + h] = product[r * B : (r + 1) * B, h * B : (h + 1) * B]

    for offset in range(0, CL, PAIR):
        multiply(own[offset * B : (offset + PAIR) * B, :], offset, first, last)
    for piece, mark in zip(pieces, marks):
        count = piece.shape[0] // B
        for at in range(0, count, PAIR):
            low, high = mark + at, mark + at + PAIR - 1
            c0, c1 = max(first, high - REACH - PAIR + 1), min(last, high + REACH)
            if c0 <= c1:
                row = jnp.where(odd == 1, at, count - PAIR - at) * B
                multiply(piece[pl.ds(pl.multiple_of(row, PAIR * B), PAIR * B), :], natural(low, high), c0, c1)

    base = wide * CL - REACH
    start = natural(first, last)
    for out, mask in zip(outs, (3, 1, 2, 0)):
        slot0 = (me ^ mask) * share
        for r in range(last - first + 1):
            for s in range(share):
                where = lax.rem(pattern[start + r, slot0 + s] - base + clusters, clusters)
                out[r, s] = dense[start + r, where]


def blocks(clusters, share, first, last, pattern, left, own, window):
    marks = [m for m, v in window.items() if m + v.shape[0] // B > first - REACH and m <= last + REACH]
    shape = jax.ShapeDtypeStruct((last - first + 1, share, B, B), jnp.bfloat16)
    return pl.pallas_call(
        functools.partial(blocks_kernel, clusters, share, marks, first, last),
        out_shape=[shape] * 4,
        in_specs=[SMEM] + [VMEM] * (2 + len(marks)),
        out_specs=[VMEM] * 4,
        scratch_shapes=[pltpu.VMEM((CL, CL + 2 * REACH, B, B), jnp.bfloat16)],
        compiler_params=pltpu.CompilerParams(vmem_limit_bytes=LIMIT),
        name=f"blocks_{first}_{last}",
    )(pattern, left, own, *[window[m] for m in marks])


def per_device(slab, occupation, column_band, pattern):
    clusters = CL * lax.axis_size("wide")
    share = pattern.shape[1] // lax.axis_size("narrow")
    odd = lax.axis_index("wide") % 2
    rows = PAIR * B
    partner = lambda w: w ^ 1

    near_rows = lax.dynamic_slice_in_dim(slab, (1 - odd) * 2 * rows, rows, 0)
    end_rows = lax.dynamic_slice_in_dim(slab, odd * 2 * rows, rows, 0)
    far_rows = lax.dynamic_slice_in_dim(slab, odd * rows, 2 * rows, 0)
    window = {}
    window[-2] = move(near_rows, "wide", partner)
    window[-6] = move(far_rows, "wide", partner)
    window[6] = move(far_rows, "wide", across)
    window[-8] = move(end_rows, "wide", inward)
    window[12] = move(near_rows, "wide", outward)
    window[10] = move(window[-2], "wide", outward)

    picks = column_band[:, None] == jnp.arange(occupation.shape[0], dtype=jnp.int32)[None, :]
    weight = jnp.sum(jnp.where(picks, occupation[None, :], jnp.float32(0.0)), axis=1)
    scaled = (slab.astype(jnp.float32) * weight[None, :]).astype(jnp.bfloat16)

    send_far, send_near, keep_far, keep_near = blocks(clusters, share, 0, CL - 1, pattern, scaled, slab, window)
    got_far = move(send_far, "narrow", lambda n: n ^ 1)
    got_near = move(send_near, "narrow", lambda n: n ^ 1)
    far = (keep_far.astype(jnp.float32) + got_far.astype(jnp.float32)).astype(jnp.bfloat16)
    got = move(far, "narrow", lambda n: n ^ 2)
    near = keep_near.astype(jnp.float32) + got_near.astype(jnp.float32)
    return (near + got.astype(jnp.float32)).astype(jnp.bfloat16)


def solution(mesh):
    placed = (P("wide", "narrow"), P(), P("narrow"), P("wide", None))
    return jax.shard_map(
        per_device,
        mesh=mesh,
        in_specs=placed,
        out_specs=P("wide", "narrow", None, None),
        check_vma=False,
    )
```

```python
import functools

import jax
import jax.numpy as jnp
from jax import lax
from jax.experimental import pallas as pl
from jax.experimental.pallas import tpu as pltpu
from jax.sharding import PartitionSpec as P

B = 128
REACH = 8
CL = 6
PAIR = 2
VMEM = pl.BlockSpec(memory_space=pltpu.VMEM)
SMEM = pl.BlockSpec(memory_space=pltpu.SMEM)
LIMIT = 40 * 1024 * 1024
LONG = pl.CostEstimate(flops=20 * 10**9, bytes_accessed=1, transcendentals=0)
SHORT = pl.CostEstimate(flops=1, bytes_accessed=1, transcendentals=0)


def move(value, axis, target):
    count = lax.axis_size(axis)
    return lax.ppermute(value, axis, [(s, target(s) % count) for s in range(count)])


def outward(w):
    return w + 2 if w % 2 == 0 else w - 2


def across(w):
    return w - 1 if w % 2 == 0 else w + 1


def inward(w):
    return w - 2 if w % 2 == 0 else w + 2


def blocks_kernel(clusters, share, marks, first, last, pattern, left, own, after, *refs):
    pieces = refs[: len(marks)]
    outs = refs[len(marks) : len(marks) + 4]
    dense = refs[len(marks) + 4]
    wide = lax.axis_index("wide")
    me = lax.axis_index("narrow")
    odd = lax.rem(wide, 2)

    def natural(low, high):
        return jnp.where(odd == 1, low, CL - 1 - high)

    def multiply(rows, offset, c0, c1):
        count = c1 - c0 + 1
        start = natural(c0, c1)
        product = lax.dot_general(
            left[pl.ds(pl.multiple_of(start * B, B), count * B), :],
            rows,
            (((1,), (1,)), ((), ())),
            preferred_element_type=jnp.float32,
        ).astype(jnp.bfloat16)
        for r in range(count):
            for h in range(PAIR):
                dense[start + r, offset + REACH + h] = product[r * B : (r + 1) * B, h * B : (h + 1) * B]

    for offset in range(0, CL, PAIR):
        multiply(own[offset * B : (offset + PAIR) * B, :], offset, first, last)
    for piece, mark in zip(pieces, marks):
        count = piece.shape[0] // B
        for at in range(0, count, PAIR):
            low, high = mark + at, mark + at + PAIR - 1
            c0, c1 = max(first, high - REACH - PAIR + 1), min(last, high + REACH)
            if c0 <= c1:
                row = jnp.where(odd == 1, at, count - PAIR - at) * B
                multiply(piece[pl.ds(pl.multiple_of(row, PAIR * B), PAIR * B), :], natural(low, high), c0, c1)

    base = wide * CL - REACH
    start = natural(first, last)
    for out, mask in zip(outs, (3, 1, 2, 0)):
        slot0 = (me ^ mask) * share
        for r in range(last - first + 1):
            for s in range(share):
                where = lax.rem(pattern[start + r, slot0 + s] - base + clusters, clusters)
                out[r, s] = dense[start + r, where]


def blocks(clusters, share, first, last, pattern, left, own, window, after, cost):
    marks = [m for m, v in window.items() if m + v.shape[0] // B > first - REACH and m <= last + REACH]
    shape = jax.ShapeDtypeStruct((last - first + 1, share, B, B), jnp.bfloat16)
    return pl.pallas_call(
        functools.partial(blocks_kernel, clusters, share, marks, first, last),
        out_shape=[shape] * 4,
        in_specs=[SMEM] + [VMEM] * (3 + len(marks)),
        out_specs=[VMEM] * 4,
        scratch_shapes=[pltpu.VMEM((CL, CL + 2 * REACH, B, B), jnp.bfloat16)],
        compiler_params=pltpu.CompilerParams(vmem_limit_bytes=LIMIT),
        cost_estimate=cost,
        name=f"blocks_{first}_{last}",
    )(pattern, left, own, after, *[window[m] for m in marks])


def add_kernel(x, y, out):
    out[...] = (x[...].astype(jnp.float32) + y[...].astype(jnp.float32)).astype(jnp.bfloat16)


def add(x, y):
    return pl.pallas_call(
        add_kernel,
        out_shape=jax.ShapeDtypeStruct(x.shape, x.dtype),
        in_specs=[VMEM, VMEM],
        out_specs=VMEM,
        compiler_params=pltpu.CompilerParams(vmem_limit_bytes=LIMIT),
        cost_estimate=SHORT,
        name="add",
    )(x, y)


def total_kernel(near, got_near, got, out):
    total = near[...].astype(jnp.float32) + got_near[...].astype(jnp.float32) + got[...].astype(jnp.float32)
    out[...] = total.astype(jnp.bfloat16)


def total(near, got_near, got):
    return pl.pallas_call(
        total_kernel,
        out_shape=jax.ShapeDtypeStruct(near.shape, near.dtype),
        in_specs=[VMEM] * 3,
        out_specs=VMEM,
        compiler_params=pltpu.CompilerParams(vmem_limit_bytes=LIMIT),
        cost_estimate=LONG,
        name="total",
    )(near, got_near, got)


def finish_kernel(chunks, early, near, got_near, got, out):
    odd = lax.rem(lax.axis_index("wide"), 2)
    start, later = [jnp.where(odd == 1, first, CL - 1 - last) for first, last in chunks]
    for r in range(early.shape[0]):
        out[start + r] = early[r]
    for r in range(near.shape[0]):
        total = near[r].astype(jnp.float32) + got_near[r].astype(jnp.float32) + got[r].astype(jnp.float32)
        out[later + r] = total.astype(jnp.bfloat16)


def take_kernel(slab, after, out):
    row = pl.multiple_of(lax.rem(lax.axis_index("wide"), 2) * 2 * PAIR * B, PAIR * B)
    out[...] = slab[pl.ds(row, PAIR * B), :]


def take(slab, after):
    return pl.pallas_call(
        take_kernel,
        out_shape=jax.ShapeDtypeStruct((PAIR * B, slab.shape[1]), slab.dtype),
        in_specs=[VMEM] * 2,
        out_specs=VMEM,
        compiler_params=pltpu.CompilerParams(vmem_limit_bytes=LIMIT),
        cost_estimate=SHORT,
        name="take",
    )(slab, after)


def per_device(slab, occupation, column_band, pattern):
    clusters = CL * lax.axis_size("wide")
    share = pattern.shape[1] // lax.axis_size("narrow")
    odd = lax.axis_index("wide") % 2
    rows = PAIR * B
    partner = lambda w: w ^ 1

    picks = column_band[:, None] == jnp.arange(occupation.shape[0], dtype=jnp.int32)[None, :]
    weight = jnp.sum(jnp.where(picks, occupation[None, :], jnp.float32(0.0)), axis=1)
    scaled = (slab.astype(jnp.float32) * weight[None, :]).astype(jnp.bfloat16)

    near_rows = lax.dynamic_slice_in_dim(slab, (1 - odd) * 2 * rows, rows, 0)
    end_rows = take(slab, weight)
    window = {}
    window[-4] = move(slab[rows : 2 * rows], "wide", partner)
    window[-2] = move(near_rows, "wide", partner)
    window[-8] = move(end_rows, "wide", inward)
    window[6] = move(end_rows, "wide", across)
    window[-6] = move(end_rows, "wide", partner)
    window[8] = move(window[-4], "wide", outward)
    window[10] = move(window[-2], "wide", outward)
    window[12] = move(near_rows, "wide", outward)

    chunks = ((0, 3), (4, 5))
    parts = []
    after, cost = near_rows, LONG
    for first, last in chunks:
        send_far, send_near, keep_far, keep_near = blocks(
            clusters, share, first, last, pattern, scaled, slab, window, after, cost
        )
        got_far = move(send_far, "narrow", lambda n: n ^ 1)
        got_near = move(send_near, "narrow", lambda n: n ^ 1)
        far = add(keep_far, got_far)
        parts.append([keep_near, got_near, move(far, "narrow", lambda n: n ^ 2)])
        after, cost = got_far, SHORT
    return pl.pallas_call(
        functools.partial(finish_kernel, chunks),
        out_shape=jax.ShapeDtypeStruct((CL, share, B, B), jnp.bfloat16),
        in_specs=[VMEM] * 4,
        out_specs=VMEM,
        compiler_params=pltpu.CompilerParams(vmem_limit_bytes=LIMIT),
        cost_estimate=SHORT,
        name="finish",
    )(total(*parts[0]), *parts[1])


def solution(mesh):
    placed = (P("wide", "narrow"), P(), P("narrow"), P("wide", None))
    return jax.shard_map(
        per_device,
        mesh=mesh,
        in_specs=placed,
        out_specs=P("wide", "narrow", None, None),
        check_vma=False,
    )
```

```python
import functools

import jax
import jax.numpy as jnp
from jax import lax
from jax.experimental import pallas as pl
from jax.experimental.pallas import tpu as pltpu
from jax.sharding import PartitionSpec as P

B = 128
REACH = 8
CL = 6
PAIR = 2
VMEM = pl.BlockSpec(memory_space=pltpu.VMEM)
SMEM = pl.BlockSpec(memory_space=pltpu.SMEM)
LIMIT = 40 * 1024 * 1024
LONG = pl.CostEstimate(flops=20 * 10**9, bytes_accessed=1, transcendentals=0)
SHORT = pl.CostEstimate(flops=1, bytes_accessed=1, transcendentals=0)


def move(value, axis, target):
    count = lax.axis_size(axis)
    return lax.ppermute(value, axis, [(s, target(s) % count) for s in range(count)])


def outward(w):
    return w + 2 if w % 2 == 0 else w - 2


def across(w):
    return w - 1 if w % 2 == 0 else w + 1


def inward(w):
    return w - 2 if w % 2 == 0 else w + 2


def blocks_kernel(clusters, share, marks, chunk, held, pattern, left, *refs):
    pieces = refs[: len(marks)]
    dense = refs[len(marks) + held]
    outs = refs[len(marks) + held + 1 :]
    wide = lax.axis_index("wide")
    me = lax.axis_index("narrow")
    odd = lax.rem(wide, 2)

    def natural(low, high):
        return jnp.where(odd == 1, low, CL - 1 - high)

    for piece, mark in zip(pieces, marks):
        count = piece.shape[0] // B
        for at in range(0, count, PAIR):
            low, high = mark + at, mark + at + PAIR - 1
            c0, c1 = max(0, low - REACH), min(CL - 1, high + REACH)
            offset, start, rows = natural(low, high), natural(c0, c1), (c1 - c0 + 1) * B
            row = pl.multiple_of(jnp.where(odd == 1, at, count - PAIR - at) * B, PAIR * B)
            product = lax.dot_general(
                left[pl.ds(pl.multiple_of(start * B, B), rows), :],
                piece[pl.ds(row, PAIR * B), :],
                (((1,), (1,)), ((), ())),
                preferred_element_type=jnp.float32,
            ).astype(jnp.bfloat16)
            for r in range(c1 - c0 + 1):
                for h in range(PAIR):
                    dense[start + r, offset + REACH + h] = product[r * B : (r + 1) * B, h * B : (h + 1) * B]

    if chunk is not None:
        first, last = chunk
        base = wide * CL - REACH
        start = natural(first, last)
        for out, mask in zip(outs, (3, 1, 2, 0)):
            slot0 = (me ^ mask) * share
            for r in range(last - first + 1):
                for s in range(share):
                    where = lax.rem(pattern[start + r, slot0 + s] - base + clusters, clusters)
                    out[r, s] = dense[start + r, where]


def blocks(clusters, share, pattern, left, pieces, cost, dense=None, chunk=None, after=None):
    held = [] if dense is None else [dense, after]
    shapes = [jax.ShapeDtypeStruct((CL, CL + 2 * REACH, B, B), jnp.bfloat16)]
    if chunk is not None:
        shapes += [jax.ShapeDtypeStruct((chunk[1] - chunk[0] + 1, share, B, B), jnp.bfloat16)] * 4
    return pl.pallas_call(
        functools.partial(blocks_kernel, clusters, share, list(pieces), chunk, len(held)),
        out_shape=shapes,
        in_specs=[SMEM] + [VMEM] * (1 + len(pieces) + len(held)),
        out_specs=[VMEM] * len(shapes),
        input_output_aliases={2 + len(pieces): 0} if held else {},
        compiler_params=pltpu.CompilerParams(vmem_limit_bytes=LIMIT),
        cost_estimate=cost,
        name="blocks",
    )(pattern, left, *pieces.values(), *held)


def add_kernel(x, y, out):
    out[...] = (x[...].astype(jnp.float32) + y[...].astype(jnp.float32)).astype(jnp.bfloat16)


def add(x, y):
    return pl.pallas_call(
        add_kernel,
        out_shape=jax.ShapeDtypeStruct(x.shape, x.dtype),
        in_specs=[VMEM, VMEM],
        out_specs=VMEM,
        compiler_params=pltpu.CompilerParams(vmem_limit_bytes=LIMIT),
        cost_estimate=SHORT,
        name="add",
    )(x, y)


def total_kernel(near, got_near, got, out):
    total = near[...].astype(jnp.float32) + got_near[...].astype(jnp.float32) + got[...].astype(jnp.float32)
    out[...] = total.astype(jnp.bfloat16)


def total(near, got_near, got):
    return pl.pallas_call(
        total_kernel,
        out_shape=jax.ShapeDtypeStruct(near.shape, near.dtype),
        in_specs=[VMEM] * 3,
        out_specs=VMEM,
        compiler_params=pltpu.CompilerParams(vmem_limit_bytes=LIMIT),
        cost_estimate=LONG,
        name="total",
    )(near, got_near, got)


def finish_kernel(chunks, early, near, got_near, got, out):
    odd = lax.rem(lax.axis_index("wide"), 2)
    start, later = [jnp.where(odd == 1, first, CL - 1 - last) for first, last in chunks]
    for r in range(early.shape[0]):
        out[start + r] = early[r]
    for r in range(near.shape[0]):
        total = near[r].astype(jnp.float32) + got_near[r].astype(jnp.float32) + got[r].astype(jnp.float32)
        out[later + r] = total.astype(jnp.bfloat16)


def take_kernel(slab, after, out):
    row = pl.multiple_of(lax.rem(lax.axis_index("wide"), 2) * 2 * PAIR * B, PAIR * B)
    out[...] = slab[pl.ds(row, PAIR * B), :]


def take(slab, after):
    return pl.pallas_call(
        take_kernel,
        out_shape=jax.ShapeDtypeStruct((PAIR * B, slab.shape[1]), slab.dtype),
        in_specs=[VMEM] * 2,
        out_specs=VMEM,
        compiler_params=pltpu.CompilerParams(vmem_limit_bytes=LIMIT),
        cost_estimate=SHORT,
        name="take",
    )(slab, after)


def per_device(slab, occupation, column_band, pattern):
    clusters = CL * lax.axis_size("wide")
    share = pattern.shape[1] // lax.axis_size("narrow")
    odd = lax.axis_index("wide") % 2
    rows = PAIR * B
    partner = lambda w: w ^ 1

    picks = column_band[:, None] == jnp.arange(occupation.shape[0], dtype=jnp.int32)[None, :]
    weight = jnp.sum(jnp.where(picks, occupation[None, :], jnp.float32(0.0)), axis=1)
    scaled = (slab.astype(jnp.float32) * weight[None, :]).astype(jnp.bfloat16)

    near_rows = lax.dynamic_slice_in_dim(slab, (1 - odd) * 2 * rows, rows, 0)
    end_rows = lax.dynamic_slice_in_dim(slab, odd * 2 * rows, rows, 0)
    early = {0: slab}
    early[-2] = move(near_rows, "wide", partner)
    early[-4] = move(slab[rows : 2 * rows], "wide", partner)
    early[-8] = move(end_rows, "wide", inward)
    early[10] = move(early[-2], "wide", outward)
    early[8] = move(early[-4], "wide", outward)
    later_rows = take(slab, early[-2])
    middle = {6: move(later_rows, "wide", across), -6: move(later_rows, "wide", partner)}
    late = {12: move(near_rows, "wide", outward)}

    (dense,) = blocks(clusters, share, pattern, scaled, early, LONG)
    parts = []
    after = scaled
    for pieces, chunk, cost in ((middle, (0, 3), LONG), (late, (4, 5), SHORT)):
        dense, send_far, send_near, keep_far, keep_near = blocks(
            clusters, share, pattern, scaled, pieces, cost, dense, chunk, after
        )
        got_far = move(send_far, "narrow", lambda n: n ^ 1)
        got_near = move(send_near, "narrow", lambda n: n ^ 1)
        far = add(keep_far, got_far)
        parts.append([keep_near, got_near, move(far, "narrow", lambda n: n ^ 2)])
        after = got_far
    chunks = ((0, 3), (4, 5))
    return pl.pallas_call(
        functools.partial(finish_kernel, chunks),
        out_shape=jax.ShapeDtypeStruct((CL, share, B, B), jnp.bfloat16),
        in_specs=[VMEM] * 4,
        out_specs=VMEM,
        compiler_params=pltpu.CompilerParams(vmem_limit_bytes=LIMIT),
        cost_estimate=SHORT,
        name="finish",
    )(total(*parts[0]), *parts[1])


def solution(mesh):
    placed = (P("wide", "narrow"), P(), P("narrow"), P("wide", None))
    return jax.shard_map(
        per_device,
        mesh=mesh,
        in_specs=placed,
        out_specs=P("wide", "narrow", None, None),
        check_vma=False,
    )
```

```python
import functools

import jax
import jax.numpy as jnp
from jax import lax
from jax.experimental import pallas as pl
from jax.experimental.pallas import tpu as pltpu
from jax.sharding import PartitionSpec as P

B = 128
REACH = 8
CL = 6
PAIR = 2
VMEM = pl.BlockSpec(memory_space=pltpu.VMEM)
SMEM = pl.BlockSpec(memory_space=pltpu.SMEM)
LIMIT = 40 * 1024 * 1024
LONG = pl.CostEstimate(flops=20 * 10**9, bytes_accessed=1, transcendentals=0)
SHORT = pl.CostEstimate(flops=1, bytes_accessed=1, transcendentals=0)


def move(value, axis, target):
    count = lax.axis_size(axis)
    return lax.ppermute(value, axis, [(s, target(s) % count) for s in range(count)])


def outward(w):
    return w + 2 if w % 2 == 0 else w - 2


def inward(w):
    return w - 2 if w % 2 == 0 else w + 2


def blocks_kernel(clusters, share, marks, chunk, held, pattern, left, *refs):
    pieces = refs[: len(marks)]
    dense = refs[len(marks) + held]
    outs = refs[len(marks) + held + 1 :]
    wide = lax.axis_index("wide")
    me = lax.axis_index("narrow")
    odd = lax.rem(wide, 2)

    def natural(low, high):
        return jnp.where(odd == 1, low, CL - 1 - high)

    for piece, mark in zip(pieces, marks):
        count = piece.shape[0] // B
        for at in range(0, count, PAIR):
            low, high = mark + at, mark + at + PAIR - 1
            c0, c1 = max(0, low - REACH), min(CL - 1, high + REACH)
            offset, start, rows = natural(low, high), natural(c0, c1), (c1 - c0 + 1) * B
            row = pl.multiple_of(jnp.where(odd == 1, at, count - PAIR - at) * B, PAIR * B)
            product = lax.dot_general(
                left[pl.ds(pl.multiple_of(start * B, B), rows), :],
                piece[pl.ds(row, PAIR * B), :],
                (((1,), (1,)), ((), ())),
                preferred_element_type=jnp.float32,
            ).astype(jnp.bfloat16)
            for r in range(c1 - c0 + 1):
                for h in range(PAIR):
                    dense[start + r, offset + REACH + h] = product[r * B : (r + 1) * B, h * B : (h + 1) * B]

    if chunk is not None:
        first, last = chunk
        base = wide * CL - REACH
        start = natural(first, last)
        for out, mask in zip(outs, (3, 1, 2, 0)):
            slot0 = (me ^ mask) * share
            for r in range(last - first + 1):
                for s in range(share):
                    where = lax.rem(pattern[start + r, slot0 + s] - base + clusters, clusters)
                    out[r, s] = dense[start + r, where]


def blocks(clusters, share, pattern, left, pieces, cost, dense=None, chunk=None, after=None):
    held = [] if dense is None else [dense, after]
    shapes = [jax.ShapeDtypeStruct((CL, CL + 2 * REACH, B, B), jnp.bfloat16)]
    if chunk is not None:
        shapes += [jax.ShapeDtypeStruct((chunk[1] - chunk[0] + 1, share, B, B), jnp.bfloat16)] * 4
    return pl.pallas_call(
        functools.partial(blocks_kernel, clusters, share, list(pieces), chunk, len(held)),
        out_shape=shapes,
        in_specs=[SMEM] + [VMEM] * (1 + len(pieces) + len(held)),
        out_specs=[VMEM] * len(shapes),
        input_output_aliases={2 + len(pieces): 0} if held else {},
        compiler_params=pltpu.CompilerParams(vmem_limit_bytes=LIMIT),
        cost_estimate=cost,
        name="blocks",
    )(pattern, left, *pieces.values(), *held)


def add_kernel(x, y, out):
    out[...] = (x[...].astype(jnp.float32) + y[...].astype(jnp.float32)).astype(jnp.bfloat16)


def add(x, y):
    return pl.pallas_call(
        add_kernel,
        out_shape=jax.ShapeDtypeStruct(x.shape, x.dtype),
        in_specs=[VMEM, VMEM],
        out_specs=VMEM,
        compiler_params=pltpu.CompilerParams(vmem_limit_bytes=LIMIT),
        cost_estimate=SHORT,
        name="add",
    )(x, y)


def total_kernel(near, got_near, got, out):
    total = near[...].astype(jnp.float32) + got_near[...].astype(jnp.float32) + got[...].astype(jnp.float32)
    out[...] = total.astype(jnp.bfloat16)


def total(near, got_near, got):
    return pl.pallas_call(
        total_kernel,
        out_shape=jax.ShapeDtypeStruct(near.shape, near.dtype),
        in_specs=[VMEM] * 3,
        out_specs=VMEM,
        compiler_params=pltpu.CompilerParams(vmem_limit_bytes=LIMIT),
        cost_estimate=LONG,
        name="total",
    )(near, got_near, got)


def finish_kernel(chunks, early, near, got_near, got, out):
    odd = lax.rem(lax.axis_index("wide"), 2)
    start, later = [jnp.where(odd == 1, first, CL - 1 - last) for first, last in chunks]
    for r in range(early.shape[0]):
        out[start + r] = early[r]
    for r in range(near.shape[0]):
        total = near[r].astype(jnp.float32) + got_near[r].astype(jnp.float32) + got[r].astype(jnp.float32)
        out[later + r] = total.astype(jnp.bfloat16)


def take_kernel(slab, after, out):
    row = (1 - lax.rem(lax.axis_index("wide"), 2)) * 2 * PAIR * B
    out[...] = slab[pl.ds(pl.multiple_of(row, PAIR * B), PAIR * B), :]


def take(slab, after):
    return pl.pallas_call(
        take_kernel,
        out_shape=jax.ShapeDtypeStruct((PAIR * B, slab.shape[1]), slab.dtype),
        in_specs=[VMEM] * 2,
        out_specs=VMEM,
        compiler_params=pltpu.CompilerParams(vmem_limit_bytes=LIMIT),
        cost_estimate=SHORT,
        name="take",
    )(slab, after)


def per_device(slab, occupation, column_band, pattern):
    clusters = CL * lax.axis_size("wide")
    share = pattern.shape[1] // lax.axis_size("narrow")
    odd = lax.axis_index("wide") % 2
    rows = PAIR * B
    partner = lambda w: w ^ 1

    picks = column_band[:, None] == jnp.arange(occupation.shape[0], dtype=jnp.int32)[None, :]
    weight = jnp.sum(jnp.where(picks, occupation[None, :], jnp.float32(0.0)), axis=1)
    scaled = (slab.astype(jnp.float32) * weight[None, :]).astype(jnp.bfloat16)

    near_rows = take(slab, weight)
    end_rows = lax.dynamic_slice_in_dim(slab, odd * 2 * rows, rows, 0)
    early = {0: slab}
    early[-6] = move(end_rows, "wide", partner)
    early[-4] = move(slab[rows : 2 * rows], "wide", partner)
    early[-2] = move(near_rows, "wide", partner)
    early[-8] = move(end_rows, "wide", inward)
    early[6] = move(early[-6], "wide", outward)
    early[8] = move(early[-4], "wide", outward)
    middle = {10: move(early[-2], "wide", outward)}
    late = {12: move(near_rows, "wide", outward)}

    (dense,) = blocks(clusters, share, pattern, scaled, early, LONG)
    parts = []
    after = scaled
    for pieces, chunk, cost in ((middle, (0, 3), LONG), (late, (4, 5), SHORT)):
        dense, send_far, send_near, keep_far, keep_near = blocks(
            clusters, share, pattern, scaled, pieces, cost, dense, chunk, after
        )
        got_far = move(send_far, "narrow", lambda n: n ^ 1)
        got_near = move(send_near, "narrow", lambda n: n ^ 1)
        far = add(keep_far, got_far)
        parts.append([keep_near, got_near, move(far, "narrow", lambda n: n ^ 2)])
        after = got_far
    chunks = ((0, 3), (4, 5))
    return pl.pallas_call(
        functools.partial(finish_kernel, chunks),
        out_shape=jax.ShapeDtypeStruct((CL, share, B, B), jnp.bfloat16),
        in_specs=[VMEM] * 4,
        out_specs=VMEM,
        compiler_params=pltpu.CompilerParams(vmem_limit_bytes=LIMIT),
        cost_estimate=SHORT,
        name="finish",
    )(total(*parts[0]), *parts[1])


def solution(mesh):
    placed = (P("wide", "narrow"), P(), P("narrow"), P("wide", None))
    return jax.shard_map(
        per_device,
        mesh=mesh,
        in_specs=placed,
        out_specs=P("wide", "narrow", None, None),
        check_vma=False,
    )
```

```python
import functools

import jax
import jax.numpy as jnp
from jax import lax
from jax.experimental import pallas as pl
from jax.experimental.pallas import tpu as pltpu
from jax.sharding import PartitionSpec as P

B = 128
REACH = 8
CL = 6
PAIR = 2
VMEM = pl.BlockSpec(memory_space=pltpu.VMEM)
SMEM = pl.BlockSpec(memory_space=pltpu.SMEM)
LIMIT = 40 * 1024 * 1024
LONG = pl.CostEstimate(flops=20 * 10**9, bytes_accessed=1, transcendentals=0)
SHORT = pl.CostEstimate(flops=1, bytes_accessed=1, transcendentals=0)


def move(value, axis, target):
    count = lax.axis_size(axis)
    return lax.ppermute(value, axis, [(s, target(s) % count) for s in range(count)])


def outward(w):
    return w + 2 if w % 2 == 0 else w - 2


def across(w):
    return w - 1 if w % 2 == 0 else w + 1


def natural(low, high):
    odd = lax.rem(lax.axis_index("wide"), 2)
    return jnp.where(odd == 1, low, CL - 1 - high)


def multiply(left, right):
    product = lax.dot_general(left, right, (((1,), (1,)), ((), ())), preferred_element_type=jnp.float32)
    return product.astype(jnp.bfloat16)


def add_pieces(marks, pieces, left, dense):
    for piece, mark in zip(pieces, marks):
        count = piece.shape[0] // B
        for at in range(0, count, PAIR):
            low, high = mark + at, mark + at + PAIR - 1
            c0, c1 = max(0, low - REACH), min(CL - 1, high + REACH)
            offset, start, rows = natural(low, high), natural(c0, c1), (c1 - c0 + 1) * B
            row = pl.multiple_of((offset - natural(mark, mark + count - 1)) * B, PAIR * B)
            product = multiply(
                left[pl.ds(pl.multiple_of(start * B, B), rows), :], piece[pl.ds(row, PAIR * B), :]
            )
            for r in range(c1 - c0 + 1):
                for h in range(PAIR):
                    dense[start + r, offset + REACH + h] = product[r * B : (r + 1) * B, h * B : (h + 1) * B]


def early_kernel(marks, left, *refs):
    add_pieces(marks, refs[:-1], left, refs[-1])


def early_blocks(left, pieces):
    return pl.pallas_call(
        functools.partial(early_kernel, list(pieces)),
        out_shape=jax.ShapeDtypeStruct((CL, CL + 2 * REACH, B, B), jnp.bfloat16),
        in_specs=[VMEM] * (1 + len(pieces)),
        out_specs=VMEM,
        compiler_params=pltpu.CompilerParams(vmem_limit_bytes=LIMIT),
        cost_estimate=LONG,
        name="early_blocks",
    )(left, *pieces.values())


def ends_kernel(weight, near, far, to_partner, to_far):
    scaled = lambda rows: (rows[...].astype(jnp.float32) * weight[...]).astype(jnp.bfloat16)
    for out, left, right, keep in (
        (to_partner, near, far, ((-1, 6), (-1, 7), (-2, 6))),
        (to_far, far, near, ((6, -1), (7, -1), (6, -2))),
    ):
        product = multiply(scaled(left), right[...])
        odd = lax.rem(lax.axis_index("wide"), 2) == 1
        for at, (c, m) in enumerate(keep):
            spots = []
            for place in (c, m):
                low = -2 if place < 0 else 6
                spots.append((place - low, low + 1 - place))
            (co, mo), (ce, me) = [(spots[0][p], spots[1][p]) for p in (0, 1)]
            out[at] = jnp.where(
                odd,
                product[co * B : (co + 1) * B, mo * B : (mo + 1) * B],
                product[ce * B : (ce + 1) * B, me * B : (me + 1) * B],
            )


def end_blocks(weight, near, far):
    return pl.pallas_call(
        ends_kernel,
        out_shape=[jax.ShapeDtypeStruct((3, B, B), jnp.bfloat16)] * 2,
        in_specs=[VMEM] * 3,
        out_specs=[VMEM] * 2,
        compiler_params=pltpu.CompilerParams(vmem_limit_bytes=LIMIT),
        cost_estimate=SHORT,
        name="end_blocks",
    )(weight[None, :], near, far)


def blocks_kernel(clusters, share, marks, pattern, left, from_partner, from_far, *refs):
    dense = refs[len(marks) + 1]
    outs = refs[len(marks) + 2 :]
    add_pieces(marks, refs[: len(marks)], left, dense)
    for blocks, places in (
        (from_partner, ((0, -7), (0, -8), (1, -7))),
        (from_far, ((5, 12), (4, 12), (5, 13))),
    ):
        for at, (c, m) in enumerate(places):
            dense[natural(c, c), natural(m, m) + REACH] = blocks[at]
    base = lax.axis_index("wide") * CL - REACH
    me = lax.axis_index("narrow")
    for out, mask in zip(outs, (3, 1, 2, 0)):
        slot0 = (me ^ mask) * share
        for c in range(CL):
            for s in range(share):
                where = lax.rem(pattern[c, slot0 + s] - base + clusters, clusters)
                out[c, s] = dense[c, where]


def late_blocks(clusters, share, pattern, left, from_partner, from_far, pieces, dense):
    shapes = [jax.ShapeDtypeStruct(dense.shape, dense.dtype)]
    shapes += [jax.ShapeDtypeStruct((CL, share, B, B), jnp.bfloat16)] * 4
    return pl.pallas_call(
        functools.partial(blocks_kernel, clusters, share, list(pieces)),
        out_shape=shapes,
        in_specs=[SMEM] + [VMEM] * (4 + len(pieces)),
        out_specs=[VMEM] * len(shapes),
        input_output_aliases={4 + len(pieces): 0},
        compiler_params=pltpu.CompilerParams(vmem_limit_bytes=LIMIT),
        cost_estimate=SHORT,
        name="late_blocks",
    )(pattern, left, from_partner, from_far, *pieces.values(), dense)[1:]


def take_kernel(slab, after, out):
    row = (1 - lax.rem(lax.axis_index("wide"), 2)) * 2 * PAIR * B
    out[...] = slab[pl.ds(pl.multiple_of(row, PAIR * B), PAIR * B), :]


def take(slab, after):
    return pl.pallas_call(
        take_kernel,
        out_shape=jax.ShapeDtypeStruct((PAIR * B, slab.shape[1]), slab.dtype),
        in_specs=[VMEM] * 2,
        out_specs=VMEM,
        compiler_params=pltpu.CompilerParams(vmem_limit_bytes=LIMIT),
        cost_estimate=SHORT,
        name="take",
    )(slab, after)


def per_device(slab, occupation, column_band, pattern):
    clusters = CL * lax.axis_size("wide")
    share = pattern.shape[1] // lax.axis_size("narrow")
    odd = lax.axis_index("wide") % 2
    rows = PAIR * B
    partner = lambda w: w ^ 1

    picks = column_band[:, None] == jnp.arange(occupation.shape[0], dtype=jnp.int32)[None, :]
    weight = jnp.sum(jnp.where(picks, occupation[None, :], jnp.float32(0.0)), axis=1)
    scaled = (slab.astype(jnp.float32) * weight[None, :]).astype(jnp.bfloat16)

    near_rows = take(slab, weight)
    end_rows = lax.dynamic_slice_in_dim(slab, odd * 2 * rows, rows, 0)
    early = {0: slab}
    early[-6] = move(end_rows, "wide", partner)
    early[-4] = move(slab[rows : 2 * rows], "wide", partner)
    early[-2] = move(near_rows, "wide", partner)
    early[6] = move(early[-6], "wide", outward)
    early[8] = move(early[-4], "wide", outward)
    late = {10: move(early[-2], "wide", outward)}
    to_partner, to_far = end_blocks(weight, early[-2], early[6])
    from_partner = move(to_partner, "wide", partner)
    from_far = move(to_far, "wide", across)

    dense = early_blocks(scaled, early)
    send_far, send_near, keep_far, keep_near = late_blocks(
        clusters, share, pattern, scaled, from_partner, from_far, late, dense
    )
    got_far = move(send_far, "narrow", lambda n: n ^ 1)
    got_near = move(send_near, "narrow", lambda n: n ^ 1)
    far = (keep_far.astype(jnp.float32) + got_far.astype(jnp.float32)).astype(jnp.bfloat16)
    got = move(far, "narrow", lambda n: n ^ 2)
    near = keep_near.astype(jnp.float32) + got_near.astype(jnp.float32)
    return (near + got.astype(jnp.float32)).astype(jnp.bfloat16)


def solution(mesh):
    placed = (P("wide", "narrow"), P(), P("narrow"), P("wide", None))
    return jax.shard_map(
        per_device,
        mesh=mesh,
        in_specs=placed,
        out_specs=P("wide", "narrow", None, None),
        check_vma=False,
    )
```

```python
import functools

import jax
import jax.numpy as jnp
from jax import lax
from jax.experimental import pallas as pl
from jax.experimental.pallas import tpu as pltpu
from jax.sharding import PartitionSpec as P

B = 128
REACH = 8
CL = 6
PAIR = 2
VMEM = pl.BlockSpec(memory_space=pltpu.VMEM)
SMEM = pl.BlockSpec(memory_space=pltpu.SMEM)
LIMIT = 40 * 1024 * 1024
LONG = pl.CostEstimate(flops=20 * 10**9, bytes_accessed=1, transcendentals=0)
SHORT = pl.CostEstimate(flops=1, bytes_accessed=1, transcendentals=0)


def move(value, axis, target):
    count = lax.axis_size(axis)
    return lax.ppermute(value, axis, [(s, target(s) % count) for s in range(count)])


def outward(w):
    return w + 2 if w % 2 == 0 else w - 2


def across(w):
    return w - 1 if w % 2 == 0 else w + 1


def natural(low, high):
    odd = lax.rem(lax.axis_index("wide"), 2)
    return jnp.where(odd == 1, low, CL - 1 - high)


def multiply(left, right):
    product = lax.dot_general(left, right, (((1,), (1,)), ((), ())), preferred_element_type=jnp.float32)
    return product.astype(jnp.bfloat16)


def add_pieces(marks, pieces, left, dense):
    for piece, mark in zip(pieces, marks):
        count = piece.shape[0] // B
        for at in range(0, count, PAIR):
            low, high = mark + at, mark + at + PAIR - 1
            c0, c1 = max(0, low - REACH), min(CL - 1, high + REACH)
            offset, start, rows = natural(low, high), natural(c0, c1), (c1 - c0 + 1) * B
            row = pl.multiple_of((offset - natural(mark, mark + count - 1)) * B, PAIR * B)
            product = multiply(
                left[pl.ds(pl.multiple_of(start * B, B), rows), :], piece[pl.ds(row, PAIR * B), :]
            )
            for r in range(c1 - c0 + 1):
                for h in range(PAIR):
                    dense[start + r, offset + REACH + h] = product[r * B : (r + 1) * B, h * B : (h + 1) * B]


def pieces_kernel(marks, left, *refs):
    add_pieces(marks, refs[: len(marks)], left, refs[-1])


def pieces_blocks(left, pieces, cost, dense=None):
    held = [] if dense is None else [dense]
    return pl.pallas_call(
        functools.partial(pieces_kernel, list(pieces)),
        out_shape=jax.ShapeDtypeStruct((CL, CL + 2 * REACH, B, B), jnp.bfloat16),
        in_specs=[VMEM] * (1 + len(pieces) + len(held)),
        out_specs=VMEM,
        input_output_aliases={1 + len(pieces): 0} if held else {},
        compiler_params=pltpu.CompilerParams(vmem_limit_bytes=LIMIT),
        cost_estimate=cost,
        name="pieces_blocks",
    )(left, *pieces.values(), *held)


def ends_kernel(weight, near, far, to_partner, to_far):
    scaled = lambda rows: (rows[...].astype(jnp.float32) * weight[...]).astype(jnp.bfloat16)
    for out, left, right, keep in (
        (to_partner, near, far, ((-1, 6), (-1, 7), (-2, 6))),
        (to_far, far, near, ((6, -1), (7, -1), (6, -2))),
    ):
        product = multiply(scaled(left), right[...])
        odd = lax.rem(lax.axis_index("wide"), 2) == 1
        for at, (c, m) in enumerate(keep):
            spots = []
            for place in (c, m):
                low = -2 if place < 0 else 6
                spots.append((place - low, low + 1 - place))
            (co, mo), (ce, me) = [(spots[0][p], spots[1][p]) for p in (0, 1)]
            out[at] = jnp.where(
                odd,
                product[co * B : (co + 1) * B, mo * B : (mo + 1) * B],
                product[ce * B : (ce + 1) * B, me * B : (me + 1) * B],
            )


def end_blocks(weight, near, far):
    return pl.pallas_call(
        ends_kernel,
        out_shape=[jax.ShapeDtypeStruct((3, B, B), jnp.bfloat16)] * 2,
        in_specs=[VMEM] * 3,
        out_specs=[VMEM] * 2,
        compiler_params=pltpu.CompilerParams(vmem_limit_bytes=LIMIT),
        cost_estimate=SHORT,
        name="end_blocks",
    )(weight[None, :], near, far)


def choose_kernel(clusters, share, marks, pattern, left, from_partner, from_far, *refs):
    dense = refs[len(marks) + 1]
    outs = refs[len(marks) + 2 :]
    add_pieces(marks, refs[: len(marks)], left, dense)
    for blocks, places in (
        (from_partner, ((0, -7), (0, -8), (1, -7))),
        (from_far, ((5, 12), (4, 12), (5, 13))),
    ):
        for at, (c, m) in enumerate(places):
            dense[natural(c, c), natural(m, m) + REACH] = blocks[at]
    base = lax.axis_index("wide") * CL - REACH
    me = lax.axis_index("narrow")
    for out, mask in zip(outs, (3, 1, 2, 0)):
        slot0 = (me ^ mask) * share
        for c in range(CL):
            for s in range(share):
                where = lax.rem(pattern[c, slot0 + s] - base + clusters, clusters)
                out[c, s] = dense[c, where]


def choose_blocks(clusters, share, pattern, left, from_partner, from_far, pieces, dense):
    shapes = [jax.ShapeDtypeStruct(dense.shape, dense.dtype)]
    shapes += [jax.ShapeDtypeStruct((CL, share, B, B), jnp.bfloat16)] * 4
    return pl.pallas_call(
        functools.partial(choose_kernel, clusters, share, list(pieces)),
        out_shape=shapes,
        in_specs=[SMEM] + [VMEM] * (4 + len(pieces)),
        out_specs=[VMEM] * len(shapes),
        input_output_aliases={4 + len(pieces): 0},
        compiler_params=pltpu.CompilerParams(vmem_limit_bytes=LIMIT),
        cost_estimate=SHORT,
        name="choose_blocks",
    )(pattern, left, from_partner, from_far, *pieces.values(), dense)[1:]


def take_kernel(slab, after, out):
    row = lax.rem(lax.axis_index("wide"), 2) * 2 * PAIR * B
    out[...] = slab[pl.ds(pl.multiple_of(row, PAIR * B), PAIR * B), :]


def take(slab, after):
    return pl.pallas_call(
        take_kernel,
        out_shape=jax.ShapeDtypeStruct((PAIR * B, slab.shape[1]), slab.dtype),
        in_specs=[VMEM] * 2,
        out_specs=VMEM,
        compiler_params=pltpu.CompilerParams(vmem_limit_bytes=LIMIT),
        cost_estimate=SHORT,
        name="take",
    )(slab, after)


def per_device(slab, occupation, column_band, pattern):
    clusters = CL * lax.axis_size("wide")
    share = pattern.shape[1] // lax.axis_size("narrow")
    odd = lax.axis_index("wide") % 2
    rows = PAIR * B
    partner = lambda w: w ^ 1

    picks = column_band[:, None] == jnp.arange(occupation.shape[0], dtype=jnp.int32)[None, :]
    weight = jnp.sum(jnp.where(picks, occupation[None, :], jnp.float32(0.0)), axis=1)
    scaled = (slab.astype(jnp.float32) * weight[None, :]).astype(jnp.bfloat16)

    near_rows = lax.dynamic_slice_in_dim(slab, (1 - odd) * 2 * rows, rows, 0)
    end_rows = take(slab, weight)
    early = {0: slab}
    early[-4] = move(slab[rows : 2 * rows], "wide", partner)
    early[-2] = move(near_rows, "wide", partner)
    early[6] = move(end_rows, "wide", across)
    early[8] = move(early[-4], "wide", outward)
    middle = {10: move(early[-2], "wide", outward)}
    late = {-6: move(end_rows, "wide", partner)}
    to_partner, to_far = end_blocks(weight, early[-2], early[6])
    from_partner = move(to_partner, "wide", partner)
    from_far = move(to_far, "wide", across)

    dense = pieces_blocks(scaled, early, SHORT)
    dense = pieces_blocks(scaled, middle, LONG, dense)
    send_far, send_near, keep_far, keep_near = choose_blocks(
        clusters, share, pattern, scaled, from_partner, from_far, late, dense
    )
    got_far = move(send_far, "narrow", lambda n: n ^ 1)
    got_near = move(send_near, "narrow", lambda n: n ^ 1)
    far = (keep_far.astype(jnp.float32) + got_far.astype(jnp.float32)).astype(jnp.bfloat16)
    got = move(far, "narrow", lambda n: n ^ 2)
    near = keep_near.astype(jnp.float32) + got_near.astype(jnp.float32)
    return (near + got.astype(jnp.float32)).astype(jnp.bfloat16)


def solution(mesh):
    placed = (P("wide", "narrow"), P(), P("narrow"), P("wide", None))
    return jax.shard_map(
        per_device,
        mesh=mesh,
        in_specs=placed,
        out_specs=P("wide", "narrow", None, None),
        check_vma=False,
    )
```

```python
import functools

import jax
import jax.numpy as jnp
from jax import lax
from jax.experimental import pallas as pl
from jax.experimental.pallas import tpu as pltpu
from jax.sharding import PartitionSpec as P

B = 128
REACH = 8
CL = 6
PAIR = 2
VMEM = pl.BlockSpec(memory_space=pltpu.VMEM)
SMEM = pl.BlockSpec(memory_space=pltpu.SMEM)
LIMIT = 40 * 1024 * 1024
LONG = pl.CostEstimate(flops=20 * 10**9, bytes_accessed=1, transcendentals=0)
SHORT = pl.CostEstimate(flops=1, bytes_accessed=1, transcendentals=0)


def move(value, axis, target):
    count = lax.axis_size(axis)
    return lax.ppermute(value, axis, [(s, target(s) % count) for s in range(count)])


def outward(w):
    return w + 2 if w % 2 == 0 else w - 2


def across(w):
    return w - 1 if w % 2 == 0 else w + 1


def natural(low, high):
    odd = lax.rem(lax.axis_index("wide"), 2)
    return jnp.where(odd == 1, low, CL - 1 - high)


def multiply(left, right):
    product = lax.dot_general(left, right, (((1,), (1,)), ((), ())), preferred_element_type=jnp.float32)
    return product.astype(jnp.bfloat16)


def add_pieces(marks, pieces, left, dense):
    for piece, mark in zip(pieces, marks):
        count = piece.shape[0] // B
        for at in range(0, count, PAIR):
            low, high = mark + at, mark + at + PAIR - 1
            c0, c1 = max(0, low - REACH), min(CL - 1, high + REACH)
            offset, start, rows = natural(low, high), natural(c0, c1), (c1 - c0 + 1) * B
            row = pl.multiple_of((offset - natural(mark, mark + count - 1)) * B, PAIR * B)
            product = multiply(
                left[pl.ds(pl.multiple_of(start * B, B), rows), :], piece[pl.ds(row, PAIR * B), :]
            )
            for r in range(c1 - c0 + 1):
                for h in range(PAIR):
                    dense[start + r, offset + REACH + h] = product[r * B : (r + 1) * B, h * B : (h + 1) * B]


def pieces_kernel(marks, left, *refs):
    add_pieces(marks, refs[: len(marks)], left, refs[-1])


def pieces_blocks(left, pieces, cost, dense=None):
    held = [] if dense is None else [dense]
    return pl.pallas_call(
        functools.partial(pieces_kernel, list(pieces)),
        out_shape=jax.ShapeDtypeStruct((CL, CL + 2 * REACH, B, B), jnp.bfloat16),
        in_specs=[VMEM] * (1 + len(pieces) + len(held)),
        out_specs=VMEM,
        input_output_aliases={1 + len(pieces): 0} if held else {},
        compiler_params=pltpu.CompilerParams(vmem_limit_bytes=LIMIT),
        cost_estimate=cost,
        name="pieces_blocks",
    )(left, *pieces.values(), *held)


def ends_kernel(weight, near, far, to_partner, to_far):
    scaled = lambda rows: (rows[...].astype(jnp.float32) * weight[...]).astype(jnp.bfloat16)
    for out, left, right, keep in (
        (to_partner, near, far, ((-1, 6), (-1, 7), (-2, 6))),
        (to_far, far, near, ((6, -1), (7, -1), (6, -2))),
    ):
        product = multiply(scaled(left), right[...])
        odd = lax.rem(lax.axis_index("wide"), 2) == 1
        for at, (c, m) in enumerate(keep):
            spots = []
            for place in (c, m):
                low = -2 if place < 0 else 6
                spots.append((place - low, low + 1 - place))
            (co, mo), (ce, me) = [(spots[0][p], spots[1][p]) for p in (0, 1)]
            out[at] = jnp.where(
                odd,
                product[co * B : (co + 1) * B, mo * B : (mo + 1) * B],
                product[ce * B : (ce + 1) * B, me * B : (me + 1) * B],
            )


def end_blocks(weight, near, far):
    return pl.pallas_call(
        ends_kernel,
        out_shape=[jax.ShapeDtypeStruct((3, B, B), jnp.bfloat16)] * 2,
        in_specs=[VMEM] * 3,
        out_specs=[VMEM] * 2,
        compiler_params=pltpu.CompilerParams(vmem_limit_bytes=LIMIT),
        cost_estimate=SHORT,
        name="end_blocks",
    )(weight[None, :], near, far)


def choose_kernel(clusters, share, marks, pattern, left, from_partner, from_far, *refs):
    dense = refs[len(marks) + 1]
    outs = refs[len(marks) + 2 :]
    add_pieces(marks, refs[: len(marks)], left, dense)
    for blocks, places in (
        (from_partner, ((0, -7), (0, -8), (1, -7))),
        (from_far, ((5, 12), (4, 12), (5, 13))),
    ):
        for at, (c, m) in enumerate(places):
            dense[natural(c, c), natural(m, m) + REACH] = blocks[at]
    base = lax.axis_index("wide") * CL - REACH
    me = lax.axis_index("narrow")
    for out, mask in zip(outs, (3, 1, 2, 0)):
        slot0 = (me ^ mask) * share
        for c in range(CL):
            for s in range(share):
                where = lax.rem(pattern[c, slot0 + s] - base + clusters, clusters)
                out[c, s] = dense[c, where]


def choose_blocks(clusters, share, pattern, left, from_partner, from_far, pieces, dense):
    shapes = [jax.ShapeDtypeStruct(dense.shape, dense.dtype)]
    shapes += [jax.ShapeDtypeStruct((CL, share, B, B), jnp.bfloat16)] * 4
    return pl.pallas_call(
        functools.partial(choose_kernel, clusters, share, list(pieces)),
        out_shape=shapes,
        in_specs=[SMEM] + [VMEM] * (4 + len(pieces)),
        out_specs=[VMEM] * len(shapes),
        input_output_aliases={4 + len(pieces): 0},
        compiler_params=pltpu.CompilerParams(vmem_limit_bytes=LIMIT),
        cost_estimate=SHORT,
        name="choose_blocks",
    )(pattern, left, from_partner, from_far, *pieces.values(), dense)[1:]


def take_kernel(end, slab, after, out):
    row = lax.rem(lax.axis_index("wide"), 2) * 2 * PAIR * B if end else PAIR * B
    out[...] = slab[pl.ds(pl.multiple_of(row, PAIR * B), PAIR * B), :]


def take(slab, end, after):
    return pl.pallas_call(
        functools.partial(take_kernel, end),
        out_shape=jax.ShapeDtypeStruct((PAIR * B, slab.shape[1]), slab.dtype),
        in_specs=[VMEM] * 2,
        out_specs=VMEM,
        compiler_params=pltpu.CompilerParams(vmem_limit_bytes=LIMIT),
        cost_estimate=SHORT,
        name="take",
    )(slab, after)


def per_device(slab, occupation, column_band, pattern):
    clusters = CL * lax.axis_size("wide")
    share = pattern.shape[1] // lax.axis_size("narrow")
    odd = lax.axis_index("wide") % 2
    rows = PAIR * B
    partner = lambda w: w ^ 1

    picks = column_band[:, None] == jnp.arange(occupation.shape[0], dtype=jnp.int32)[None, :]
    weight = jnp.sum(jnp.where(picks, occupation[None, :], jnp.float32(0.0)), axis=1)
    scaled = (slab.astype(jnp.float32) * weight[None, :]).astype(jnp.bfloat16)

    near_rows = lax.dynamic_slice_in_dim(slab, (1 - odd) * 2 * rows, rows, 0)
    end_rows = lax.dynamic_slice_in_dim(slab, odd * 2 * rows, rows, 0)
    early = {0: slab}
    early[-2] = move(near_rows, "wide", partner)
    early[6] = move(end_rows, "wide", across)
    early[-4] = move(take(slab, False, early[-2]), "wide", partner)
    middle = {10: move(early[-2], "wide", outward)}
    late = {8: move(early[-4], "wide", outward)}
    late[-6] = move(take(slab, True, early[-2]), "wide", partner)
    to_partner, to_far = end_blocks(weight, early[-2], early[6])
    from_partner = move(to_partner, "wide", partner)
    from_far = move(to_far, "wide", across)

    dense = pieces_blocks(scaled, early, SHORT)
    dense = pieces_blocks(scaled, middle, LONG, dense)
    send_far, send_near, keep_far, keep_near = choose_blocks(
        clusters, share, pattern, scaled, from_partner, from_far, late, dense
    )
    got_far = move(send_far, "narrow", lambda n: n ^ 1)
    got_near = move(send_near, "narrow", lambda n: n ^ 1)
    far = (keep_far.astype(jnp.float32) + got_far.astype(jnp.float32)).astype(jnp.bfloat16)
    got = move(far, "narrow", lambda n: n ^ 2)
    near = keep_near.astype(jnp.float32) + got_near.astype(jnp.float32)
    return (near + got.astype(jnp.float32)).astype(jnp.bfloat16)


def solution(mesh):
    placed = (P("wide", "narrow"), P(), P("narrow"), P("wide", None))
    return jax.shard_map(
        per_device,
        mesh=mesh,
        in_specs=placed,
        out_specs=P("wide", "narrow", None, None),
        check_vma=False,
    )
```

```python
import functools

import jax
import jax.numpy as jnp
from jax import lax
from jax.experimental import pallas as pl
from jax.experimental.pallas import tpu as pltpu
from jax.sharding import PartitionSpec as P

B = 128
REACH = 8
CL = 6
PAIR = 2
VMEM = pl.BlockSpec(memory_space=pltpu.VMEM)
SMEM = pl.BlockSpec(memory_space=pltpu.SMEM)
LIMIT = 40 * 1024 * 1024
LONG = pl.CostEstimate(flops=20 * 10**9, bytes_accessed=1, transcendentals=0)
SHORT = pl.CostEstimate(flops=1, bytes_accessed=1, transcendentals=0)


def move(value, axis, target):
    count = lax.axis_size(axis)
    return lax.ppermute(value, axis, [(s, target(s) % count) for s in range(count)])


def outward(w):
    return w + 2 if w % 2 == 0 else w - 2


def natural(low, high):
    odd = lax.rem(lax.axis_index("wide"), 2)
    return jnp.where(odd == 1, low, CL - 1 - high)


def multiply(left, right):
    product = lax.dot_general(left, right, (((1,), (1,)), ((), ())), preferred_element_type=jnp.float32)
    return product.astype(jnp.bfloat16)


def add_pieces(marks, pieces, left, dense):
    for piece, mark in zip(pieces, marks):
        count = piece.shape[0] // B
        for at in range(0, count, PAIR):
            low, high = mark + at, mark + at + PAIR - 1
            c0, c1 = max(0, low - REACH), min(CL - 1, high + REACH)
            offset, start, rows = natural(low, high), natural(c0, c1), (c1 - c0 + 1) * B
            row = pl.multiple_of((offset - natural(mark, mark + count - 1)) * B, PAIR * B)
            product = multiply(
                left[pl.ds(pl.multiple_of(start * B, B), rows), :], piece[pl.ds(row, PAIR * B), :]
            )
            for r in range(c1 - c0 + 1):
                for h in range(PAIR):
                    dense[start + r, offset + REACH + h] = product[r * B : (r + 1) * B, h * B : (h + 1) * B]


def early_kernel(marks, left, *refs):
    add_pieces(marks, refs[:-1], left, refs[-1])


def early_blocks(left, pieces):
    return pl.pallas_call(
        functools.partial(early_kernel, list(pieces)),
        out_shape=jax.ShapeDtypeStruct((CL, CL + 2 * REACH, B, B), jnp.bfloat16),
        in_specs=[VMEM] * (1 + len(pieces)),
        out_specs=VMEM,
        compiler_params=pltpu.CompilerParams(vmem_limit_bytes=LIMIT),
        cost_estimate=LONG,
        name="early_blocks",
    )(left, *pieces.values())


def ends_kernel(weight, near, far, out):
    odd = lax.rem(lax.axis_index("wide"), 2) == 1
    left = (near[...].astype(jnp.float32) * weight[...]).astype(jnp.bfloat16)
    product = multiply(left, far[...])
    for at, (c, m) in enumerate(((-1, 6), (-1, 7), (-2, 6))):
        here, there = ((c + 2) * B, (m - 6) * B), ((-1 - c) * B, (7 - m) * B)
        one, two = [product[row : row + B, column : column + B] for row, column in (here, there)]
        out[at] = jnp.where(odd, one, two)


def end_blocks(weight, near, far):
    return pl.pallas_call(
        ends_kernel,
        out_shape=jax.ShapeDtypeStruct((3, B, B), jnp.bfloat16),
        in_specs=[VMEM] * 3,
        out_specs=VMEM,
        compiler_params=pltpu.CompilerParams(vmem_limit_bytes=LIMIT),
        cost_estimate=SHORT,
        name="end_blocks",
    )(weight[None, :], near, far)


def blocks_kernel(share, marks, places, left, from_partner, *refs):
    dense = refs[len(marks) + 1]
    outs = refs[len(marks) + 2 :]
    add_pieces(marks, refs[: len(marks)], left, dense)
    for at, (c, m) in enumerate(((0, -7), (0, -8), (1, -7))):
        dense[natural(c, c), natural(m, m) + REACH] = from_partner[at]
    me = lax.axis_index("narrow")
    for out, mask in zip(outs, (3, 1, 2, 0)):
        slot0 = (me ^ mask) * share
        for c in range(CL):
            for s in range(share):
                out[c, s] = dense[c, places[c, slot0 + s]]


def late_blocks(share, places, left, from_partner, pieces, dense):
    shapes = [jax.ShapeDtypeStruct(dense.shape, dense.dtype)]
    shapes += [jax.ShapeDtypeStruct((CL, share, B, B), jnp.bfloat16)] * 4
    return pl.pallas_call(
        functools.partial(blocks_kernel, share, list(pieces)),
        out_shape=shapes,
        in_specs=[SMEM] + [VMEM] * (3 + len(pieces)),
        out_specs=[VMEM] * len(shapes),
        input_output_aliases={3 + len(pieces): 0},
        compiler_params=pltpu.CompilerParams(vmem_limit_bytes=LIMIT),
        cost_estimate=SHORT,
        name="late_blocks",
    )(places, left, from_partner, *pieces.values(), dense)[1:]


def take_kernel(near, slab, after, out):
    odd = lax.rem(lax.axis_index("wide"), 2)
    row = (1 - odd if near else odd) * 2 * PAIR * B
    out[...] = slab[pl.ds(pl.multiple_of(row, PAIR * B), PAIR * B), :]


def take(slab, near, after):
    return pl.pallas_call(
        functools.partial(take_kernel, near),
        out_shape=jax.ShapeDtypeStruct((PAIR * B, slab.shape[1]), slab.dtype),
        in_specs=[VMEM] * 2,
        out_specs=VMEM,
        compiler_params=pltpu.CompilerParams(vmem_limit_bytes=LIMIT),
        cost_estimate=SHORT,
        name="take",
    )(slab, after)


def per_device(slab, occupation, column_band, pattern):
    clusters = CL * lax.axis_size("wide")
    share = pattern.shape[1] // lax.axis_size("narrow")
    odd = lax.axis_index("wide") % 2
    rows = PAIR * B
    partner = lambda w: w ^ 1

    places = jnp.mod(pattern - (lax.axis_index("wide") * CL - REACH), clusters)
    picks = column_band[:, None] == jnp.arange(occupation.shape[0], dtype=jnp.int32)[None, :]
    weight = jnp.sum(jnp.where(picks, occupation[None, :], jnp.float32(0.0)), axis=1)
    scaled = (slab.astype(jnp.float32) * weight[None, :]).astype(jnp.bfloat16)

    near_rows = lax.dynamic_slice_in_dim(slab, (1 - odd) * 2 * rows, rows, 0)
    end_rows = lax.dynamic_slice_in_dim(slab, odd * 2 * rows, rows, 0)
    early = {0: slab}
    early[-2] = move(take(slab, True, places), "wide", partner)
    early[-6] = move(take(slab, False, places), "wide", partner)
    early[-4] = move(slab[rows : 2 * rows], "wide", partner)
    early[12] = move(near_rows, "wide", outward)
    early[10] = move(early[-2], "wide", outward)
    early[6] = move(early[-6], "wide", outward)
    late = {8: move(early[-4], "wide", outward)}
    from_partner = move(end_blocks(weight, early[-2], early[6]), "wide", partner)

    dense = early_blocks(scaled, early)
    send_far, send_near, keep_far, keep_near = late_blocks(
        share, places, scaled, from_partner, late, dense
    )
    got_far = move(send_far, "narrow", lambda n: n ^ 1)
    got_near = move(send_near, "narrow", lambda n: n ^ 1)
    far = (keep_far.astype(jnp.float32) + got_far.astype(jnp.float32)).astype(jnp.bfloat16)
    got = move(far, "narrow", lambda n: n ^ 2)
    near = keep_near.astype(jnp.float32) + got_near.astype(jnp.float32)
    return (near + got.astype(jnp.float32)).astype(jnp.bfloat16)


def solution(mesh):
    placed = (P("wide", "narrow"), P(), P("narrow"), P("wide", None))
    return jax.shard_map(
        per_device,
        mesh=mesh,
        in_specs=placed,
        out_specs=P("wide", "narrow", None, None),
        check_vma=False,
    )
```

```python
import functools

import jax
import jax.numpy as jnp
from jax import lax
from jax.experimental import pallas as pl
from jax.experimental.pallas import tpu as pltpu
from jax.sharding import PartitionSpec as P

B = 128
REACH = 8
CL = 6
PAIR = 2
VMEM = pl.BlockSpec(memory_space=pltpu.VMEM)
SMEM = pl.BlockSpec(memory_space=pltpu.SMEM)
LIMIT = 40 * 1024 * 1024
LONG = pl.CostEstimate(flops=20 * 10**9, bytes_accessed=1, transcendentals=0)
SHORT = pl.CostEstimate(flops=1, bytes_accessed=1, transcendentals=0)


def move(value, axis, target):
    count = lax.axis_size(axis)
    return lax.ppermute(value, axis, [(s, target(s) % count) for s in range(count)])


def outward(w):
    return w + 2 if w % 2 == 0 else w - 2


def natural(low, high):
    odd = lax.rem(lax.axis_index("wide"), 2)
    return jnp.where(odd == 1, low, CL - 1 - high)


def multiply(left, right):
    product = lax.dot_general(left, right, (((1,), (1,)), ((), ())), preferred_element_type=jnp.float32)
    return product.astype(jnp.bfloat16)


def add_pieces(marks, pieces, left, dense):
    for piece, mark in zip(pieces, marks):
        count = piece.shape[0] // B
        for at in range(0, count, PAIR):
            low, high = mark + at, mark + at + PAIR - 1
            c0, c1 = max(0, low - REACH), min(CL - 1, high + REACH)
            offset, start, rows = natural(low, high), natural(c0, c1), (c1 - c0 + 1) * B
            row = pl.multiple_of((offset - natural(mark, mark + count - 1)) * B, PAIR * B)
            product = multiply(
                left[pl.ds(pl.multiple_of(start * B, B), rows), :], piece[pl.ds(row, PAIR * B), :]
            )
            for r in range(c1 - c0 + 1):
                for h in range(PAIR):
                    dense[start + r, offset + REACH + h] = product[r * B : (r + 1) * B, h * B : (h + 1) * B]


def early_kernel(marks, left, *refs):
    add_pieces(marks, refs[:-1], left, refs[-1])


def early_blocks(left, pieces):
    return pl.pallas_call(
        functools.partial(early_kernel, list(pieces)),
        out_shape=jax.ShapeDtypeStruct((CL, CL + 2 * REACH, B, B), jnp.bfloat16),
        in_specs=[VMEM] * (1 + len(pieces)),
        out_specs=VMEM,
        compiler_params=pltpu.CompilerParams(vmem_limit_bytes=LIMIT),
        cost_estimate=LONG,
        name="early_blocks",
    )(left, *pieces.values())


def ends_kernel(weight, near, far, out):
    odd = lax.rem(lax.axis_index("wide"), 2) == 1
    left = (near[...].astype(jnp.float32) * weight[...]).astype(jnp.bfloat16)
    product = multiply(left, far[...])
    for at, (c, m) in enumerate(((-1, 6), (-1, 7), (-2, 6))):
        here, there = ((c + 2) * B, (m - 6) * B), ((-1 - c) * B, (7 - m) * B)
        one, two = [product[row : row + B, column : column + B] for row, column in (here, there)]
        out[at] = jnp.where(odd, one, two)


def end_blocks(weight, near, far):
    return pl.pallas_call(
        ends_kernel,
        out_shape=jax.ShapeDtypeStruct((3, B, B), jnp.bfloat16),
        in_specs=[VMEM] * 3,
        out_specs=VMEM,
        compiler_params=pltpu.CompilerParams(vmem_limit_bytes=LIMIT),
        cost_estimate=SHORT,
        name="end_blocks",
    )(weight[None, :], near, far)


def blocks_kernel(share, marks, places, left, from_partner, *refs):
    dense = refs[len(marks) + 1]
    outs = refs[len(marks) + 2 :]
    add_pieces(marks, refs[: len(marks)], left, dense)
    for at, (c, m) in enumerate(((0, -7), (0, -8), (1, -7))):
        dense[natural(c, c), natural(m, m) + REACH] = from_partner[at]
    me = lax.axis_index("narrow")
    for out, mask in zip(outs, (3, 1, 2, 0)):
        slot0 = (me ^ mask) * share
        for c in range(CL):
            for s in range(share):
                out[c, s] = dense[c, places[c, slot0 + s]]


def late_blocks(share, places, left, from_partner, pieces, dense):
    shapes = [jax.ShapeDtypeStruct(dense.shape, dense.dtype)]
    shapes += [jax.ShapeDtypeStruct((CL, share, B, B), jnp.bfloat16)] * 4
    return pl.pallas_call(
        functools.partial(blocks_kernel, share, list(pieces)),
        out_shape=shapes,
        in_specs=[SMEM] + [VMEM] * (3 + len(pieces)),
        out_specs=[VMEM] * len(shapes),
        input_output_aliases={3 + len(pieces): 0},
        compiler_params=pltpu.CompilerParams(vmem_limit_bytes=LIMIT),
        cost_estimate=SHORT,
        name="late_blocks",
    )(places, left, from_partner, *pieces.values(), dense)[1:]


def take_kernel(which, slab, after, out, done):
    odd = lax.rem(lax.axis_index("wide"), 2)
    row = {"end": odd * 2, "middle": 1, "near": (1 - odd) * 2}[which] * PAIR * B
    copy = pltpu.make_async_copy(slab.at[pl.ds(pl.multiple_of(row, PAIR * B), PAIR * B), :], out, done)
    copy.start()
    copy.wait()


def take(slab, which, after):
    return pl.pallas_call(
        functools.partial(take_kernel, which),
        out_shape=jax.ShapeDtypeStruct((PAIR * B, slab.shape[1]), slab.dtype),
        in_specs=[pl.BlockSpec(memory_space=pl.ANY), VMEM],
        out_specs=VMEM,
        scratch_shapes=[pltpu.SemaphoreType.DMA],
        compiler_params=pltpu.CompilerParams(vmem_limit_bytes=LIMIT),
        cost_estimate=SHORT,
        name=f"take_{which}",
    )(slab, after)


def per_device(slab, occupation, column_band, pattern):
    clusters = CL * lax.axis_size("wide")
    share = pattern.shape[1] // lax.axis_size("narrow")
    odd = lax.axis_index("wide") % 2
    rows = PAIR * B
    partner = lambda w: w ^ 1

    places = jnp.mod(pattern - (lax.axis_index("wide") * CL - REACH), clusters)
    picks = column_band[:, None] == jnp.arange(occupation.shape[0], dtype=jnp.int32)[None, :]
    weight = jnp.sum(jnp.where(picks, occupation[None, :], jnp.float32(0.0)), axis=1)
    scaled = (slab.astype(jnp.float32) * weight[None, :]).astype(jnp.bfloat16)

    early = {0: slab}
    near_rows = take(slab, "near", jnp.zeros((8, 128), jnp.float32))
    end_rows = take(slab, "end", jnp.zeros((8, 128), jnp.float32))
    middle_rows = take(slab, "middle", places)
    later_rows = take(slab, "near", places.astype(jnp.float32))
    early[-2] = move(near_rows, "wide", partner)
    early[-6] = move(end_rows, "wide", partner)
    early[-4] = move(middle_rows, "wide", partner)
    early[12] = move(later_rows, "wide", outward)
    early[10] = move(early[-2], "wide", outward)
    early[6] = move(early[-6], "wide", outward)
    late = {8: move(early[-4], "wide", outward)}
    from_partner = move(end_blocks(weight, early[-2], early[6]), "wide", partner)

    dense = early_blocks(scaled, early)
    send_far, send_near, keep_far, keep_near = late_blocks(
        share, places, scaled, from_partner, late, dense
    )
    got_far = move(send_far, "narrow", lambda n: n ^ 1)
    got_near = move(send_near, "narrow", lambda n: n ^ 1)
    far = (keep_far.astype(jnp.float32) + got_far.astype(jnp.float32)).astype(jnp.bfloat16)
    got = move(far, "narrow", lambda n: n ^ 2)
    near = keep_near.astype(jnp.float32) + got_near.astype(jnp.float32)
    return (near + got.astype(jnp.float32)).astype(jnp.bfloat16)


def solution(mesh):
    placed = (P("wide", "narrow"), P(), P("narrow"), P("wide", None))
    return jax.shard_map(
        per_device,
        mesh=mesh,
        in_specs=placed,
        out_specs=P("wide", "narrow", None, None),
        check_vma=False,
    )
```

```python
import functools

import jax
import jax.numpy as jnp
from jax import lax
from jax.experimental import pallas as pl
from jax.experimental.pallas import tpu as pltpu
from jax.sharding import PartitionSpec as P

B = 128
REACH = 8
CL = 6
PAIR = 2
VMEM = pl.BlockSpec(memory_space=pltpu.VMEM)
SMEM = pl.BlockSpec(memory_space=pltpu.SMEM)
LIMIT = 40 * 1024 * 1024
LONG = pl.CostEstimate(flops=20 * 10**9, bytes_accessed=1, transcendentals=0)
SHORT = pl.CostEstimate(flops=1, bytes_accessed=1, transcendentals=0)


def move(value, axis, target):
    count = lax.axis_size(axis)
    return lax.ppermute(value, axis, [(s, target(s) % count) for s in range(count)])


def outward(w):
    return w + 2 if w % 2 == 0 else w - 2


def natural(low, high):
    odd = lax.rem(lax.axis_index("wide"), 2)
    return jnp.where(odd == 1, low, CL - 1 - high)


def multiply(left, right):
    product = lax.dot_general(left, right, (((1,), (1,)), ((), ())), preferred_element_type=jnp.float32)
    return product.astype(jnp.bfloat16)


def add_pieces(marks, pieces, left, dense):
    for piece, mark in zip(pieces, marks):
        count = piece.shape[0] // B
        for at in range(0, count, PAIR):
            low, high = mark + at, mark + at + PAIR - 1
            c0, c1 = max(0, low - REACH), min(CL - 1, high + REACH)
            offset, start, rows = natural(low, high), natural(c0, c1), (c1 - c0 + 1) * B
            row = pl.multiple_of((offset - natural(mark, mark + count - 1)) * B, PAIR * B)
            product = multiply(
                left[pl.ds(pl.multiple_of(start * B, B), rows), :], piece[pl.ds(row, PAIR * B), :]
            )
            for r in range(c1 - c0 + 1):
                for h in range(PAIR):
                    dense[start + r, offset + REACH + h] = product[r * B : (r + 1) * B, h * B : (h + 1) * B]


def pieces_kernel(marks, left, *refs):
    add_pieces(marks, refs[: len(marks)], left, refs[-1])


def pieces_blocks(left, pieces, cost, dense=None):
    held = [] if dense is None else [dense]
    return pl.pallas_call(
        functools.partial(pieces_kernel, list(pieces)),
        out_shape=jax.ShapeDtypeStruct((CL, CL + 2 * REACH, B, B), jnp.bfloat16),
        in_specs=[VMEM] * (1 + len(pieces) + len(held)),
        out_specs=VMEM,
        input_output_aliases={1 + len(pieces): 0} if held else {},
        compiler_params=pltpu.CompilerParams(vmem_limit_bytes=LIMIT),
        cost_estimate=cost,
        name="pieces_blocks",
    )(left, *pieces.values(), *held)


def ends_kernel(weight, near, far, out):
    odd = lax.rem(lax.axis_index("wide"), 2) == 1
    left = (near[...].astype(jnp.float32) * weight[...]).astype(jnp.bfloat16)
    product = multiply(left, far[...])
    for at, (c, m) in enumerate(((-1, 6), (-1, 7), (-2, 6))):
        here, there = ((c + 2) * B, (m - 6) * B), ((-1 - c) * B, (7 - m) * B)
        one, two = [product[row : row + B, column : column + B] for row, column in (here, there)]
        out[at] = jnp.where(odd, one, two)


def end_blocks(weight, near, far):
    return pl.pallas_call(
        ends_kernel,
        out_shape=jax.ShapeDtypeStruct((3, B, B), jnp.bfloat16),
        in_specs=[VMEM] * 3,
        out_specs=VMEM,
        compiler_params=pltpu.CompilerParams(vmem_limit_bytes=LIMIT),
        cost_estimate=SHORT,
        name="end_blocks",
    )(weight[None, :], near, far)


def choose_kernel(share, marks, chunk, ends, places, left, from_partner, after, *refs):
    dense = refs[len(marks) + 1]
    outs = refs[len(marks) + 2 :]
    add_pieces(marks, refs[: len(marks)], left, dense)
    if ends:
        for at, (c, m) in enumerate(((0, -7), (0, -8), (1, -7))):
            dense[natural(c, c), natural(m, m) + REACH] = from_partner[at]
    first, last = chunk
    start = natural(first, last)
    me = lax.axis_index("narrow")
    for out, mask in zip(outs, (3, 1, 2, 0)):
        slot0 = (me ^ mask) * share
        for c in range(last - first + 1):
            for s in range(share):
                out[c, s] = dense[start + c, places[start + c, slot0 + s]]


def choose_blocks(share, chunk, ends, places, left, from_partner, after, pieces, dense):
    shapes = [jax.ShapeDtypeStruct(dense.shape, dense.dtype)]
    shapes += [jax.ShapeDtypeStruct((chunk[1] - chunk[0] + 1, share, B, B), jnp.bfloat16)] * 4
    return pl.pallas_call(
        functools.partial(choose_kernel, share, list(pieces), chunk, ends),
        out_shape=shapes,
        in_specs=[SMEM] + [VMEM] * (4 + len(pieces)),
        out_specs=[VMEM] * len(shapes),
        input_output_aliases={4 + len(pieces): 0},
        compiler_params=pltpu.CompilerParams(vmem_limit_bytes=LIMIT),
        cost_estimate=SHORT,
        name="choose_blocks",
    )(places, left, from_partner, after, *pieces.values(), dense)


def add_kernel(x, y, out):
    out[...] = (x[...].astype(jnp.float32) + y[...].astype(jnp.float32)).astype(jnp.bfloat16)


def add(x, y):
    return pl.pallas_call(
        add_kernel,
        out_shape=jax.ShapeDtypeStruct(x.shape, x.dtype),
        in_specs=[VMEM] * 2,
        out_specs=VMEM,
        compiler_params=pltpu.CompilerParams(vmem_limit_bytes=LIMIT),
        cost_estimate=SHORT,
        name="add",
    )(x, y)


def total_kernel(near, got_near, got, out):
    total = near[...].astype(jnp.float32) + got_near[...].astype(jnp.float32) + got[...].astype(jnp.float32)
    out[...] = total.astype(jnp.bfloat16)


def total(near, got_near, got):
    return pl.pallas_call(
        total_kernel,
        out_shape=jax.ShapeDtypeStruct(near.shape, near.dtype),
        in_specs=[VMEM] * 3,
        out_specs=VMEM,
        compiler_params=pltpu.CompilerParams(vmem_limit_bytes=LIMIT),
        cost_estimate=LONG,
        name="total",
    )(near, got_near, got)


def finish_kernel(chunks, early, near, got_near, got, out):
    start, later = [natural(first, last) for first, last in chunks]
    for r in range(early.shape[0]):
        out[start + r] = early[r]
    for r in range(near.shape[0]):
        total = near[r].astype(jnp.float32) + got_near[r].astype(jnp.float32) + got[r].astype(jnp.float32)
        out[later + r] = total.astype(jnp.bfloat16)


def finish(chunks, early, near, got_near, got):
    return pl.pallas_call(
        functools.partial(finish_kernel, chunks),
        out_shape=jax.ShapeDtypeStruct((CL,) + near.shape[1:], near.dtype),
        in_specs=[VMEM] * 4,
        out_specs=VMEM,
        compiler_params=pltpu.CompilerParams(vmem_limit_bytes=LIMIT),
        cost_estimate=SHORT,
        name="finish",
    )(early, near, got_near, got)


def take_kernel(which, slab, after, out, done):
    odd = lax.rem(lax.axis_index("wide"), 2)
    row = {"end": odd * 2, "middle": 1, "near": (1 - odd) * 2}[which] * PAIR * B
    copy = pltpu.make_async_copy(slab.at[pl.ds(pl.multiple_of(row, PAIR * B), PAIR * B), :], out, done)
    copy.start()
    copy.wait()


def take(slab, which, after):
    return pl.pallas_call(
        functools.partial(take_kernel, which),
        out_shape=jax.ShapeDtypeStruct((PAIR * B, slab.shape[1]), slab.dtype),
        in_specs=[pl.BlockSpec(memory_space=pltpu.HBM), VMEM],
        out_specs=VMEM,
        scratch_shapes=[pltpu.SemaphoreType.DMA],
        compiler_params=pltpu.CompilerParams(vmem_limit_bytes=LIMIT),
        cost_estimate=SHORT,
        name=f"take_{which}",
    )(slab, after)


def per_device(slab, occupation, column_band, pattern):
    clusters = CL * lax.axis_size("wide")
    share = pattern.shape[1] // lax.axis_size("narrow")
    odd = lax.axis_index("wide") % 2
    rows = PAIR * B
    partner = lambda w: w ^ 1

    places = jnp.mod(pattern - (lax.axis_index("wide") * CL - REACH), clusters)
    picks = column_band[:, None] == jnp.arange(occupation.shape[0], dtype=jnp.int32)[None, :]
    weight = jnp.sum(jnp.where(picks, occupation[None, :], jnp.float32(0.0)), axis=1)
    scaled = (slab.astype(jnp.float32) * weight[None, :]).astype(jnp.bfloat16)

    early = {0: slab}
    end_rows = take(slab, "end", jnp.zeros((8, 128), jnp.float32))
    early[-6] = move(end_rows, "wide", partner)
    near_rows = take(slab, "near", end_rows)
    early[12] = move(near_rows, "wide", outward)
    early[-4] = move(take(slab, "middle", near_rows), "wide", partner)
    early[6] = move(early[-6], "wide", outward)
    middle = {-2: move(take(slab, "near", early[-6]), "wide", partner)}
    middle[8] = move(early[-4], "wide", outward)
    late = {10: move(middle[-2], "wide", outward)}
    from_partner = move(end_blocks(weight, middle[-2], early[6]), "wide", partner)

    dense = pieces_blocks(scaled, early, LONG)
    dense = pieces_blocks(scaled, middle, LONG, dense)
    chunks = ((0, 1), (2, 5))

    parts = []
    after = scaled
    for pieces, chunk, ends in (({}, chunks[0], True), (late, chunks[1], False)):
        dense, send_far, send_near, keep_far, keep_near = choose_blocks(
            share, chunk, ends, places, scaled, from_partner, after, pieces, dense
        )
        got_far = move(send_far, "narrow", lambda n: n ^ 1)
        got_near = move(send_near, "narrow", lambda n: n ^ 1)
        parts.append((keep_near, got_near, move(add(keep_far, got_far), "narrow", lambda n: n ^ 2)))
        after = got_far
    return finish(chunks, total(*parts[0]), *parts[1])


def solution(mesh):
    placed = (P("wide", "narrow"), P(), P("narrow"), P("wide", None))
    return jax.shard_map(
        per_device,
        mesh=mesh,
        in_specs=placed,
        out_specs=P("wide", "narrow", None, None),
        check_vma=False,
    )
```

```python
import functools

import jax
import jax.numpy as jnp
from jax import lax
from jax.experimental import pallas as pl
from jax.experimental.pallas import tpu as pltpu
from jax.sharding import PartitionSpec as P

B = 128
REACH = 8
CL = 6
PAIR = 2
VMEM = pl.BlockSpec(memory_space=pltpu.VMEM)
SMEM = pl.BlockSpec(memory_space=pltpu.SMEM)
LIMIT = 40 * 1024 * 1024
LONG = pl.CostEstimate(flops=20 * 10**9, bytes_accessed=1, transcendentals=0)
SHORT = pl.CostEstimate(flops=1, bytes_accessed=1, transcendentals=0)


def move(value, axis, target):
    count = lax.axis_size(axis)
    return lax.ppermute(value, axis, [(s, target(s) % count) for s in range(count)])


def outward(w):
    return w + 2 if w % 2 == 0 else w - 2


def natural(low, high):
    odd = lax.rem(lax.axis_index("wide"), 2)
    return jnp.where(odd == 1, low, CL - 1 - high)


def multiply(left, right):
    product = lax.dot_general(left, right, (((1,), (1,)), ((), ())), preferred_element_type=jnp.float32)
    return product.astype(jnp.bfloat16)


def add_pieces(marks, pieces, left, dense):
    for piece, mark in zip(pieces, marks):
        count = piece.shape[0] // B
        for at in range(0, count, PAIR):
            low, high = mark + at, mark + at + PAIR - 1
            c0, c1 = max(0, low - REACH), min(CL - 1, high + REACH)
            offset, start, rows = natural(low, high), natural(c0, c1), (c1 - c0 + 1) * B
            row = pl.multiple_of((offset - natural(mark, mark + count - 1)) * B, PAIR * B)
            product = multiply(
                left[pl.ds(pl.multiple_of(start * B, B), rows), :], piece[pl.ds(row, PAIR * B), :]
            )
            for r in range(c1 - c0 + 1):
                for h in range(PAIR):
                    dense[start + r, offset + REACH + h] = product[r * B : (r + 1) * B, h * B : (h + 1) * B]


def pieces_kernel(marks, left, *refs):
    add_pieces(marks, refs[: len(marks)], left, refs[-1])


def pieces_blocks(left, pieces, cost, dense=None):
    held = [] if dense is None else [dense]
    return pl.pallas_call(
        functools.partial(pieces_kernel, list(pieces)),
        out_shape=jax.ShapeDtypeStruct((CL, CL + 2 * REACH, B, B), jnp.bfloat16),
        in_specs=[VMEM] * (1 + len(pieces) + len(held)),
        out_specs=VMEM,
        input_output_aliases={1 + len(pieces): 0} if held else {},
        compiler_params=pltpu.CompilerParams(vmem_limit_bytes=LIMIT),
        cost_estimate=cost,
        name="pieces_blocks",
    )(left, *pieces.values(), *held)


def ends_kernel(weight, near, far, out):
    odd = lax.rem(lax.axis_index("wide"), 2) == 1
    left = (near[...].astype(jnp.float32) * weight[...]).astype(jnp.bfloat16)
    product = multiply(left, far[...])
    for at, (c, m) in enumerate(((-1, 6), (-1, 7), (-2, 6))):
        here, there = ((c + 2) * B, (m - 6) * B), ((-1 - c) * B, (7 - m) * B)
        one, two = [product[row : row + B, column : column + B] for row, column in (here, there)]
        out[at] = jnp.where(odd, one, two)


def end_blocks(weight, near, far):
    return pl.pallas_call(
        ends_kernel,
        out_shape=jax.ShapeDtypeStruct((3, B, B), jnp.bfloat16),
        in_specs=[VMEM] * 3,
        out_specs=VMEM,
        compiler_params=pltpu.CompilerParams(vmem_limit_bytes=LIMIT),
        cost_estimate=SHORT,
        name="end_blocks",
    )(weight[None, :], near, far)


def choose_kernel(share, marks, chunk, ends, places, left, from_partner, after, *refs):
    dense = refs[len(marks) + 1]
    outs = refs[len(marks) + 2 :]
    add_pieces(marks, refs[: len(marks)], left, dense)
    if ends:
        for at, (c, m) in enumerate(((0, -7), (0, -8), (1, -7))):
            dense[natural(c, c), natural(m, m) + REACH] = from_partner[at]
    first, last = chunk
    start = natural(first, last)
    me = lax.axis_index("narrow")
    for out, mask in zip(outs, (3, 1, 2, 0)):
        slot0 = (me ^ mask) * share
        for c in range(last - first + 1):
            for s in range(share):
                out[c, s] = dense[start + c, places[start + c, slot0 + s]]


def choose_blocks(share, chunk, ends, places, left, from_partner, after, pieces, dense):
    shapes = [jax.ShapeDtypeStruct(dense.shape, dense.dtype)]
    shapes += [jax.ShapeDtypeStruct((chunk[1] - chunk[0] + 1, share, B, B), jnp.bfloat16)] * 4
    return pl.pallas_call(
        functools.partial(choose_kernel, share, list(pieces), chunk, ends),
        out_shape=shapes,
        in_specs=[SMEM] + [VMEM] * (4 + len(pieces)),
        out_specs=[VMEM] * len(shapes),
        input_output_aliases={4 + len(pieces): 0},
        compiler_params=pltpu.CompilerParams(vmem_limit_bytes=LIMIT),
        cost_estimate=SHORT,
        name="choose_blocks",
    )(places, left, from_partner, after, *pieces.values(), dense)


def add_kernel(x, y, out):
    out[...] = (x[...].astype(jnp.float32) + y[...].astype(jnp.float32)).astype(jnp.bfloat16)


def add(x, y):
    return pl.pallas_call(
        add_kernel,
        out_shape=jax.ShapeDtypeStruct(x.shape, x.dtype),
        in_specs=[VMEM] * 2,
        out_specs=VMEM,
        compiler_params=pltpu.CompilerParams(vmem_limit_bytes=LIMIT),
        cost_estimate=SHORT,
        name="add",
    )(x, y)


def total_kernel(near, got_near, got, out):
    total = near[...].astype(jnp.float32) + got_near[...].astype(jnp.float32) + got[...].astype(jnp.float32)
    out[...] = total.astype(jnp.bfloat16)


def total(near, got_near, got):
    return pl.pallas_call(
        total_kernel,
        out_shape=jax.ShapeDtypeStruct(near.shape, near.dtype),
        in_specs=[VMEM] * 3,
        out_specs=VMEM,
        compiler_params=pltpu.CompilerParams(vmem_limit_bytes=LIMIT),
        cost_estimate=LONG,
        name="total",
    )(near, got_near, got)


def finish_kernel(chunks, early, near, got_near, got, out):
    start, later = [natural(first, last) for first, last in chunks]
    for r in range(early.shape[0]):
        out[start + r] = early[r]
    for r in range(near.shape[0]):
        total = near[r].astype(jnp.float32) + got_near[r].astype(jnp.float32) + got[r].astype(jnp.float32)
        out[later + r] = total.astype(jnp.bfloat16)


def finish(chunks, early, near, got_near, got):
    return pl.pallas_call(
        functools.partial(finish_kernel, chunks),
        out_shape=jax.ShapeDtypeStruct((CL,) + near.shape[1:], near.dtype),
        in_specs=[VMEM] * 4,
        out_specs=VMEM,
        compiler_params=pltpu.CompilerParams(vmem_limit_bytes=LIMIT),
        cost_estimate=SHORT,
        name="finish",
    )(early, near, got_near, got)


def take_kernel(which, slab, after, out, done):
    odd = lax.rem(lax.axis_index("wide"), 2)
    row = {"end": odd * 2, "middle": 1, "near": (1 - odd) * 2}[which] * PAIR * B
    copy = pltpu.make_async_copy(slab.at[pl.ds(pl.multiple_of(row, PAIR * B), PAIR * B), :], out, done)
    copy.start()
    copy.wait()


def take(slab, which, after):
    return pl.pallas_call(
        functools.partial(take_kernel, which),
        out_shape=jax.ShapeDtypeStruct((PAIR * B, slab.shape[1]), slab.dtype),
        in_specs=[pl.BlockSpec(memory_space=pltpu.HBM), VMEM],
        out_specs=VMEM,
        scratch_shapes=[pltpu.SemaphoreType.DMA],
        compiler_params=pltpu.CompilerParams(vmem_limit_bytes=LIMIT),
        cost_estimate=SHORT,
        name=f"take_{which}",
    )(slab, after)


def per_device(slab, occupation, column_band, pattern):
    clusters = CL * lax.axis_size("wide")
    share = pattern.shape[1] // lax.axis_size("narrow")
    odd = lax.axis_index("wide") % 2
    rows = PAIR * B
    partner = lambda w: w ^ 1

    places = jnp.mod(pattern - (lax.axis_index("wide") * CL - REACH), clusters)
    picks = column_band[:, None] == jnp.arange(occupation.shape[0], dtype=jnp.int32)[None, :]
    weight = jnp.sum(jnp.where(picks, occupation[None, :], jnp.float32(0.0)), axis=1)
    scaled = (slab.astype(jnp.float32) * weight[None, :]).astype(jnp.bfloat16)

    early = {0: slab}
    middle_rows = take(slab, "middle", jnp.zeros((8, 128), jnp.float32))
    end_rows = take(slab, "end", jnp.zeros((8, 128), jnp.float32))
    later_rows = take(slab, "near", places)
    near_rows = take(slab, "near", places.astype(jnp.float32))
    early[-4] = move(middle_rows, "wide", partner)
    early[-6] = move(end_rows, "wide", partner)
    early[12] = move(later_rows, "wide", outward)
    near = move(near_rows, "wide", partner)
    early[8] = move(early[-4], "wide", outward)
    early[6] = move(early[-6], "wide", outward)
    early[-2] = near
    late = {10: move(near, "wide", outward)}
    from_partner = move(end_blocks(weight, near, early[6]), "wide", partner)

    dense = pieces_blocks(scaled, early, LONG)
    chunks = ((0, 1), (2, 5))

    parts = []
    after = scaled
    for pieces, chunk, ends in (({}, chunks[0], True), (late, chunks[1], False)):
        dense, send_far, send_near, keep_far, keep_near = choose_blocks(
            share, chunk, ends, places, scaled, from_partner, after, pieces, dense
        )
        got_far = move(send_far, "narrow", lambda n: n ^ 1)
        got_near = move(send_near, "narrow", lambda n: n ^ 1)
        parts.append((keep_near, got_near, move(add(keep_far, got_far), "narrow", lambda n: n ^ 2)))
        after = got_far
    return finish(chunks, total(*parts[0]), *parts[1])


def solution(mesh):
    placed = (P("wide", "narrow"), P(), P("narrow"), P("wide", None))
    return jax.shard_map(
        per_device,
        mesh=mesh,
        in_specs=placed,
        out_specs=P("wide", "narrow", None, None),
        check_vma=False,
    )
```

```python
import functools

import jax
import jax.numpy as jnp
from jax import lax
from jax.experimental import pallas as pl
from jax.experimental.pallas import tpu as pltpu
from jax.sharding import PartitionSpec as P

B = 128
REACH = 8
CL = 6
PAIR = 2
VMEM = pl.BlockSpec(memory_space=pltpu.VMEM)
SMEM = pl.BlockSpec(memory_space=pltpu.SMEM)
LIMIT = 40 * 1024 * 1024
LONG = pl.CostEstimate(flops=20 * 10**9, bytes_accessed=1, transcendentals=0)
SHORT = pl.CostEstimate(flops=1, bytes_accessed=1, transcendentals=0)


def move(value, axis, target):
    count = lax.axis_size(axis)
    return lax.ppermute(value, axis, [(s, target(s) % count) for s in range(count)])


def outward(w):
    return w + 2 if w % 2 == 0 else w - 2


def natural(low, high):
    odd = lax.rem(lax.axis_index("wide"), 2)
    return jnp.where(odd == 1, low, CL - 1 - high)


def multiply(left, right):
    product = lax.dot_general(left, right, (((1,), (1,)), ((), ())), preferred_element_type=jnp.float32)
    return product.astype(jnp.bfloat16)


def add_pieces(marks, pieces, left, dense):
    for piece, mark in zip(pieces, marks):
        count = piece.shape[0] // B
        for at in range(0, count, PAIR):
            low, high = mark + at, mark + at + PAIR - 1
            c0, c1 = max(0, low - REACH), min(CL - 1, high + REACH)
            offset, start, rows = natural(low, high), natural(c0, c1), (c1 - c0 + 1) * B
            row = pl.multiple_of((offset - natural(mark, mark + count - 1)) * B, PAIR * B)
            product = multiply(
                left[pl.ds(pl.multiple_of(start * B, B), rows), :], piece[pl.ds(row, PAIR * B), :]
            )
            for r in range(c1 - c0 + 1):
                for h in range(PAIR):
                    dense[start + r, offset + REACH + h] = product[r * B : (r + 1) * B, h * B : (h + 1) * B]


def pieces_kernel(marks, left, *refs):
    add_pieces(marks, refs[: len(marks)], left, refs[-1])


def pieces_blocks(left, pieces, cost, dense=None):
    held = [] if dense is None else [dense]
    return pl.pallas_call(
        functools.partial(pieces_kernel, list(pieces)),
        out_shape=jax.ShapeDtypeStruct((CL, CL + 2 * REACH, B, B), jnp.bfloat16),
        in_specs=[VMEM] * (1 + len(pieces) + len(held)),
        out_specs=VMEM,
        input_output_aliases={1 + len(pieces): 0} if held else {},
        compiler_params=pltpu.CompilerParams(vmem_limit_bytes=LIMIT),
        cost_estimate=cost,
        name="pieces_blocks",
    )(left, *pieces.values(), *held)


def ends_kernel(weight, near, far, out):
    odd = lax.rem(lax.axis_index("wide"), 2) == 1
    left = (near[...].astype(jnp.float32) * weight[...]).astype(jnp.bfloat16)
    product = multiply(left, far[...])
    for at, (c, m) in enumerate(((-1, 6), (-1, 7), (-2, 6))):
        here, there = ((c + 2) * B, (m - 6) * B), ((-1 - c) * B, (7 - m) * B)
        one, two = [product[row : row + B, column : column + B] for row, column in (here, there)]
        out[at] = jnp.where(odd, one, two)


def end_blocks(weight, near, far):
    return pl.pallas_call(
        ends_kernel,
        out_shape=jax.ShapeDtypeStruct((3, B, B), jnp.bfloat16),
        in_specs=[VMEM] * 3,
        out_specs=VMEM,
        compiler_params=pltpu.CompilerParams(vmem_limit_bytes=LIMIT),
        cost_estimate=SHORT,
        name="end_blocks",
    )(weight[None, :], near, far)


def choose_kernel(share, marks, chunk, ends, places, left, from_partner, after, *refs):
    dense = refs[len(marks) + 1]
    outs = refs[len(marks) + 2 :]
    add_pieces(marks, refs[: len(marks)], left, dense)
    if ends:
        for at, (c, m) in enumerate(((0, -7), (0, -8), (1, -7))):
            dense[natural(c, c), natural(m, m) + REACH] = from_partner[at]
    first, last = chunk
    start = natural(first, last)
    me = lax.axis_index("narrow")
    for out, mask in zip(outs, (3, 1, 2, 0)):
        slot0 = (me ^ mask) * share
        for c in range(last - first + 1):
            for s in range(share):
                out[c, s] = dense[start + c, places[start + c, slot0 + s]]


def choose_blocks(share, chunk, ends, places, left, from_partner, after, pieces, dense):
    shapes = [jax.ShapeDtypeStruct(dense.shape, dense.dtype)]
    shapes += [jax.ShapeDtypeStruct((chunk[1] - chunk[0] + 1, share, B, B), jnp.bfloat16)] * 4
    return pl.pallas_call(
        functools.partial(choose_kernel, share, list(pieces), chunk, ends),
        out_shape=shapes,
        in_specs=[SMEM] + [VMEM] * (4 + len(pieces)),
        out_specs=[VMEM] * len(shapes),
        input_output_aliases={4 + len(pieces): 0},
        compiler_params=pltpu.CompilerParams(vmem_limit_bytes=LIMIT),
        cost_estimate=SHORT,
        name="choose_blocks",
    )(places, left, from_partner, after, *pieces.values(), dense)


def add_kernel(x, y, out):
    out[...] = (x[...].astype(jnp.float32) + y[...].astype(jnp.float32)).astype(jnp.bfloat16)


def add(x, y):
    return pl.pallas_call(
        add_kernel,
        out_shape=jax.ShapeDtypeStruct(x.shape, x.dtype),
        in_specs=[VMEM] * 2,
        out_specs=VMEM,
        compiler_params=pltpu.CompilerParams(vmem_limit_bytes=LIMIT),
        cost_estimate=SHORT,
        name="add",
    )(x, y)


def total_kernel(near, got_near, got, out):
    total = near[...].astype(jnp.float32) + got_near[...].astype(jnp.float32) + got[...].astype(jnp.float32)
    out[...] = total.astype(jnp.bfloat16)


def total(near, got_near, got):
    return pl.pallas_call(
        total_kernel,
        out_shape=jax.ShapeDtypeStruct(near.shape, near.dtype),
        in_specs=[VMEM] * 3,
        out_specs=VMEM,
        compiler_params=pltpu.CompilerParams(vmem_limit_bytes=LIMIT),
        cost_estimate=LONG,
        name="total",
    )(near, got_near, got)


def finish_kernel(chunks, early, near, got_near, got, out):
    start, later = [natural(first, last) for first, last in chunks]
    for r in range(early.shape[0]):
        out[start + r] = early[r]
    for r in range(near.shape[0]):
        total = near[r].astype(jnp.float32) + got_near[r].astype(jnp.float32) + got[r].astype(jnp.float32)
        out[later + r] = total.astype(jnp.bfloat16)


def finish(chunks, early, near, got_near, got):
    return pl.pallas_call(
        functools.partial(finish_kernel, chunks),
        out_shape=jax.ShapeDtypeStruct((CL,) + near.shape[1:], near.dtype),
        in_specs=[VMEM] * 4,
        out_specs=VMEM,
        compiler_params=pltpu.CompilerParams(vmem_limit_bytes=LIMIT),
        cost_estimate=SHORT,
        name="finish",
    )(early, near, got_near, got)


def take_kernel(which, slab, after, out, done):
    odd = lax.rem(lax.axis_index("wide"), 2)
    row = {"end": odd * 2, "middle": 1, "near": (1 - odd) * 2}[which] * PAIR * B
    copy = pltpu.make_async_copy(slab.at[pl.ds(pl.multiple_of(row, PAIR * B), PAIR * B), :], out, done)
    copy.start()
    copy.wait()


def take(slab, which, after):
    return pl.pallas_call(
        functools.partial(take_kernel, which),
        out_shape=jax.ShapeDtypeStruct((PAIR * B, slab.shape[1]), slab.dtype),
        in_specs=[pl.BlockSpec(memory_space=pltpu.HBM), VMEM],
        out_specs=VMEM,
        scratch_shapes=[pltpu.SemaphoreType.DMA],
        compiler_params=pltpu.CompilerParams(vmem_limit_bytes=LIMIT),
        cost_estimate=SHORT,
        name=f"take_{which}",
    )(slab, after)


def per_device(slab, occupation, column_band, pattern):
    clusters = CL * lax.axis_size("wide")
    share = pattern.shape[1] // lax.axis_size("narrow")
    odd = lax.axis_index("wide") % 2
    rows = PAIR * B
    partner = lambda w: w ^ 1

    places = jnp.mod(pattern - (lax.axis_index("wide") * CL - REACH), clusters)
    picks = column_band[:, None] == jnp.arange(occupation.shape[0], dtype=jnp.int32)[None, :]
    weight = jnp.sum(jnp.where(picks, occupation[None, :], jnp.float32(0.0)), axis=1)
    scaled = (slab.astype(jnp.float32) * weight[None, :]).astype(jnp.bfloat16)

    early = {0: slab}
    middle_rows = take(slab, "middle", jnp.zeros((8, 128), jnp.float32))
    end_rows = take(slab, "end", jnp.zeros((8, 128), jnp.float32))
    later_rows = take(slab, "near", jnp.zeros((8, 128), jnp.float32))
    near_rows = take(slab, "near", later_rows)
    early[-4] = move(middle_rows, "wide", partner)
    early[-6] = move(end_rows, "wide", partner)
    early[12] = move(later_rows, "wide", outward)
    near = move(near_rows, "wide", partner)
    early[8] = move(early[-4], "wide", outward)
    early[6] = move(early[-6], "wide", outward)
    early[-2] = near
    late = {10: move(near, "wide", outward)}
    from_partner = move(end_blocks(weight, near, early[6]), "wide", partner)

    dense = pieces_blocks(scaled, early, LONG)
    chunks = ((0, 1), (2, 5))

    parts = []
    after = scaled
    for pieces, chunk, ends in (({}, chunks[0], True), (late, chunks[1], False)):
        dense, send_far, send_near, keep_far, keep_near = choose_blocks(
            share, chunk, ends, places, scaled, from_partner, after, pieces, dense
        )
        got_far = move(send_far, "narrow", lambda n: n ^ 1)
        got_near = move(send_near, "narrow", lambda n: n ^ 1)
        parts.append((keep_near, got_near, move(add(keep_far, got_far), "narrow", lambda n: n ^ 2)))
        after = got_far
    return finish(chunks, total(*parts[0]), *parts[1])


def solution(mesh):
    placed = (P("wide", "narrow"), P(), P("narrow"), P("wide", None))
    return jax.shard_map(
        per_device,
        mesh=mesh,
        in_specs=placed,
        out_specs=P("wide", "narrow", None, None),
        check_vma=False,
    )
```

```python
import functools

import jax
import jax.numpy as jnp
from jax import lax
from jax.experimental import pallas as pl
from jax.experimental.pallas import tpu as pltpu
from jax.sharding import PartitionSpec as P

B = 128
REACH = 8
CL = 6
PAIR = 2
ENDS = [(0, -7), (0, -8), (1, -7)]
LATE = [(2, 10), (3, 10), (3, 11), (4, 10), (4, 11), (5, 10), (5, 11)]
LATE_PLACES = (10, 11)
MASKS = (3, 1, 2, 0)
VMEM = pl.BlockSpec(memory_space=pltpu.VMEM)
SMEM = pl.BlockSpec(memory_space=pltpu.SMEM)
LIMIT = 40 * 1024 * 1024
LONG = pl.CostEstimate(flops=20 * 10**9, bytes_accessed=1, transcendentals=0)
SHORT = pl.CostEstimate(flops=1, bytes_accessed=1, transcendentals=0)


def move(value, axis, target):
    count = lax.axis_size(axis)
    return lax.ppermute(value, axis, [(s, target(s) % count) for s in range(count)])


def outward(w):
    return w + 2 if w % 2 == 0 else w - 2


def natural(low, high):
    odd = lax.rem(lax.axis_index("wide"), 2)
    return jnp.where(odd == 1, low, CL - 1 - high)


def multiply(left, right):
    product = lax.dot_general(left, right, (((1,), (1,)), ((), ())), preferred_element_type=jnp.float32)
    return product.astype(jnp.bfloat16)


def add_pieces(marks, pieces, left, dense):
    for piece, mark in zip(pieces, marks):
        count = piece.shape[0] // B
        for at in range(0, count, PAIR):
            low, high = mark + at, mark + at + PAIR - 1
            c0, c1 = max(0, low - REACH), min(CL - 1, high + REACH)
            offset, start, rows = natural(low, high), natural(c0, c1), (c1 - c0 + 1) * B
            row = pl.multiple_of((offset - natural(mark, mark + count - 1)) * B, PAIR * B)
            product = multiply(
                left[pl.ds(pl.multiple_of(start * B, B), rows), :], piece[pl.ds(row, PAIR * B), :]
            )
            for r in range(c1 - c0 + 1):
                for h in range(PAIR):
                    dense[start + r, offset + REACH + h] = product[r * B : (r + 1) * B, h * B : (h + 1) * B]


def choose(share, chunk, places, dense, outs):
    first, last = chunk
    start = natural(first, last)
    me = lax.axis_index("narrow")
    for out, mask in zip(outs, MASKS):
        slot0 = (me ^ mask) * share
        for r in range(last - first + 1):
            for s in range(share):
                out[r, s] = dense[start + r, places[start + r, slot0 + s]]


def put(spot, row, block, outs):
    for out, mask in zip(outs, MASKS):

        @pl.when(spot[0] == mask)
        def _(out=out):
            out[row, spot[1]] = block()


def chosen_shapes(chunk, share):
    return [jax.ShapeDtypeStruct((chunk[1] - chunk[0] + 1, share, B, B), jnp.bfloat16)] * 4


def early_kernel(share, marks, chunk, places, left, *refs):
    dense, spots = refs[len(marks) : len(marks) + 2]
    add_pieces(marks, refs[: len(marks)], left, dense)
    choose(share, chunk, places, dense, refs[len(marks) + 2 :])
    me = lax.axis_index("narrow")
    for at, (c, m) in enumerate(ENDS + LATE):
        row, place = natural(c, c), natural(m, m) + REACH
        slot = jnp.int32(-1)
        for s in range(places.shape[1]):
            slot = jnp.where(places[row, s] == place, s, slot)
        spots[at, 0] = jnp.where(slot < 0, -1, lax.div(slot, share) ^ me)
        spots[at, 1] = lax.rem(slot, share)


def early_blocks(share, chunk, places, left, pieces):
    shapes = [
        jax.ShapeDtypeStruct((CL, CL + 2 * REACH, B, B), jnp.bfloat16),
        jax.ShapeDtypeStruct((len(ENDS + LATE), 2), jnp.int32),
    ] + chosen_shapes(chunk, share)
    return pl.pallas_call(
        functools.partial(early_kernel, share, list(pieces), chunk),
        out_shape=shapes,
        in_specs=[SMEM] + [VMEM] * (1 + len(pieces)),
        out_specs=[VMEM, SMEM] + [VMEM] * 4,
        compiler_params=pltpu.CompilerParams(vmem_limit_bytes=LIMIT),
        cost_estimate=LONG,
        name="early_blocks",
    )(places, left, *pieces.values())


def ends_put_kernel(chunk, spots, from_partner, *refs):
    outs = refs[4:]
    for at, (c, m) in enumerate(ENDS):
        row = natural(c, c) - natural(*chunk)
        put([spots[at, k] for k in range(2)], row, lambda at=at: from_partner[at], outs)


def ends_put(chunk, spots, from_partner, chosen):
    return pl.pallas_call(
        functools.partial(ends_put_kernel, chunk),
        out_shape=[jax.ShapeDtypeStruct(x.shape, x.dtype) for x in chosen],
        in_specs=[SMEM] + [VMEM] * 5,
        out_specs=[VMEM] * 4,
        input_output_aliases={2 + k: k for k in range(4)},
        compiler_params=pltpu.CompilerParams(vmem_limit_bytes=LIMIT),
        cost_estimate=SHORT,
        name="ends_put",
    )(spots, from_partner, *chosen)


def choose_kernel(share, chunk, places, dense, after, *outs):
    choose(share, chunk, places, dense, outs)


def choose_blocks(share, chunk, places, dense, after):
    shapes = chosen_shapes(chunk, share)
    return pl.pallas_call(
        functools.partial(choose_kernel, share, chunk),
        out_shape=shapes,
        in_specs=[SMEM] + [VMEM] * 2,
        out_specs=[VMEM] * 4,
        compiler_params=pltpu.CompilerParams(vmem_limit_bytes=LIMIT),
        cost_estimate=SHORT,
        name="choose_blocks",
    )(places, dense, after)


def late_kernel(chunk, spots, left, piece, after, *refs):
    outs, late = refs[4:8], refs[8]
    first, last = chunk
    start, rows = natural(first, last), (last - first + 1) * B
    product = multiply(left[pl.ds(pl.multiple_of(start * B, B), rows), :], piece[...])
    for r in range(last - first + 1):
        for h in range(PAIR):
            late[r, h] = product[r * B : (r + 1) * B, h * B : (h + 1) * B]
    for at, (c, m) in enumerate(LATE):
        row, column = natural(c, c) - start, natural(m, m) - natural(*LATE_PLACES)
        put(
            [spots[len(ENDS) + at, k] for k in range(2)],
            row,
            lambda row=row, column=column: late[row, column],
            outs,
        )


def late_put(chunk, spots, left, piece, after, chosen):
    return pl.pallas_call(
        functools.partial(late_kernel, chunk),
        out_shape=[jax.ShapeDtypeStruct(x.shape, x.dtype) for x in chosen],
        in_specs=[SMEM] + [VMEM] * 7,
        out_specs=[VMEM] * 4,
        scratch_shapes=[pltpu.VMEM((chunk[1] - chunk[0] + 1, PAIR, B, B), jnp.bfloat16)],
        input_output_aliases={4 + k: k for k in range(4)},
        compiler_params=pltpu.CompilerParams(vmem_limit_bytes=LIMIT),
        cost_estimate=SHORT,
        name="late_put",
    )(spots, left, piece, after, *chosen)


def ends_kernel(weight, near, far, out):
    odd = lax.rem(lax.axis_index("wide"), 2) == 1
    left = (near[...].astype(jnp.float32) * weight[...]).astype(jnp.bfloat16)
    product = multiply(left, far[...])
    for at, (c, m) in enumerate(((-1, 6), (-1, 7), (-2, 6))):
        here, there = ((c + 2) * B, (m - 6) * B), ((-1 - c) * B, (7 - m) * B)
        one, two = [product[row : row + B, column : column + B] for row, column in (here, there)]
        out[at] = jnp.where(odd, one, two)


def end_blocks(weight, near, far):
    return pl.pallas_call(
        ends_kernel,
        out_shape=jax.ShapeDtypeStruct((3, B, B), jnp.bfloat16),
        in_specs=[VMEM] * 3,
        out_specs=VMEM,
        compiler_params=pltpu.CompilerParams(vmem_limit_bytes=LIMIT),
        cost_estimate=SHORT,
        name="end_blocks",
    )(weight[None, :], near, far)


def add_kernel(x, y, out):
    out[...] = (x[...].astype(jnp.float32) + y[...].astype(jnp.float32)).astype(jnp.bfloat16)


def add(x, y):
    return pl.pallas_call(
        add_kernel,
        out_shape=jax.ShapeDtypeStruct(x.shape, x.dtype),
        in_specs=[VMEM] * 2,
        out_specs=VMEM,
        compiler_params=pltpu.CompilerParams(vmem_limit_bytes=LIMIT),
        cost_estimate=SHORT,
        name="add",
    )(x, y)


def total_kernel(near, got_near, got, out):
    total = near[...].astype(jnp.float32) + got_near[...].astype(jnp.float32) + got[...].astype(jnp.float32)
    out[...] = total.astype(jnp.bfloat16)


def total(near, got_near, got):
    return pl.pallas_call(
        total_kernel,
        out_shape=jax.ShapeDtypeStruct(near.shape, near.dtype),
        in_specs=[VMEM] * 3,
        out_specs=VMEM,
        compiler_params=pltpu.CompilerParams(vmem_limit_bytes=LIMIT),
        cost_estimate=LONG,
        name="total",
    )(near, got_near, got)


def finish_kernel(chunks, early, near, got_near, got, out, rows, done):
    start, later = [natural(first, last) for first, last in chunks]
    copies = []
    for r in range(early.shape[0]):
        copies.append(pltpu.make_async_copy(early.at[r], out.at[start + r], done.at[r]))
        copies[-1].start()
    for r in range(near.shape[0]):
        total = near[r].astype(jnp.float32) + got_near[r].astype(jnp.float32) + got[r].astype(jnp.float32)
        rows[r] = total.astype(jnp.bfloat16)
        copies.append(pltpu.make_async_copy(rows.at[r], out.at[later + r], done.at[early.shape[0] + r]))
        copies[-1].start()
    for copy in copies:
        copy.wait()


def finish(chunks, early, near, got_near, got):
    return pl.pallas_call(
        functools.partial(finish_kernel, chunks),
        out_shape=jax.ShapeDtypeStruct((CL,) + near.shape[1:], near.dtype),
        in_specs=[VMEM] * 4,
        out_specs=pl.BlockSpec(memory_space=pl.ANY),
        scratch_shapes=[pltpu.VMEM(near.shape, near.dtype), pltpu.SemaphoreType.DMA((CL,))],
        compiler_params=pltpu.CompilerParams(vmem_limit_bytes=LIMIT),
        cost_estimate=SHORT,
        name="finish",
    )(early, near, got_near, got)


def take_kernel(which, slab, after, out, done):
    odd = lax.rem(lax.axis_index("wide"), 2)
    row = {"end": odd * 2, "middle": 1, "near": (1 - odd) * 2}[which] * PAIR * B
    copy = pltpu.make_async_copy(slab.at[pl.ds(pl.multiple_of(row, PAIR * B), PAIR * B), :], out, done)
    copy.start()
    copy.wait()


def take(slab, which, after):
    return pl.pallas_call(
        functools.partial(take_kernel, which),
        out_shape=jax.ShapeDtypeStruct((PAIR * B, slab.shape[1]), slab.dtype),
        in_specs=[pl.BlockSpec(memory_space=pltpu.HBM), VMEM],
        out_specs=VMEM,
        scratch_shapes=[pltpu.SemaphoreType.DMA],
        compiler_params=pltpu.CompilerParams(vmem_limit_bytes=LIMIT),
        cost_estimate=SHORT,
        name=f"take_{which}",
    )(slab, after)


def per_device(slab, occupation, column_band, pattern):
    clusters = CL * lax.axis_size("wide")
    share = pattern.shape[1] // lax.axis_size("narrow")
    odd = lax.axis_index("wide") % 2
    rows = PAIR * B
    partner = lambda w: w ^ 1

    places = jnp.mod(pattern - (lax.axis_index("wide") * CL - REACH), clusters)
    picks = column_band[:, None] == jnp.arange(occupation.shape[0], dtype=jnp.int32)[None, :]
    weight = jnp.sum(jnp.where(picks, occupation[None, :], jnp.float32(0.0)), axis=1)
    scaled = (slab.astype(jnp.float32) * weight[None, :]).astype(jnp.bfloat16)

    early = {0: slab}
    end_rows = take(slab, "end", jnp.zeros((8, 128), jnp.float32))
    later_rows = take(slab, "near", jnp.zeros((8, 128), jnp.float32))
    middle_rows = take(slab, "middle", jnp.zeros((8, 128), jnp.float32))
    near_rows = take(slab, "near", later_rows)
    early[-6] = move(end_rows, "wide", partner)
    early[12] = move(later_rows, "wide", outward)
    early[-4] = move(middle_rows, "wide", partner)
    near = move(near_rows, "wide", partner)
    early[6] = move(early[-6], "wide", outward)
    early[8] = move(early[-4], "wide", outward)
    early[-2] = near
    late = {10: move(near, "wide", outward)}
    from_partner = move(end_blocks(weight, near, early[6]), "wide", partner)

    chunks = ((0, 1), (2, 5))

    def swapped(chosen):
        send_far, send_near, keep_far, keep_near = chosen
        got_far = move(send_far, "narrow", lambda n: n ^ 1)
        got_near = move(send_near, "narrow", lambda n: n ^ 1)
        return got_far, (keep_near, got_near, move(add(keep_far, got_far), "narrow", lambda n: n ^ 2))

    dense, spots, *chosen = early_blocks(share, chunks[0], places, scaled, early)
    chosen = ends_put(chunks[0], spots, from_partner, chosen)
    after, first_parts = swapped(chosen)
    chosen = choose_blocks(share, chunks[1], places, dense, chosen[2])
    chosen = late_put(chunks[1], spots, scaled, late[LATE_PLACES[0]], after, chosen)
    _, parts = swapped(chosen)
    return finish(chunks, total(*first_parts), *parts)


def solution(mesh):
    placed = (P("wide", "narrow"), P(), P("narrow"), P("wide", None))
    return jax.shard_map(
        per_device,
        mesh=mesh,
        in_specs=placed,
        out_specs=P("wide", "narrow", None, None),
        check_vma=False,
    )
```

```python
import functools

import jax
import jax.numpy as jnp
from jax import lax
from jax.experimental import pallas as pl
from jax.experimental.pallas import tpu as pltpu
from jax.sharding import PartitionSpec as P

B = 128
REACH = 8
CL = 6
PAIR = 2
VMEM = pl.BlockSpec(memory_space=pltpu.VMEM)
SMEM = pl.BlockSpec(memory_space=pltpu.SMEM)
LIMIT = 40 * 1024 * 1024
LONG = pl.CostEstimate(flops=20 * 10**9, bytes_accessed=1, transcendentals=0)
SHORT = pl.CostEstimate(flops=1, bytes_accessed=1, transcendentals=0)


def move(value, axis, target):
    count = lax.axis_size(axis)
    return lax.ppermute(value, axis, [(s, target(s) % count) for s in range(count)])


def outward(w):
    return w + 2 if w % 2 == 0 else w - 2


def natural(low, high):
    odd = lax.rem(lax.axis_index("wide"), 2)
    return jnp.where(odd == 1, low, CL - 1 - high)


def multiply(left, right):
    product = lax.dot_general(left, right, (((1,), (1,)), ((), ())), preferred_element_type=jnp.float32)
    return product.astype(jnp.bfloat16)


def add_pieces(marks, pieces, left, dense):
    for piece, mark in zip(pieces, marks):
        count = piece.shape[0] // B
        width = min(count, PAIR)
        for at in range(0, count, width):
            low, high = mark + at, mark + at + width - 1
            c0, c1 = max(0, low - REACH), min(CL - 1, high + REACH)
            offset, start, rows = natural(low, high), natural(c0, c1), (c1 - c0 + 1) * B
            row = pl.multiple_of((offset - natural(mark, mark + count - 1)) * B, width * B)
            product = multiply(
                left[pl.ds(pl.multiple_of(start * B, B), rows), :], piece[pl.ds(row, width * B), :]
            )
            for r in range(c1 - c0 + 1):
                for h in range(width):
                    dense[start + r, offset + REACH + h] = product[r * B : (r + 1) * B, h * B : (h + 1) * B]


def pieces_kernel(marks, left, *refs):
    add_pieces(marks, refs[: len(marks)], left, refs[-1])


def pieces_blocks(left, pieces, cost, dense=None):
    held = [] if dense is None else [dense]
    return pl.pallas_call(
        functools.partial(pieces_kernel, list(pieces)),
        out_shape=jax.ShapeDtypeStruct((CL, CL + 2 * REACH, B, B), jnp.bfloat16),
        in_specs=[VMEM] * (1 + len(pieces) + len(held)),
        out_specs=VMEM,
        input_output_aliases={1 + len(pieces): 0} if held else {},
        compiler_params=pltpu.CompilerParams(vmem_limit_bytes=LIMIT),
        cost_estimate=cost,
        name="pieces_blocks",
    )(left, *pieces.values(), *held)


def ends_kernel(weight, near0, near1, far, out):
    odd = lax.rem(lax.axis_index("wide"), 2) == 1
    for near, spots in ((near0, ((0, 0), (1, 1))), (near1, ((2, 0),))):
        left = (near[...].astype(jnp.float32) * weight[...]).astype(jnp.bfloat16)
        product = multiply(left, far[...])
        low, high = product[:, :B], product[:, B:]
        for at, m in spots:
            out[at] = jnp.where(odd, high if m else low, low if m else high)


def end_blocks(weight, near0, near1, far):
    return pl.pallas_call(
        ends_kernel,
        out_shape=jax.ShapeDtypeStruct((3, B, B), jnp.bfloat16),
        in_specs=[VMEM] * 4,
        out_specs=VMEM,
        compiler_params=pltpu.CompilerParams(vmem_limit_bytes=LIMIT),
        cost_estimate=SHORT,
        name="end_blocks",
    )(weight[None, :], near0, near1, far)


def choose_kernel(share, marks, held, chunk, parted, places, left, from_partner, *refs):
    refs = refs[held:]
    dense = refs[len(marks) + 1]
    outs = refs[len(marks) + 2 :]
    add_pieces(marks, refs[: len(marks)], left, dense)
    first, last = chunk
    if first == 0:
        for at, (c, m) in enumerate(((0, -7), (0, -8), (1, -7))):
            dense[natural(c, c), natural(m, m) + REACH] = from_partner[at]
    start = natural(first, last)
    me = lax.axis_index("narrow")
    parts = last - first + 1 if parted else 1
    rows = [outs[:parts]] + [[out] for out in outs[parts:]]
    for arrays, mask in zip(rows, (3, 1, 2, 0)):
        slot0 = (me ^ mask) * share
        for r in range(last - first + 1):
            for s in range(share):
                block = dense[start + r, places[start + r, slot0 + s]]
                if len(arrays) > 1:
                    arrays[r][0, s] = block
                else:
                    arrays[0][r, s] = block


def choose_blocks(share, chunk, parted, places, left, from_partner, after, pieces, dense):
    count = chunk[1] - chunk[0] + 1
    sizes = ([1] * count if parted else [count]) + [count] * 3
    shapes = [jax.ShapeDtypeStruct(dense.shape, dense.dtype)]
    shapes += [jax.ShapeDtypeStruct((size, share, B, B), jnp.bfloat16) for size in sizes]
    dense, *chosen = pl.pallas_call(
        functools.partial(choose_kernel, share, list(pieces), len(after), chunk, parted),
        out_shape=shapes,
        in_specs=[SMEM] + [VMEM] * (3 + len(after) + len(pieces)),
        out_specs=[VMEM] * len(shapes),
        input_output_aliases={3 + len(after) + len(pieces): 0},
        compiler_params=pltpu.CompilerParams(vmem_limit_bytes=LIMIT),
        cost_estimate=SHORT,
        name="choose_blocks",
    )(places, left, from_partner, *after, *pieces.values(), dense)
    return dense, chosen[:-3], *chosen[-3:]


def add_kernel(x, *refs):
    out, at = refs[-1], 0
    for y in refs[:-1]:
        rows = pl.ds(at, y.shape[0])
        out[rows] = (x[rows].astype(jnp.float32) + y[...].astype(jnp.float32)).astype(jnp.bfloat16)
        at += y.shape[0]


def add(x, parts):
    return pl.pallas_call(
        add_kernel,
        out_shape=jax.ShapeDtypeStruct(x.shape, x.dtype),
        in_specs=[VMEM] * (1 + len(parts)),
        out_specs=VMEM,
        compiler_params=pltpu.CompilerParams(vmem_limit_bytes=LIMIT),
        cost_estimate=SHORT,
        name="add",
    )(x, *parts)


def total_kernel(near, got_near, got, out):
    total = near[...].astype(jnp.float32) + got_near[...].astype(jnp.float32) + got[...].astype(jnp.float32)
    out[...] = total.astype(jnp.bfloat16)


def total(near, got_near, got):
    return pl.pallas_call(
        total_kernel,
        out_shape=jax.ShapeDtypeStruct(near.shape, near.dtype),
        in_specs=[VMEM] * 3,
        out_specs=VMEM,
        compiler_params=pltpu.CompilerParams(vmem_limit_bytes=LIMIT),
        cost_estimate=LONG,
        name="total",
    )(near, got_near, got)


def finish_kernel(chunks, early, near, got_near, got, out, rows, done):
    start, later = [natural(first, last) for first, last in chunks]
    copies = []
    for r in range(early.shape[0]):
        copies.append(pltpu.make_async_copy(early.at[r], out.at[start + r], done.at[r]))
        copies[-1].start()
    for r in range(near.shape[0]):
        total = near[r].astype(jnp.float32) + got_near[r].astype(jnp.float32) + got[r].astype(jnp.float32)
        rows[r] = total.astype(jnp.bfloat16)
        copies.append(pltpu.make_async_copy(rows.at[r], out.at[later + r], done.at[early.shape[0] + r]))
        copies[-1].start()
    for copy in copies:
        copy.wait()


def finish(chunks, early, near, got_near, got):
    return pl.pallas_call(
        functools.partial(finish_kernel, chunks),
        out_shape=jax.ShapeDtypeStruct((CL,) + near.shape[1:], near.dtype),
        in_specs=[VMEM] * 4,
        out_specs=pl.BlockSpec(memory_space=pl.ANY),
        scratch_shapes=[pltpu.VMEM(near.shape, near.dtype), pltpu.SemaphoreType.DMA((CL,))],
        compiler_params=pltpu.CompilerParams(vmem_limit_bytes=LIMIT),
        cost_estimate=SHORT,
        name="finish",
    )(early, near, got_near, got)


def take_kernel(place, slab, after, out, done):
    count = out.shape[0] // B
    row = pl.multiple_of(natural(place, place + count - 1) * B, B)
    copy = pltpu.make_async_copy(slab.at[pl.ds(row, out.shape[0]), :], out, done)
    copy.start()
    copy.wait()


def take(slab, place, count, after):
    return pl.pallas_call(
        functools.partial(take_kernel, place),
        out_shape=jax.ShapeDtypeStruct((count * B, slab.shape[1]), slab.dtype),
        in_specs=[pl.BlockSpec(memory_space=pl.ANY), VMEM],
        out_specs=VMEM,
        scratch_shapes=[pltpu.SemaphoreType.DMA],
        compiler_params=pltpu.CompilerParams(vmem_limit_bytes=LIMIT),
        cost_estimate=SHORT,
        name=f"take_{place}_{count}",
    )(slab, after)


def per_device(slab, occupation, column_band, pattern):
    clusters = CL * lax.axis_size("wide")
    share = pattern.shape[1] // lax.axis_size("narrow")
    odd = lax.axis_index("wide") % 2
    rows = PAIR * B
    partner = lambda w: w ^ 1

    places = jnp.mod(pattern - (lax.axis_index("wide") * CL - REACH), clusters)
    picks = column_band[:, None] == jnp.arange(occupation.shape[0], dtype=jnp.int32)[None, :]
    weight = jnp.sum(jnp.where(picks, occupation[None, :], jnp.float32(0.0)), axis=1)
    scaled = (slab.astype(jnp.float32) * weight[None, :]).astype(jnp.bfloat16)

    early = {0: slab}
    end_rows = take(slab, 4, 2, jnp.zeros((8, 128), jnp.float32))
    later_rows = take(slab, 0, 2, end_rows)
    middle_rows = take(slab, 2, 2, later_rows)
    next_rows = take(slab, 1, 1, middle_rows)
    near_rows = take(slab, 0, 1, next_rows)
    early[-6] = move(end_rows, "wide", partner)
    early[12] = move(later_rows, "wide", outward)
    early[-4] = move(middle_rows, "wide", partner)
    early[-2] = move(next_rows, "wide", partner)
    early[-1] = move(near_rows, "wide", partner)
    early[6] = move(early[-6], "wide", outward)
    early[8] = move(early[-4], "wide", outward)
    middle = {10: move(early[-2], "wide", outward)}
    late = {11: move(early[-1], "wide", outward)}
    from_partner = move(end_blocks(weight, early[-1], early[-2], early[6]), "wide", partner)

    dense = pieces_blocks(scaled, early, LONG)
    chunks = ((0, 2), (3, 5))

    parts = []
    after = []
    for pieces, chunk in ((middle, chunks[0]), (late, chunks[1])):
        dense, send_far, send_near, keep_far, keep_near = choose_blocks(
            share, chunk, chunk == chunks[0], places, scaled, from_partner, after, pieces, dense
        )
        got_far = [move(part, "narrow", lambda n: n ^ 1) for part in send_far]
        got_near = move(send_near, "narrow", lambda n: n ^ 1)
        parts.append((keep_near, got_near, move(add(keep_far, got_far), "narrow", lambda n: n ^ 2)))
        after = got_far
    return finish(chunks, total(*parts[0]), *parts[1])


def solution(mesh):
    placed = (P("wide", "narrow"), P(), P("narrow"), P("wide", None))
    return jax.shard_map(
        per_device,
        mesh=mesh,
        in_specs=placed,
        out_specs=P("wide", "narrow", None, None),
        check_vma=False,
    )
```

```python
import functools

import jax
import jax.numpy as jnp
from jax import lax
from jax.experimental import pallas as pl
from jax.experimental.pallas import tpu as pltpu
from jax.sharding import PartitionSpec as P

B = 128
REACH = 8
CL = 6
PAIR = 2
VMEM = pl.BlockSpec(memory_space=pltpu.VMEM)
SMEM = pl.BlockSpec(memory_space=pltpu.SMEM)
LIMIT = 40 * 1024 * 1024
WHOLE = 65280 * 1024
LONG = pl.CostEstimate(flops=20 * 10**9, bytes_accessed=1, transcendentals=0)
SHORT = pl.CostEstimate(flops=1, bytes_accessed=1, transcendentals=0)


def move(value, axis, target):
    count = lax.axis_size(axis)
    return lax.ppermute(value, axis, [(s, target(s) % count) for s in range(count)])


def outward(w):
    return w + 2 if w % 2 == 0 else w - 2


def natural(low, high):
    odd = lax.rem(lax.axis_index("wide"), 2)
    return jnp.where(odd == 1, low, CL - 1 - high)


def multiply(left, right):
    product = lax.dot_general(left, right, (((1,), (1,)), ((), ())), preferred_element_type=jnp.float32)
    return product.astype(jnp.bfloat16)


def add_pieces(marks, pieces, left, dense):
    for piece, mark in zip(pieces, marks):
        count = piece.shape[0] // B
        for at in range(0, count, PAIR):
            low, high = mark + at, mark + at + PAIR - 1
            c0, c1 = max(0, low - REACH), min(CL - 1, high + REACH)
            offset, start, rows = natural(low, high), natural(c0, c1), (c1 - c0 + 1) * B
            row = pl.multiple_of((offset - natural(mark, mark + count - 1)) * B, PAIR * B)
            product = multiply(
                left[pl.ds(pl.multiple_of(start * B, B), rows), :], piece[pl.ds(row, PAIR * B), :]
            )
            for r in range(c1 - c0 + 1):
                for h in range(PAIR):
                    dense[start + r, offset + REACH + h] = product[r * B : (r + 1) * B, h * B : (h + 1) * B]


def pieces_kernel(marks, left, *refs):
    add_pieces(marks, refs[: len(marks)], left, refs[-1])


def pieces_blocks(left, pieces, cost, dense=None):
    held = [] if dense is None else [dense]
    return pl.pallas_call(
        functools.partial(pieces_kernel, list(pieces)),
        out_shape=jax.ShapeDtypeStruct((CL, CL + 2 * REACH, B, B), jnp.bfloat16),
        in_specs=[VMEM] * (1 + len(pieces) + len(held)),
        out_specs=VMEM,
        input_output_aliases={1 + len(pieces): 0} if held else {},
        compiler_params=pltpu.CompilerParams(vmem_limit_bytes=LIMIT),
        cost_estimate=cost,
        name="pieces_blocks",
    )(left, *pieces.values(), *held)


def ends_kernel(weight, near, far, out):
    odd = lax.rem(lax.axis_index("wide"), 2) == 1
    left = (near[...].astype(jnp.float32) * weight[...]).astype(jnp.bfloat16)
    product = multiply(left, far[...])
    for at, (c, m) in enumerate(((-1, 6), (-1, 7), (-2, 6))):
        here, there = ((c + 2) * B, (m - 6) * B), ((-1 - c) * B, (7 - m) * B)
        one, two = [product[row : row + B, column : column + B] for row, column in (here, there)]
        out[at] = jnp.where(odd, one, two)


def end_blocks(weight, near, far):
    return pl.pallas_call(
        ends_kernel,
        out_shape=jax.ShapeDtypeStruct((3, B, B), jnp.bfloat16),
        in_specs=[VMEM] * 3,
        out_specs=VMEM,
        compiler_params=pltpu.CompilerParams(vmem_limit_bytes=LIMIT),
        cost_estimate=SHORT,
        name="end_blocks",
    )(weight[None, :], near, far)


def choose_kernel(share, marks, chunk, ends, places, left, from_partner, after, *refs):
    dense = refs[len(marks) + 1]
    outs = refs[len(marks) + 2 :]
    add_pieces(marks, refs[: len(marks)], left, dense)
    if ends:
        for at, (c, m) in enumerate(((0, -7), (0, -8), (1, -7))):
            dense[natural(c, c), natural(m, m) + REACH] = from_partner[at]
    first, last = chunk
    start = natural(first, last)
    me = lax.axis_index("narrow")
    for out, mask in zip(outs, (3, 1, 2, 0)):
        slot0 = (me ^ mask) * share
        for c in range(last - first + 1):
            for s in range(share):
                out[c, s] = dense[start + c, places[start + c, slot0 + s]]


def choose_blocks(share, chunk, ends, places, left, from_partner, after, pieces, dense):
    shapes = [jax.ShapeDtypeStruct(dense.shape, dense.dtype)]
    shapes += [jax.ShapeDtypeStruct((chunk[1] - chunk[0] + 1, share, B, B), jnp.bfloat16)] * 4
    return pl.pallas_call(
        functools.partial(choose_kernel, share, list(pieces), chunk, ends),
        out_shape=shapes,
        in_specs=[SMEM] + [VMEM] * (4 + len(pieces)),
        out_specs=[VMEM] * len(shapes),
        input_output_aliases={4 + len(pieces): 0},
        compiler_params=pltpu.CompilerParams(vmem_limit_bytes=LIMIT),
        cost_estimate=SHORT,
        name="choose_blocks",
    )(places, left, from_partner, after, *pieces.values(), dense)


def add_kernel(x, y, out):
    out[...] = (x[...].astype(jnp.float32) + y[...].astype(jnp.float32)).astype(jnp.bfloat16)


def add(x, y):
    return pl.pallas_call(
        add_kernel,
        out_shape=jax.ShapeDtypeStruct(x.shape, x.dtype),
        in_specs=[VMEM] * 2,
        out_specs=VMEM,
        compiler_params=pltpu.CompilerParams(vmem_limit_bytes=LIMIT),
        cost_estimate=SHORT,
        name="add",
    )(x, y)


def total_kernel(near, got_near, got, out):
    total = near[...].astype(jnp.float32) + got_near[...].astype(jnp.float32) + got[...].astype(jnp.float32)
    out[...] = total.astype(jnp.bfloat16)


def total(near, got_near, got):
    return pl.pallas_call(
        total_kernel,
        out_shape=jax.ShapeDtypeStruct(near.shape, near.dtype),
        in_specs=[VMEM] * 3,
        out_specs=VMEM,
        compiler_params=pltpu.CompilerParams(vmem_limit_bytes=LIMIT),
        cost_estimate=LONG,
        name="total",
    )(near, got_near, got)


def finish_kernel(chunks, early, near, got_near, got, out, rows, done):
    start, later = [natural(first, last) for first, last in chunks]
    copies = []
    for r in range(early.shape[0]):
        copies.append(pltpu.make_async_copy(early.at[r], out.at[start + r], done.at[r]))
        copies[-1].start()
    for r in range(near.shape[0]):
        total = near[r].astype(jnp.float32) + got_near[r].astype(jnp.float32) + got[r].astype(jnp.float32)
        rows[r] = total.astype(jnp.bfloat16)
        copies.append(pltpu.make_async_copy(rows.at[r], out.at[later + r], done.at[early.shape[0] + r]))
        copies[-1].start()
    for copy in copies:
        copy.wait()


def finish(chunks, early, near, got_near, got):
    return pl.pallas_call(
        functools.partial(finish_kernel, chunks),
        out_shape=jax.ShapeDtypeStruct((CL,) + near.shape[1:], near.dtype),
        in_specs=[VMEM] * 4,
        out_specs=pl.BlockSpec(memory_space=pl.ANY),
        scratch_shapes=[pltpu.VMEM(near.shape, near.dtype), pltpu.SemaphoreType.DMA((CL,))],
        compiler_params=pltpu.CompilerParams(vmem_limit_bytes=LIMIT),
        cost_estimate=SHORT,
        name="finish",
    )(early, near, got_near, got)


def take_kernel(which, slab, after, out, done):
    odd = lax.rem(lax.axis_index("wide"), 2)
    row = {"end": odd * 2, "middle": 1, "near": (1 - odd) * 2}[which] * PAIR * B
    copy = pltpu.make_async_copy(slab.at[pl.ds(pl.multiple_of(row, PAIR * B), PAIR * B), :], out, done)
    copy.start()
    copy.wait()


def first_take_kernel(slab, out, done):
    odd = lax.rem(lax.axis_index("wide"), 2)
    copy = pltpu.make_async_copy(slab.at[pl.ds(pl.multiple_of(odd * 2 * PAIR * B, PAIR * B), PAIR * B), :], out, done)
    copy.start()
    copy.wait()


def first_take(slab):
    hbm = pl.BlockSpec(memory_space=pl.ANY)
    return pl.pallas_call(
        first_take_kernel,
        out_shape=jax.ShapeDtypeStruct((PAIR * B, slab.shape[1]), slab.dtype),
        in_specs=[hbm],
        out_specs=hbm,
        scratch_shapes=[pltpu.SemaphoreType.DMA],
        compiler_params=pltpu.CompilerParams(vmem_limit_bytes=WHOLE),
        cost_estimate=SHORT,
        name="take_end",
    )(slab)


def take(slab, which, after):
    return pl.pallas_call(
        functools.partial(take_kernel, which),
        out_shape=jax.ShapeDtypeStruct((PAIR * B, slab.shape[1]), slab.dtype),
        in_specs=[pl.BlockSpec(memory_space=pltpu.HBM), VMEM],
        out_specs=VMEM,
        scratch_shapes=[pltpu.SemaphoreType.DMA],
        compiler_params=pltpu.CompilerParams(vmem_limit_bytes=LIMIT),
        cost_estimate=SHORT,
        name=f"take_{which}",
    )(slab, after)


def per_device(slab, occupation, column_band, pattern):
    clusters = CL * lax.axis_size("wide")
    share = pattern.shape[1] // lax.axis_size("narrow")
    odd = lax.axis_index("wide") % 2
    rows = PAIR * B
    partner = lambda w: w ^ 1

    places = jnp.mod(pattern - (lax.axis_index("wide") * CL - REACH), clusters)
    picks = column_band[:, None] == jnp.arange(occupation.shape[0], dtype=jnp.int32)[None, :]
    weight = jnp.sum(jnp.where(picks, occupation[None, :], jnp.float32(0.0)), axis=1)
    scaled = (slab.astype(jnp.float32) * weight[None, :]).astype(jnp.bfloat16)

    early = {0: slab}
    end_rows = first_take(slab)
    later_rows = take(slab, "near", jnp.zeros((8, 128), jnp.float32))
    middle_rows = take(slab, "middle", later_rows)
    near_rows = take(slab, "near", middle_rows)
    early[-6] = move(end_rows, "wide", partner)
    early[12] = move(later_rows, "wide", outward)
    early[-4] = move(middle_rows, "wide", partner)
    near = move(near_rows, "wide", partner)
    early[6] = move(early[-6], "wide", outward)
    early[8] = move(early[-4], "wide", outward)
    early[-2] = near
    late = {10: move(near, "wide", outward)}
    from_partner = move(end_blocks(weight, near, early[6]), "wide", partner)

    dense = pieces_blocks(scaled, early, LONG)
    chunks = ((0, 1), (2, 5))

    parts = []
    after = scaled
    for pieces, chunk, ends in (({}, chunks[0], True), (late, chunks[1], False)):
        dense, send_far, send_near, keep_far, keep_near = choose_blocks(
            share, chunk, ends, places, scaled, from_partner, after, pieces, dense
        )
        got_far = move(send_far, "narrow", lambda n: n ^ 1)
        got = move(add(keep_far, got_far), "narrow", lambda n: n ^ 2)
        got_near = move(send_near, "narrow", lambda n: n ^ 1)
        parts.append((keep_near, got_near, got))
        after = got_far
    return finish(chunks, total(*parts[0]), *parts[1])


def solution(mesh):
    placed = (P("wide", "narrow"), P(), P("narrow"), P("wide", None))
    return jax.shard_map(
        per_device,
        mesh=mesh,
        in_specs=placed,
        out_specs=P("wide", "narrow", None, None),
        check_vma=False,
    )
```

```python
import functools

import jax
import jax.numpy as jnp
from jax import lax
from jax.experimental import pallas as pl
from jax.experimental.pallas import tpu as pltpu
from jax.sharding import PartitionSpec as P

B = 128
REACH = 8
CL = 6
PAIR = 2
VMEM = pl.BlockSpec(memory_space=pltpu.VMEM)
SMEM = pl.BlockSpec(memory_space=pltpu.SMEM)
LIMIT = 40 * 1024 * 1024
LONG = pl.CostEstimate(flops=20 * 10**9, bytes_accessed=1, transcendentals=0)
SHORT = pl.CostEstimate(flops=1, bytes_accessed=1, transcendentals=0)


def move(value, axis, target):
    count = lax.axis_size(axis)
    return lax.ppermute(value, axis, [(s, target(s) % count) for s in range(count)])


def outward(w):
    return w + 2 if w % 2 == 0 else w - 2


def natural(low, high):
    odd = lax.rem(lax.axis_index("wide"), 2)
    return jnp.where(odd == 1, low, CL - 1 - high)


def multiply(left, right):
    product = lax.dot_general(left, right, (((1,), (1,)), ((), ())), preferred_element_type=jnp.float32)
    return product.astype(jnp.bfloat16)


def add_pieces(marks, pieces, left, dense):
    for piece, mark in zip(pieces, marks):
        count = piece.shape[0] // B
        for at in range(0, count, PAIR):
            low, high = mark + at, mark + at + PAIR - 1
            c0, c1 = max(0, low - REACH), min(CL - 1, high + REACH)
            offset, start, rows = natural(low, high), natural(c0, c1), (c1 - c0 + 1) * B
            row = pl.multiple_of((offset - natural(mark, mark + count - 1)) * B, PAIR * B)
            product = multiply(
                left[pl.ds(pl.multiple_of(start * B, B), rows), :], piece[pl.ds(row, PAIR * B), :]
            )
            for r in range(c1 - c0 + 1):
                for h in range(PAIR):
                    dense[start + r, offset + REACH + h] = product[r * B : (r + 1) * B, h * B : (h + 1) * B]


def pieces_kernel(marks, left, *refs):
    add_pieces(marks, refs[: len(marks)], left, refs[-1])


def pieces_blocks(left, pieces, cost, dense=None):
    held = [] if dense is None else [dense]
    return pl.pallas_call(
        functools.partial(pieces_kernel, list(pieces)),
        out_shape=jax.ShapeDtypeStruct((CL, CL + 2 * REACH, B, B), jnp.bfloat16),
        in_specs=[VMEM] * (1 + len(pieces) + len(held)),
        out_specs=VMEM,
        input_output_aliases={1 + len(pieces): 0} if held else {},
        compiler_params=pltpu.CompilerParams(vmem_limit_bytes=LIMIT),
        cost_estimate=cost,
        name="pieces_blocks",
    )(left, *pieces.values(), *held)


def ends_kernel(weight, near, far, out):
    odd = lax.rem(lax.axis_index("wide"), 2) == 1
    left = (near[...].astype(jnp.float32) * weight[...]).astype(jnp.bfloat16)
    product = multiply(left, far[...])
    for at, (c, m) in enumerate(((-1, 6), (-1, 7), (-2, 6))):
        here, there = ((c + 2) * B, (m - 6) * B), ((-1 - c) * B, (7 - m) * B)
        one, two = [product[row : row + B, column : column + B] for row, column in (here, there)]
        out[at] = jnp.where(odd, one, two)


def end_blocks(weight, near, far):
    return pl.pallas_call(
        ends_kernel,
        out_shape=jax.ShapeDtypeStruct((3, B, B), jnp.bfloat16),
        in_specs=[VMEM] * 3,
        out_specs=VMEM,
        compiler_params=pltpu.CompilerParams(vmem_limit_bytes=LIMIT),
        cost_estimate=SHORT,
        name="end_blocks",
    )(weight[None, :], near, far)


def choose_kernel(share, marks, chunk, ends, places, left, from_partner, after, *refs):
    dense = refs[len(marks) + 1]
    outs = refs[len(marks) + 2 :]
    add_pieces(marks, refs[: len(marks)], left, dense)
    if ends:
        for at, (c, m) in enumerate(((0, -7), (0, -8), (1, -7))):
            dense[natural(c, c), natural(m, m) + REACH] = from_partner[at]
    first, last = chunk
    start = natural(first, last)
    me = lax.axis_index("narrow")
    for out, mask in zip(outs, (3, 1, 2, 0)):
        slot0 = (me ^ mask) * share
        for c in range(last - first + 1):
            for s in range(share):
                out[c, s] = dense[start + c, places[start + c, slot0 + s]]


def choose_blocks(share, chunk, ends, places, left, from_partner, after, pieces, dense):
    shapes = [jax.ShapeDtypeStruct(dense.shape, dense.dtype)]
    shapes += [jax.ShapeDtypeStruct((chunk[1] - chunk[0] + 1, share, B, B), jnp.bfloat16)] * 4
    return pl.pallas_call(
        functools.partial(choose_kernel, share, list(pieces), chunk, ends),
        out_shape=shapes,
        in_specs=[SMEM] + [VMEM] * (4 + len(pieces)),
        out_specs=[VMEM] * len(shapes),
        input_output_aliases={4 + len(pieces): 0},
        compiler_params=pltpu.CompilerParams(vmem_limit_bytes=LIMIT),
        cost_estimate=SHORT,
        name="choose_blocks",
    )(places, left, from_partner, after, *pieces.values(), dense)


def add_kernel(x, y, after, out):
    out[...] = (x[...].astype(jnp.float32) + y[...].astype(jnp.float32)).astype(jnp.bfloat16)


def add(x, y, after):
    return pl.pallas_call(
        add_kernel,
        out_shape=jax.ShapeDtypeStruct(x.shape, x.dtype),
        in_specs=[VMEM] * 3,
        out_specs=VMEM,
        compiler_params=pltpu.CompilerParams(vmem_limit_bytes=LIMIT),
        cost_estimate=SHORT,
        name="add",
    )(x, y, after)


def total_kernel(near, got_near, got, out):
    total = near[...].astype(jnp.float32) + got_near[...].astype(jnp.float32) + got[...].astype(jnp.float32)
    out[...] = total.astype(jnp.bfloat16)


def total(near, got_near, got):
    return pl.pallas_call(
        total_kernel,
        out_shape=jax.ShapeDtypeStruct(near.shape, near.dtype),
        in_specs=[VMEM] * 3,
        out_specs=VMEM,
        compiler_params=pltpu.CompilerParams(vmem_limit_bytes=LIMIT),
        cost_estimate=LONG,
        name="total",
    )(near, got_near, got)


def finish_kernel(chunks, early, near, got_near, got, out, rows, done):
    start, later = [natural(first, last) for first, last in chunks]
    copies = []
    for r in range(early.shape[0]):
        copies.append(pltpu.make_async_copy(early.at[r], out.at[start + r], done.at[r]))
        copies[-1].start()
    for r in range(near.shape[0]):
        total = near[r].astype(jnp.float32) + got_near[r].astype(jnp.float32) + got[r].astype(jnp.float32)
        rows[r] = total.astype(jnp.bfloat16)
        copies.append(pltpu.make_async_copy(rows.at[r], out.at[later + r], done.at[early.shape[0] + r]))
        copies[-1].start()
    for copy in copies:
        copy.wait()


def finish(chunks, early, near, got_near, got):
    return pl.pallas_call(
        functools.partial(finish_kernel, chunks),
        out_shape=jax.ShapeDtypeStruct((CL,) + near.shape[1:], near.dtype),
        in_specs=[VMEM] * 4,
        out_specs=pl.BlockSpec(memory_space=pl.ANY),
        scratch_shapes=[pltpu.VMEM(near.shape, near.dtype), pltpu.SemaphoreType.DMA((CL,))],
        compiler_params=pltpu.CompilerParams(vmem_limit_bytes=LIMIT),
        cost_estimate=SHORT,
        name="finish",
    )(early, near, got_near, got)


def hold_kernel(rows, out):
    out[...] = rows[...]


def hold(rows):
    return pl.pallas_call(
        hold_kernel,
        out_shape=jax.ShapeDtypeStruct(rows.shape, rows.dtype),
        in_specs=[VMEM],
        out_specs=VMEM,
        compiler_params=pltpu.CompilerParams(vmem_limit_bytes=LIMIT),
        cost_estimate=LONG,
        name="hold",
    )(rows)


def take_kernel(which, slab, after, out, done):
    odd = lax.rem(lax.axis_index("wide"), 2)
    row = {"end": odd * 2, "middle": 1, "near": (1 - odd) * 2}[which] * PAIR * B
    copy = pltpu.make_async_copy(slab.at[pl.ds(pl.multiple_of(row, PAIR * B), PAIR * B), :], out, done)
    copy.start()
    copy.wait()


def take(slab, which, after):
    return pl.pallas_call(
        functools.partial(take_kernel, which),
        out_shape=jax.ShapeDtypeStruct((PAIR * B, slab.shape[1]), slab.dtype),
        in_specs=[pl.BlockSpec(memory_space=pltpu.HBM), VMEM],
        out_specs=VMEM,
        scratch_shapes=[pltpu.SemaphoreType.DMA],
        compiler_params=pltpu.CompilerParams(vmem_limit_bytes=LIMIT),
        cost_estimate=SHORT,
        name=f"take_{which}",
    )(slab, after)


def per_device(slab, occupation, column_band, pattern):
    clusters = CL * lax.axis_size("wide")
    share = pattern.shape[1] // lax.axis_size("narrow")
    odd = lax.axis_index("wide") % 2
    rows = PAIR * B
    partner = lambda w: w ^ 1

    places = jnp.mod(pattern - (lax.axis_index("wide") * CL - REACH), clusters)
    picks = column_band[:, None] == jnp.arange(occupation.shape[0], dtype=jnp.int32)[None, :]
    weight = jnp.sum(jnp.where(picks, occupation[None, :], jnp.float32(0.0)), axis=1)
    scaled = (slab.astype(jnp.float32) * weight[None, :]).astype(jnp.bfloat16)

    early = {0: slab}
    end_rows = take(slab, "end", jnp.zeros((8, 128), jnp.float32))
    later_rows = take(slab, "near", jnp.zeros((8, 128), jnp.float32))
    middle_rows = take(slab, "middle", jnp.zeros((8, 128), jnp.float32))
    near_rows = take(slab, "near", later_rows)
    early[-6] = move(end_rows, "wide", partner)
    early[12] = move(later_rows, "wide", outward)
    early[-4] = move(middle_rows, "wide", partner)
    near = move(near_rows, "wide", partner)
    early[6] = move(early[-6], "wide", outward)
    early[8] = move(early[-4], "wide", outward)
    early[-2] = near
    late = {10: move(near, "wide", outward)}
    from_partner = move(end_blocks(weight, near, early[6]), "wide", partner)

    dense = pieces_blocks(scaled, early, LONG)
    chunks = ((0, 1), (2, 5))

    parts = []
    after = scaled
    for pieces, chunk, ends in (({}, chunks[0], True), (late, chunks[1], False)):
        dense, send_far, send_near, keep_far, keep_near = choose_blocks(
            share, chunk, ends, places, scaled, from_partner, after, pieces, dense
        )
        got_far = move(send_far, "narrow", lambda n: n ^ 1)
        got_near = move(send_near, "narrow", lambda n: n ^ 1)
        parts.append((keep_near, got_near, move(add(keep_far, got_far, late[10]), "narrow", lambda n: n ^ 2)))
        after = got_far
    return finish(chunks, hold(total(*parts[0])), *parts[1])


def solution(mesh):
    placed = (P("wide", "narrow"), P(), P("narrow"), P("wide", None))
    return jax.shard_map(
        per_device,
        mesh=mesh,
        in_specs=placed,
        out_specs=P("wide", "narrow", None, None),
        check_vma=False,
    )
```

```python
import functools

import jax
import jax.numpy as jnp
from jax import lax
from jax.experimental import pallas as pl
from jax.experimental.pallas import tpu as pltpu
from jax.sharding import PartitionSpec as P

B = 128
REACH = 8
CL = 6
PAIR = 2
VMEM = pl.BlockSpec(memory_space=pltpu.VMEM)
SMEM = pl.BlockSpec(memory_space=pltpu.SMEM)
LIMIT = 40 * 1024 * 1024
LONG = pl.CostEstimate(flops=20 * 10**9, bytes_accessed=1, transcendentals=0)
SHORT = pl.CostEstimate(flops=1, bytes_accessed=1, transcendentals=0)


def move(value, axis, target):
    count = lax.axis_size(axis)
    return lax.ppermute(value, axis, [(s, target(s) % count) for s in range(count)])


def outward(w):
    return w + 2 if w % 2 == 0 else w - 2


def natural(low, high):
    odd = lax.rem(lax.axis_index("wide"), 2)
    return jnp.where(odd == 1, low, CL - 1 - high)


def multiply(left, right):
    product = lax.dot_general(left, right, (((1,), (1,)), ((), ())), preferred_element_type=jnp.float32)
    return product.astype(jnp.bfloat16)


def add_pieces(marks, pieces, left, dense):
    for piece, mark in zip(pieces, marks):
        count = piece.shape[0] // B
        for at in range(0, count, PAIR):
            low, high = mark + at, mark + at + PAIR - 1
            c0, c1 = max(0, low - REACH), min(CL - 1, high + REACH)
            offset, start, rows = natural(low, high), natural(c0, c1), (c1 - c0 + 1) * B
            row = pl.multiple_of((offset - natural(mark, mark + count - 1)) * B, PAIR * B)
            product = multiply(
                left[pl.ds(pl.multiple_of(start * B, B), rows), :], piece[pl.ds(row, PAIR * B), :]
            )
            for r in range(c1 - c0 + 1):
                for h in range(PAIR):
                    dense[start + r, offset + REACH + h] = product[r * B : (r + 1) * B, h * B : (h + 1) * B]


def pieces_kernel(marks, left, *refs):
    add_pieces(marks, refs[: len(marks)], left, refs[-1])


def pieces_blocks(left, pieces, cost, dense=None):
    held = [] if dense is None else [dense]
    return pl.pallas_call(
        functools.partial(pieces_kernel, list(pieces)),
        out_shape=jax.ShapeDtypeStruct((CL, CL + 2 * REACH, B, B), jnp.bfloat16),
        in_specs=[VMEM] * (1 + len(pieces) + len(held)),
        out_specs=VMEM,
        input_output_aliases={1 + len(pieces): 0} if held else {},
        compiler_params=pltpu.CompilerParams(vmem_limit_bytes=LIMIT),
        cost_estimate=cost,
        name="pieces_blocks",
    )(left, *pieces.values(), *held)


def ends_kernel(weight, near, far, out):
    odd = lax.rem(lax.axis_index("wide"), 2) == 1
    left = (near[...].astype(jnp.float32) * weight[...]).astype(jnp.bfloat16)
    product = multiply(left, far[...])
    for at, (c, m) in enumerate(((-1, 6), (-1, 7), (-2, 6))):
        here, there = ((c + 2) * B, (m - 6) * B), ((-1 - c) * B, (7 - m) * B)
        one, two = [product[row : row + B, column : column + B] for row, column in (here, there)]
        out[at] = jnp.where(odd, one, two)


def end_blocks(weight, near, far):
    return pl.pallas_call(
        ends_kernel,
        out_shape=jax.ShapeDtypeStruct((3, B, B), jnp.bfloat16),
        in_specs=[VMEM] * 3,
        out_specs=VMEM,
        compiler_params=pltpu.CompilerParams(vmem_limit_bytes=LIMIT),
        cost_estimate=SHORT,
        name="end_blocks",
    )(weight[None, :], near, far)


def choose_kernel(share, marks, chunk, ends, all_places, left, from_partner, after, *refs):
    dense = refs[len(marks) + 1]
    outs = refs[len(marks) + 2 : -2]
    places, done = refs[-2:]
    fetch = pltpu.make_async_copy(all_places, places, done)
    fetch.start()
    add_pieces(marks, refs[: len(marks)], left, dense)
    if ends:
        for at, (c, m) in enumerate(((0, -7), (0, -8), (1, -7))):
            dense[natural(c, c), natural(m, m) + REACH] = from_partner[at]
    fetch.wait()
    first, last = chunk
    start = natural(first, last)
    me = lax.axis_index("narrow")
    for out, mask in zip(outs, (3, 1, 2, 0)):
        slot0 = (me ^ mask) * share
        for c in range(last - first + 1):
            for s in range(share):
                out[c, s] = dense[start + c, places[start + c, slot0 + s]]


def choose_blocks(share, chunk, ends, places, left, from_partner, after, pieces, dense):
    shapes = [jax.ShapeDtypeStruct(dense.shape, dense.dtype)]
    shapes += [jax.ShapeDtypeStruct((chunk[1] - chunk[0] + 1, share, B, B), jnp.bfloat16)] * 4
    return pl.pallas_call(
        functools.partial(choose_kernel, share, list(pieces), chunk, ends),
        out_shape=shapes,
        in_specs=[VMEM] * (5 + len(pieces)),
        out_specs=[VMEM] * len(shapes),
        scratch_shapes=[pltpu.SMEM(places.shape, places.dtype), pltpu.SemaphoreType.DMA],
        input_output_aliases={4 + len(pieces): 0},
        compiler_params=pltpu.CompilerParams(vmem_limit_bytes=LIMIT),
        cost_estimate=SHORT,
        name="choose_blocks",
    )(places, left, from_partner, after, *pieces.values(), dense)


def add_kernel(x, y, out):
    out[...] = (x[...].astype(jnp.float32) + y[...].astype(jnp.float32)).astype(jnp.bfloat16)


def add(x, y):
    return pl.pallas_call(
        add_kernel,
        out_shape=jax.ShapeDtypeStruct(x.shape, x.dtype),
        in_specs=[VMEM] * 2,
        out_specs=VMEM,
        compiler_params=pltpu.CompilerParams(vmem_limit_bytes=LIMIT),
        cost_estimate=SHORT,
        name="add",
    )(x, y)


def total_kernel(near, got_near, got, out):
    total = near[...].astype(jnp.float32) + got_near[...].astype(jnp.float32) + got[...].astype(jnp.float32)
    out[...] = total.astype(jnp.bfloat16)


def total(near, got_near, got):
    return pl.pallas_call(
        total_kernel,
        out_shape=jax.ShapeDtypeStruct(near.shape, near.dtype),
        in_specs=[VMEM] * 3,
        out_specs=VMEM,
        compiler_params=pltpu.CompilerParams(vmem_limit_bytes=LIMIT),
        cost_estimate=LONG,
        name="total",
    )(near, got_near, got)


def finish_kernel(chunks, early, near, got_near, got, out, rows, done):
    start, later = [natural(first, last) for first, last in chunks]
    copies = []
    for r in range(early.shape[0]):
        copies.append(pltpu.make_async_copy(early.at[r], out.at[start + r], done.at[r]))
        copies[-1].start()
    for r in range(near.shape[0]):
        total = near[r].astype(jnp.float32) + got_near[r].astype(jnp.float32) + got[r].astype(jnp.float32)
        rows[r] = total.astype(jnp.bfloat16)
        copies.append(pltpu.make_async_copy(rows.at[r], out.at[later + r], done.at[early.shape[0] + r]))
        copies[-1].start()
    for copy in copies:
        copy.wait()


def finish(chunks, early, near, got_near, got):
    return pl.pallas_call(
        functools.partial(finish_kernel, chunks),
        out_shape=jax.ShapeDtypeStruct((CL,) + near.shape[1:], near.dtype),
        in_specs=[VMEM] * 4,
        out_specs=pl.BlockSpec(memory_space=pl.ANY),
        scratch_shapes=[pltpu.VMEM(near.shape, near.dtype), pltpu.SemaphoreType.DMA((CL,))],
        compiler_params=pltpu.CompilerParams(vmem_limit_bytes=LIMIT),
        cost_estimate=SHORT,
        name="finish",
    )(early, near, got_near, got)


def take_kernel(which, slab, after, out, done):
    odd = lax.rem(lax.axis_index("wide"), 2)
    row = {"end": odd * 2, "middle": 1, "near": (1 - odd) * 2}[which] * PAIR * B
    copy = pltpu.make_async_copy(slab.at[pl.ds(pl.multiple_of(row, PAIR * B), PAIR * B), :], out, done)
    copy.start()
    copy.wait()


def take(slab, which, after):
    return pl.pallas_call(
        functools.partial(take_kernel, which),
        out_shape=jax.ShapeDtypeStruct((PAIR * B, slab.shape[1]), slab.dtype),
        in_specs=[pl.BlockSpec(memory_space=pltpu.HBM), VMEM],
        out_specs=VMEM,
        scratch_shapes=[pltpu.SemaphoreType.DMA],
        compiler_params=pltpu.CompilerParams(vmem_limit_bytes=LIMIT),
        cost_estimate=SHORT,
        name=f"take_{which}",
    )(slab, after)


def per_device(slab, occupation, column_band, pattern):
    clusters = CL * lax.axis_size("wide")
    share = pattern.shape[1] // lax.axis_size("narrow")
    odd = lax.axis_index("wide") % 2
    rows = PAIR * B
    partner = lambda w: w ^ 1

    places = jnp.mod(pattern - (lax.axis_index("wide") * CL - REACH), clusters)
    picks = column_band[:, None] == jnp.arange(occupation.shape[0], dtype=jnp.int32)[None, :]
    weight = jnp.sum(jnp.where(picks, occupation[None, :], jnp.float32(0.0)), axis=1)
    scaled = (slab.astype(jnp.float32) * weight[None, :]).astype(jnp.bfloat16)

    early = {0: slab}
    end_rows = take(slab, "end", jnp.zeros((8, 128), jnp.float32))
    later_rows = take(slab, "near", jnp.zeros((8, 128), jnp.float32))
    middle_rows = take(slab, "middle", jnp.zeros((8, 128), jnp.float32))
    near_rows = take(slab, "near", later_rows)
    early[-6] = move(end_rows, "wide", partner)
    early[12] = move(later_rows, "wide", outward)
    early[-4] = move(middle_rows, "wide", partner)
    near = move(near_rows, "wide", partner)
    early[6] = move(early[-6], "wide", outward)
    early[8] = move(early[-4], "wide", outward)
    early[-2] = near
    late = {10: move(near, "wide", outward)}
    from_partner = move(end_blocks(weight, near, early[6]), "wide", partner)

    dense = pieces_blocks(scaled, early, LONG)
    chunks = ((0, 1), (2, 5))

    parts = []
    after = scaled
    for pieces, chunk, ends in (({}, chunks[0], True), (late, chunks[1], False)):
        dense, send_far, send_near, keep_far, keep_near = choose_blocks(
            share, chunk, ends, places, scaled, from_partner, after, pieces, dense
        )
        got_far = move(send_far, "narrow", lambda n: n ^ 1)
        got = move(add(keep_far, got_far), "narrow", lambda n: n ^ 2)
        got_near = move(send_near, "narrow", lambda n: n ^ 1)
        parts.append((keep_near, got_near, got))
        after = got_far
    return finish(chunks, total(*parts[0]), *parts[1])


def solution(mesh):
    placed = (P("wide", "narrow"), P(), P("narrow"), P("wide", None))
    return jax.shard_map(
        per_device,
        mesh=mesh,
        in_specs=placed,
        out_specs=P("wide", "narrow", None, None),
        check_vma=False,
    )
```

```python
import functools

import jax
import jax.numpy as jnp
from jax import lax
from jax.experimental import pallas as pl
from jax.experimental.pallas import tpu as pltpu
from jax.sharding import PartitionSpec as P

B = 128
REACH = 8
CL = 6
PAIR = 2
VMEM = pl.BlockSpec(memory_space=pltpu.VMEM)
SMEM = pl.BlockSpec(memory_space=pltpu.SMEM)
LIMIT = 40 * 1024 * 1024
LONG = pl.CostEstimate(flops=20 * 10**9, bytes_accessed=1, transcendentals=0)
SHORT = pl.CostEstimate(flops=1, bytes_accessed=1, transcendentals=0)


def move(value, axis, target):
    count = lax.axis_size(axis)
    return lax.ppermute(value, axis, [(s, target(s) % count) for s in range(count)])


def outward(w):
    return w + 2 if w % 2 == 0 else w - 2


def natural(low, high):
    odd = lax.rem(lax.axis_index("wide"), 2)
    return jnp.where(odd == 1, low, CL - 1 - high)


def multiply(left, right):
    product = lax.dot_general(left, right, (((1,), (1,)), ((), ())), preferred_element_type=jnp.float32)
    return product.astype(jnp.bfloat16)


def add_pieces(marks, pieces, left, dense):
    for piece, mark in zip(pieces, marks):
        count = piece.shape[0] // B
        for at in range(0, count, PAIR):
            low, high = mark + at, mark + at + PAIR - 1
            c0, c1 = max(0, low - REACH), min(CL - 1, high + REACH)
            offset, start, rows = natural(low, high), natural(c0, c1), (c1 - c0 + 1) * B
            row = pl.multiple_of((offset - natural(mark, mark + count - 1)) * B, PAIR * B)
            product = multiply(
                left[pl.ds(pl.multiple_of(start * B, B), rows), :], piece[pl.ds(row, PAIR * B), :]
            )
            for r in range(c1 - c0 + 1):
                for h in range(PAIR):
                    dense[start + r, offset + REACH + h] = product[r * B : (r + 1) * B, h * B : (h + 1) * B]


def pieces_kernel(marks, left, *refs):
    add_pieces(marks, refs[: len(marks)], left, refs[-1])


def pieces_blocks(left, pieces, cost, dense=None):
    held = [] if dense is None else [dense]
    return pl.pallas_call(
        functools.partial(pieces_kernel, list(pieces)),
        out_shape=jax.ShapeDtypeStruct((CL, CL + 2 * REACH, B, B), jnp.bfloat16),
        in_specs=[VMEM] * (1 + len(pieces) + len(held)),
        out_specs=VMEM,
        input_output_aliases={1 + len(pieces): 0} if held else {},
        compiler_params=pltpu.CompilerParams(vmem_limit_bytes=LIMIT),
        cost_estimate=cost,
        name="pieces_blocks",
    )(left, *pieces.values(), *held)


def ends_kernel(weight, near, far, out):
    odd = lax.rem(lax.axis_index("wide"), 2) == 1
    left = (near[...].astype(jnp.float32) * weight[...]).astype(jnp.bfloat16)
    product = multiply(left, far[...])
    for at, (c, m) in enumerate(((-1, 6), (-1, 7), (-2, 6))):
        here, there = ((c + 2) * B, (m - 6) * B), ((-1 - c) * B, (7 - m) * B)
        one, two = [product[row : row + B, column : column + B] for row, column in (here, there)]
        out[at] = jnp.where(odd, one, two)


def end_blocks(weight, near, far):
    return pl.pallas_call(
        ends_kernel,
        out_shape=jax.ShapeDtypeStruct((3, B, B), jnp.bfloat16),
        in_specs=[VMEM] * 3,
        out_specs=VMEM,
        compiler_params=pltpu.CompilerParams(vmem_limit_bytes=LIMIT),
        cost_estimate=SHORT,
        name="end_blocks",
    )(weight[None, :], near, far)


def choose_kernel(share, marks, chunk, ends, all_places, left, from_partner, after, *refs):
    dense = refs[len(marks) + 1]
    outs = refs[len(marks) + 2 : -2]
    places, done = refs[-2:]
    fetch = pltpu.make_async_copy(all_places, places, done)
    fetch.start()
    add_pieces(marks, refs[: len(marks)], left, dense)
    if ends:
        for at, (c, m) in enumerate(((0, -7), (0, -8), (1, -7))):
            dense[natural(c, c), natural(m, m) + REACH] = from_partner[at]
    fetch.wait()
    first, last = chunk
    start = natural(first, last)
    me = lax.axis_index("narrow")
    for out, mask in zip(outs, (3, 1, 2, 0)):
        slot0 = (me ^ mask) * share
        for c in range(last - first + 1):
            for s in range(share):
                out[c, s] = dense[start + c, places[start + c, slot0 + s]]


def choose_blocks(share, chunk, ends, places, left, from_partner, after, pieces, dense):
    shapes = [jax.ShapeDtypeStruct(dense.shape, dense.dtype)]
    shapes += [jax.ShapeDtypeStruct((chunk[1] - chunk[0] + 1, share, B, B), jnp.bfloat16)] * 4
    return pl.pallas_call(
        functools.partial(choose_kernel, share, list(pieces), chunk, ends),
        out_shape=shapes,
        in_specs=[VMEM] * (5 + len(pieces)),
        out_specs=[VMEM] * len(shapes),
        scratch_shapes=[pltpu.SMEM(places.shape, places.dtype), pltpu.SemaphoreType.DMA],
        input_output_aliases={4 + len(pieces): 0},
        compiler_params=pltpu.CompilerParams(vmem_limit_bytes=LIMIT),
        cost_estimate=SHORT,
        name="choose_blocks",
    )(places, left, from_partner, after, *pieces.values(), dense)


def add_kernel(x, y, out):
    out[...] = (x[...].astype(jnp.float32) + y[...].astype(jnp.float32)).astype(jnp.bfloat16)


def add(x, y):
    return pl.pallas_call(
        add_kernel,
        out_shape=jax.ShapeDtypeStruct(x.shape, x.dtype),
        in_specs=[VMEM] * 2,
        out_specs=VMEM,
        compiler_params=pltpu.CompilerParams(vmem_limit_bytes=LIMIT),
        cost_estimate=SHORT,
        name="add",
    )(x, y)


def total_kernel(near, got, out):
    out[...] = near[...].astype(jnp.float32) + got[...].astype(jnp.float32)


def total(near, got):
    return pl.pallas_call(
        total_kernel,
        out_shape=jax.ShapeDtypeStruct(near.shape, jnp.float32),
        in_specs=[VMEM] * 2,
        out_specs=VMEM,
        compiler_params=pltpu.CompilerParams(vmem_limit_bytes=LIMIT),
        cost_estimate=LONG,
        name="total",
    )(near, got)


def finish_kernel(chunks, early, got_early, near, got_near, got, out, rows, done):
    copies = []

    def write(chunk, r, total):
        at = len(copies)
        rows[at] = total.astype(jnp.bfloat16)
        copies.append(pltpu.make_async_copy(rows.at[at], out.at[natural(*chunk) + r], done.at[at]))
        copies[-1].start()

    for r in range(early.shape[0]):
        write(chunks[0], r, early[r] + got_early[r].astype(jnp.float32))
    for r in range(near.shape[0]):
        total = near[r].astype(jnp.float32) + got_near[r].astype(jnp.float32) + got[r].astype(jnp.float32)
        write(chunks[1], r, total)
    for copy in copies:
        copy.wait()


def finish(chunks, early, got_early, near, got_near, got):
    shape = (CL,) + near.shape[1:]
    return pl.pallas_call(
        functools.partial(finish_kernel, chunks),
        out_shape=jax.ShapeDtypeStruct(shape, near.dtype),
        in_specs=[VMEM] * 5,
        out_specs=pl.BlockSpec(memory_space=pl.ANY),
        scratch_shapes=[pltpu.VMEM(shape, near.dtype), pltpu.SemaphoreType.DMA((CL,))],
        compiler_params=pltpu.CompilerParams(vmem_limit_bytes=LIMIT),
        cost_estimate=SHORT,
        name="finish",
    )(early, got_early, near, got_near, got)


def take_kernel(which, slab, after, out, done):
    odd = lax.rem(lax.axis_index("wide"), 2)
    row = {"end": odd * 2, "middle": 1, "near": (1 - odd) * 2}[which] * PAIR * B
    copy = pltpu.make_async_copy(slab.at[pl.ds(pl.multiple_of(row, PAIR * B), PAIR * B), :], out, done)
    copy.start()
    copy.wait()


def take(slab, which, after):
    return pl.pallas_call(
        functools.partial(take_kernel, which),
        out_shape=jax.ShapeDtypeStruct((PAIR * B, slab.shape[1]), slab.dtype),
        in_specs=[pl.BlockSpec(memory_space=pltpu.HBM), VMEM],
        out_specs=VMEM,
        scratch_shapes=[pltpu.SemaphoreType.DMA],
        compiler_params=pltpu.CompilerParams(vmem_limit_bytes=LIMIT),
        cost_estimate=SHORT,
        name=f"take_{which}",
    )(slab, after)


def per_device(slab, occupation, column_band, pattern):
    clusters = CL * lax.axis_size("wide")
    share = pattern.shape[1] // lax.axis_size("narrow")
    odd = lax.axis_index("wide") % 2
    rows = PAIR * B
    partner = lambda w: w ^ 1

    places = jnp.mod(pattern - (lax.axis_index("wide") * CL - REACH), clusters)
    picks = column_band[:, None] == jnp.arange(occupation.shape[0], dtype=jnp.int32)[None, :]
    weight = jnp.sum(jnp.where(picks, occupation[None, :], jnp.float32(0.0)), axis=1)
    scaled = (slab.astype(jnp.float32) * weight[None, :]).astype(jnp.bfloat16)

    early = {0: slab}
    end_rows = take(slab, "end", jnp.zeros((8, 128), jnp.float32))
    later_rows = take(slab, "near", jnp.zeros((8, 128), jnp.float32))
    middle_rows = take(slab, "middle", jnp.zeros((8, 128), jnp.float32))
    near_rows = take(slab, "near", later_rows)
    early[-6] = move(end_rows, "wide", partner)
    early[12] = move(later_rows, "wide", outward)
    early[-4] = move(middle_rows, "wide", partner)
    near = move(near_rows, "wide", partner)
    early[6] = move(early[-6], "wide", outward)
    early[8] = move(early[-4], "wide", outward)
    early[-2] = near
    late = {10: move(near, "wide", outward)}
    from_partner = move(end_blocks(weight, near, early[6]), "wide", partner)

    dense = pieces_blocks(scaled, early, LONG)
    chunks = ((0, 1), (2, 5))

    parts = []
    after = scaled
    for pieces, chunk, ends in (({}, chunks[0], True), (late, chunks[1], False)):
        dense, send_far, send_near, keep_far, keep_near = choose_blocks(
            share, chunk, ends, places, scaled, from_partner, after, pieces, dense
        )
        got_far = move(send_far, "narrow", lambda n: n ^ 1)
        got = move(add(keep_far, got_far), "narrow", lambda n: n ^ 2)
        got_near = move(send_near, "narrow", lambda n: n ^ 1)
        parts.append((keep_near, got_near, got))
        after = got_far
    (near, got_near, got), later = parts
    return finish(chunks, total(near, got), got_near, *later)


def solution(mesh):
    placed = (P("wide", "narrow"), P(), P("narrow"), P("wide", None))
    return jax.shard_map(
        per_device,
        mesh=mesh,
        in_specs=placed,
        out_specs=P("wide", "narrow", None, None),
        check_vma=False,
    )
```

```python
import functools

import jax
import jax.numpy as jnp
from jax import lax
from jax.experimental import pallas as pl
from jax.experimental.pallas import tpu as pltpu
from jax.sharding import PartitionSpec as P

B = 128
REACH = 8
CL = 6
PAIR = 2
VMEM = pl.BlockSpec(memory_space=pltpu.VMEM)
SMEM = pl.BlockSpec(memory_space=pltpu.SMEM)
LIMIT = 40 * 1024 * 1024
LONG = pl.CostEstimate(flops=20 * 10**9, bytes_accessed=1, transcendentals=0)
SHORT = pl.CostEstimate(flops=1, bytes_accessed=1, transcendentals=0)


def move(value, axis, target):
    count = lax.axis_size(axis)
    return lax.ppermute(value, axis, [(s, target(s) % count) for s in range(count)])


def outward(w):
    return w + 2 if w % 2 == 0 else w - 2


def natural(low, high):
    odd = lax.rem(lax.axis_index("wide"), 2)
    return jnp.where(odd == 1, low, CL - 1 - high)


def multiply(left, right):
    product = lax.dot_general(left, right, (((1,), (1,)), ((), ())), preferred_element_type=jnp.float32)
    return product.astype(jnp.bfloat16)


def add_pieces(marks, pieces, left, dense):
    for piece, mark in zip(pieces, marks):
        count = piece.shape[0] // B
        for at in range(0, count, PAIR):
            low, high = mark + at, mark + at + PAIR - 1
            c0, c1 = max(0, low - REACH), min(CL - 1, high + REACH)
            offset, start, rows = natural(low, high), natural(c0, c1), (c1 - c0 + 1) * B
            row = pl.multiple_of((offset - natural(mark, mark + count - 1)) * B, PAIR * B)
            product = multiply(
                left[pl.ds(pl.multiple_of(start * B, B), rows), :], piece[pl.ds(row, PAIR * B), :]
            )
            for r in range(c1 - c0 + 1):
                for h in range(PAIR):
                    dense[start + r, offset + REACH + h] = product[r * B : (r + 1) * B, h * B : (h + 1) * B]


def pieces_kernel(marks, left, *refs):
    add_pieces(marks, refs[: len(marks)], left, refs[-1])


def pieces_blocks(left, pieces, cost, dense=None):
    held = [] if dense is None else [dense]
    return pl.pallas_call(
        functools.partial(pieces_kernel, list(pieces)),
        out_shape=jax.ShapeDtypeStruct((CL, CL + 2 * REACH, B, B), jnp.bfloat16),
        in_specs=[VMEM] * (1 + len(pieces) + len(held)),
        out_specs=VMEM,
        input_output_aliases={1 + len(pieces): 0} if held else {},
        compiler_params=pltpu.CompilerParams(vmem_limit_bytes=LIMIT),
        cost_estimate=cost,
        name="pieces_blocks",
    )(left, *pieces.values(), *held)


def ends_kernel(weight, near, far, out):
    odd = lax.rem(lax.axis_index("wide"), 2) == 1
    left = (near[...].astype(jnp.float32) * weight[...]).astype(jnp.bfloat16)
    product = multiply(left, far[...])
    for at, (c, m) in enumerate(((-1, 6), (-1, 7), (-2, 6))):
        here, there = ((c + 2) * B, (m - 6) * B), ((-1 - c) * B, (7 - m) * B)
        one, two = [product[row : row + B, column : column + B] for row, column in (here, there)]
        out[at] = jnp.where(odd, one, two)


def end_blocks(weight, near, far):
    return pl.pallas_call(
        ends_kernel,
        out_shape=jax.ShapeDtypeStruct((3, B, B), jnp.bfloat16),
        in_specs=[VMEM] * 3,
        out_specs=VMEM,
        compiler_params=pltpu.CompilerParams(vmem_limit_bytes=LIMIT),
        cost_estimate=SHORT,
        name="end_blocks",
    )(weight[None, :], near, far)


def choose_kernel(share, marks, shares, ends, all_places, left, from_partner, after, *refs):
    dense = refs[len(marks) + 1]
    outs = refs[len(marks) + 2 : -2]
    places, done = refs[-2:]
    fetch = pltpu.make_async_copy(all_places, places, done)
    fetch.start()
    add_pieces(marks, refs[: len(marks)], left, dense)
    if ends:
        for at, (c, m) in enumerate(((0, -7), (0, -8), (1, -7))):
            dense[natural(c, c), natural(m, m) + REACH] = from_partner[at]
    fetch.wait()
    me = lax.axis_index("narrow")
    for out, (mask, (first, last)) in zip(outs, shares):
        start, slot0 = natural(first, last), (me ^ mask) * share
        for c in range(last - first + 1):
            for s in range(share):
                out[c, s] = dense[start + c, places[start + c, slot0 + s]]


def choose_blocks(share, shares, ends, places, left, from_partner, after, pieces, dense):
    shapes = [jax.ShapeDtypeStruct(dense.shape, dense.dtype)]
    shapes += [jax.ShapeDtypeStruct((last - first + 1, share, B, B), jnp.bfloat16) for _, (first, last) in shares]
    return pl.pallas_call(
        functools.partial(choose_kernel, share, list(pieces), shares, ends),
        out_shape=shapes,
        in_specs=[VMEM] * (5 + len(pieces)),
        out_specs=[VMEM] * len(shapes),
        scratch_shapes=[pltpu.SMEM(places.shape, places.dtype), pltpu.SemaphoreType.DMA],
        input_output_aliases={4 + len(pieces): 0},
        compiler_params=pltpu.CompilerParams(vmem_limit_bytes=LIMIT),
        cost_estimate=SHORT,
        name="choose_blocks",
    )(places, left, from_partner, after, *pieces.values(), dense)


def add_kernel(x, y, out):
    out[...] = (x[...].astype(jnp.float32) + y[...].astype(jnp.float32)).astype(jnp.bfloat16)


def add(x, y):
    return pl.pallas_call(
        add_kernel,
        out_shape=jax.ShapeDtypeStruct(x.shape, x.dtype),
        in_specs=[VMEM] * 2,
        out_specs=VMEM,
        compiler_params=pltpu.CompilerParams(vmem_limit_bytes=LIMIT),
        cost_estimate=SHORT,
        name="add",
    )(x, y)


def total_kernel(chunk, near, got, out):
    start = natural(*chunk)
    for r in range(out.shape[0]):
        out[r] = near[start + r].astype(jnp.float32) + got[r].astype(jnp.float32)


def total(chunk, near, got):
    return pl.pallas_call(
        functools.partial(total_kernel, chunk),
        out_shape=jax.ShapeDtypeStruct(got.shape, jnp.float32),
        in_specs=[VMEM] * 2,
        out_specs=VMEM,
        compiler_params=pltpu.CompilerParams(vmem_limit_bytes=LIMIT),
        cost_estimate=LONG,
        name="total",
    )(near, got)


def finish_kernel(chunks, early, near, got_near, got, out, rows, done):
    copies = []

    def write(row, total):
        at = len(copies)
        rows[at] = total.astype(jnp.bfloat16)
        copies.append(pltpu.make_async_copy(rows.at[at], out.at[row], done.at[at]))
        copies[-1].start()

    start, later = [natural(*chunk) for chunk in chunks]
    for r in range(early.shape[0]):
        write(start + r, early[r] + got_near[start + r].astype(jnp.float32))
    for r in range(got.shape[0]):
        total = near[later + r].astype(jnp.float32) + got_near[later + r].astype(jnp.float32)
        write(later + r, total + got[r].astype(jnp.float32))
    for copy in copies:
        copy.wait()


def finish(chunks, early, near, got_near, got):
    return pl.pallas_call(
        functools.partial(finish_kernel, chunks),
        out_shape=jax.ShapeDtypeStruct(near.shape, near.dtype),
        in_specs=[VMEM] * 4,
        out_specs=pl.BlockSpec(memory_space=pl.ANY),
        scratch_shapes=[pltpu.VMEM(near.shape, near.dtype), pltpu.SemaphoreType.DMA((CL,))],
        compiler_params=pltpu.CompilerParams(vmem_limit_bytes=LIMIT),
        cost_estimate=SHORT,
        name="finish",
    )(early, near, got_near, got)


def take_kernel(which, slab, after, out, done):
    odd = lax.rem(lax.axis_index("wide"), 2)
    row = {"end": odd * 2, "middle": 1, "near": (1 - odd) * 2}[which] * PAIR * B
    copy = pltpu.make_async_copy(slab.at[pl.ds(pl.multiple_of(row, PAIR * B), PAIR * B), :], out, done)
    copy.start()
    copy.wait()


def take(slab, which, after):
    return pl.pallas_call(
        functools.partial(take_kernel, which),
        out_shape=jax.ShapeDtypeStruct((PAIR * B, slab.shape[1]), slab.dtype),
        in_specs=[pl.BlockSpec(memory_space=pltpu.HBM), VMEM],
        out_specs=VMEM,
        scratch_shapes=[pltpu.SemaphoreType.DMA],
        compiler_params=pltpu.CompilerParams(vmem_limit_bytes=LIMIT),
        cost_estimate=SHORT,
        name=f"take_{which}",
    )(slab, after)


def per_device(slab, occupation, column_band, pattern):
    clusters = CL * lax.axis_size("wide")
    share = pattern.shape[1] // lax.axis_size("narrow")
    odd = lax.axis_index("wide") % 2
    rows = PAIR * B
    partner = lambda w: w ^ 1

    places = jnp.mod(pattern - (lax.axis_index("wide") * CL - REACH), clusters)
    picks = column_band[:, None] == jnp.arange(occupation.shape[0], dtype=jnp.int32)[None, :]
    weight = jnp.sum(jnp.where(picks, occupation[None, :], jnp.float32(0.0)), axis=1)
    scaled = (slab.astype(jnp.float32) * weight[None, :]).astype(jnp.bfloat16)

    early = {0: slab}
    end_rows = take(slab, "end", jnp.zeros((8, 128), jnp.float32))
    later_rows = take(slab, "near", jnp.zeros((8, 128), jnp.float32))
    middle_rows = take(slab, "middle", jnp.zeros((8, 128), jnp.float32))
    near_rows = take(slab, "near", later_rows)
    early[-6] = move(end_rows, "wide", partner)
    early[12] = move(later_rows, "wide", outward)
    early[-4] = move(middle_rows, "wide", partner)
    near = move(near_rows, "wide", partner)
    early[6] = move(early[-6], "wide", outward)
    early[8] = move(early[-4], "wide", outward)
    early[-2] = near
    late = {10: move(near, "wide", outward)}
    from_partner = move(end_blocks(weight, near, early[6]), "wide", partner)

    dense = pieces_blocks(scaled, early, LONG)
    chunks = ((0, 1), (2, 5))

    after = scaled
    sums = []
    for pieces, chunk, ends in (({}, chunks[0], True), (late, chunks[1], False)):
        dense, send, keep = choose_blocks(
            share, [(3, chunk), (2, chunk)], ends, places, scaled, from_partner, after, pieces, dense
        )
        after = move(send, "narrow", lambda n: n ^ 1)
        sums.append(move(add(keep, after), "narrow", lambda n: n ^ 2))
    everyone = (0, CL - 1)
    _, send, near = choose_blocks(
        share, [(1, everyone), (0, everyone)], False, places, scaled, from_partner, scaled, {}, dense
    )
    got_near = move(send, "narrow", lambda n: n ^ 1)
    return finish(chunks, total(chunks[0], near, sums[0]), near, got_near, sums[1])


def solution(mesh):
    placed = (P("wide", "narrow"), P(), P("narrow"), P("wide", None))
    return jax.shard_map(
        per_device,
        mesh=mesh,
        in_specs=placed,
        out_specs=P("wide", "narrow", None, None),
        check_vma=False,
    )
```

```python
import functools

import jax
import jax.numpy as jnp
from jax import lax
from jax.experimental import pallas as pl
from jax.experimental.pallas import tpu as pltpu
from jax.sharding import PartitionSpec as P

B = 128
REACH = 8
CL = 6
PAIR = 2
VMEM = pl.BlockSpec(memory_space=pltpu.VMEM)
SMEM = pl.BlockSpec(memory_space=pltpu.SMEM)
LIMIT = 40 * 1024 * 1024
LONG = pl.CostEstimate(flops=20 * 10**9, bytes_accessed=1, transcendentals=0)
SHORT = pl.CostEstimate(flops=1, bytes_accessed=1, transcendentals=0)


def move(value, axis, target):
    count = lax.axis_size(axis)
    return lax.ppermute(value, axis, [(s, target(s) % count) for s in range(count)])


def outward(w):
    return w + 2 if w % 2 == 0 else w - 2


def natural(low, high):
    odd = lax.rem(lax.axis_index("wide"), 2)
    return jnp.where(odd == 1, low, CL - 1 - high)


def multiply(left, right):
    product = lax.dot_general(left, right, (((1,), (1,)), ((), ())), preferred_element_type=jnp.float32)
    return product.astype(jnp.bfloat16)


def add_pieces(marks, pieces, left, dense):
    for piece, mark in zip(pieces, marks):
        count = piece.shape[0] // B
        for at in range(0, count, PAIR):
            low, high = mark + at, mark + at + PAIR - 1
            c0, c1 = max(0, low - REACH), min(CL - 1, high + REACH)
            offset, start, rows = natural(low, high), natural(c0, c1), (c1 - c0 + 1) * B
            row = pl.multiple_of((offset - natural(mark, mark + count - 1)) * B, PAIR * B)
            product = multiply(
                left[pl.ds(pl.multiple_of(start * B, B), rows), :], piece[pl.ds(row, PAIR * B), :]
            )
            for r in range(c1 - c0 + 1):
                for h in range(PAIR):
                    dense[start + r, offset + REACH + h] = product[r * B : (r + 1) * B, h * B : (h + 1) * B]


def pieces_kernel(marks, left, *refs):
    add_pieces(marks, refs[: len(marks)], left, refs[-1])


def pieces_blocks(left, pieces, cost, dense=None):
    held = [] if dense is None else [dense]
    return pl.pallas_call(
        functools.partial(pieces_kernel, list(pieces)),
        out_shape=jax.ShapeDtypeStruct((CL, CL + 2 * REACH, B, B), jnp.bfloat16),
        in_specs=[VMEM] * (1 + len(pieces) + len(held)),
        out_specs=VMEM,
        input_output_aliases={1 + len(pieces): 0} if held else {},
        compiler_params=pltpu.CompilerParams(vmem_limit_bytes=LIMIT),
        cost_estimate=cost,
        name="pieces_blocks",
    )(left, *pieces.values(), *held)


def ends_kernel(weight, near, far, out):
    odd = lax.rem(lax.axis_index("wide"), 2) == 1
    left = (near[...].astype(jnp.float32) * weight[...]).astype(jnp.bfloat16)
    product = multiply(left, far[...])
    for at, (c, m) in enumerate(((-1, 6), (-1, 7), (-2, 6))):
        here, there = ((c + 2) * B, (m - 6) * B), ((-1 - c) * B, (7 - m) * B)
        one, two = [product[row : row + B, column : column + B] for row, column in (here, there)]
        out[at] = jnp.where(odd, one, two)


def end_blocks(weight, near, far):
    return pl.pallas_call(
        ends_kernel,
        out_shape=jax.ShapeDtypeStruct((3, B, B), jnp.bfloat16),
        in_specs=[VMEM] * 3,
        out_specs=VMEM,
        compiler_params=pltpu.CompilerParams(vmem_limit_bytes=LIMIT),
        cost_estimate=SHORT,
        name="end_blocks",
    )(weight[None, :], near, far)


def choose_kernel(share, marks, shares, ends, all_places, left, from_partner, after, *refs):
    dense = refs[len(marks) + 1]
    outs = refs[len(marks) + 2 : -2]
    places, done = refs[-2:]
    fetch = pltpu.make_async_copy(all_places, places, done)
    fetch.start()
    add_pieces(marks, refs[: len(marks)], left, dense)
    if ends:
        for at, (c, m) in enumerate(((0, -7), (0, -8), (1, -7))):
            dense[natural(c, c), natural(m, m) + REACH] = from_partner[at]
    fetch.wait()
    me = lax.axis_index("narrow")
    for out, (mask, (first, last)) in zip(outs, shares):
        start, slot0 = natural(first, last), (me ^ mask) * share
        for c in range(last - first + 1):
            for s in range(share):
                out[c, s] = dense[start + c, places[start + c, slot0 + s]]


def choose_blocks(share, shares, ends, places, left, from_partner, after, pieces, dense):
    shapes = [jax.ShapeDtypeStruct(dense.shape, dense.dtype)]
    shapes += [jax.ShapeDtypeStruct((last - first + 1, share, B, B), jnp.bfloat16) for _, (first, last) in shares]
    return pl.pallas_call(
        functools.partial(choose_kernel, share, list(pieces), shares, ends),
        out_shape=shapes,
        in_specs=[VMEM] * (5 + len(pieces)),
        out_specs=[VMEM] * len(shapes),
        scratch_shapes=[pltpu.SMEM(places.shape, places.dtype), pltpu.SemaphoreType.DMA],
        input_output_aliases={4 + len(pieces): 0},
        compiler_params=pltpu.CompilerParams(vmem_limit_bytes=LIMIT),
        cost_estimate=SHORT,
        name="choose_blocks",
    )(places, left, from_partner, after, *pieces.values(), dense)


def add_kernel(x, y, out):
    out[...] = (x[...].astype(jnp.float32) + y[...].astype(jnp.float32)).astype(jnp.bfloat16)


def add(x, y):
    return pl.pallas_call(
        add_kernel,
        out_shape=jax.ShapeDtypeStruct(x.shape, x.dtype),
        in_specs=[VMEM] * 2,
        out_specs=VMEM,
        compiler_params=pltpu.CompilerParams(vmem_limit_bytes=LIMIT),
        cost_estimate=SHORT,
        name="add",
    )(x, y)


def total_kernel(chunk, near, got, out):
    start = natural(*chunk)
    for r in range(out.shape[0]):
        out[r] = near[start + r].astype(jnp.float32) + got[r].astype(jnp.float32)


def total(chunk, near, got):
    return pl.pallas_call(
        functools.partial(total_kernel, chunk),
        out_shape=jax.ShapeDtypeStruct(got.shape, jnp.float32),
        in_specs=[VMEM] * 2,
        out_specs=VMEM,
        compiler_params=pltpu.CompilerParams(vmem_limit_bytes=LIMIT),
        cost_estimate=LONG,
        name="total",
    )(near, got)


def finish_kernel(chunks, early, near, got_near, got, out, rows, done):
    copies = []

    def write(row, total):
        at = len(copies)
        rows[at] = total.astype(jnp.bfloat16)
        copies.append(pltpu.make_async_copy(rows.at[at], out.at[row], done.at[at]))
        copies[-1].start()

    start, later = [natural(*chunk) for chunk in chunks]
    for r in range(early.shape[0]):
        write(start + r, early[r] + got_near[start + r].astype(jnp.float32))
    for r in range(got.shape[0]):
        total = near[later + r].astype(jnp.float32) + got_near[later + r].astype(jnp.float32)
        write(later + r, total + got[r].astype(jnp.float32))
    for copy in copies:
        copy.wait()


def finish(chunks, early, near, got_near, got):
    return pl.pallas_call(
        functools.partial(finish_kernel, chunks),
        out_shape=jax.ShapeDtypeStruct(near.shape, near.dtype),
        in_specs=[VMEM] * 4,
        out_specs=pl.BlockSpec(memory_space=pl.ANY),
        scratch_shapes=[pltpu.VMEM(near.shape, near.dtype), pltpu.SemaphoreType.DMA((CL,))],
        compiler_params=pltpu.CompilerParams(vmem_limit_bytes=LIMIT),
        cost_estimate=SHORT,
        name="finish",
    )(early, near, got_near, got)


def take_kernel(which, slab, *refs):
    out, done = refs[-2:]
    odd = lax.rem(lax.axis_index("wide"), 2)
    row = {"end": odd * 2, "middle": 1, "near": (1 - odd) * 2}[which] * PAIR * B
    copy = pltpu.make_async_copy(slab.at[pl.ds(pl.multiple_of(row, PAIR * B), PAIR * B), :], out, done)
    copy.start()
    copy.wait()


def take(slab, which, *after):
    return pl.pallas_call(
        functools.partial(take_kernel, which),
        out_shape=jax.ShapeDtypeStruct((PAIR * B, slab.shape[1]), slab.dtype),
        in_specs=[pl.BlockSpec(memory_space=pl.ANY)] + [VMEM] * len(after),
        out_specs=VMEM,
        scratch_shapes=[pltpu.SemaphoreType.DMA],
        compiler_params=pltpu.CompilerParams(vmem_limit_bytes=LIMIT),
        cost_estimate=SHORT,
        name=f"take_{which}",
    )(slab, *after)


def per_device(slab, occupation, column_band, pattern):
    clusters = CL * lax.axis_size("wide")
    share = pattern.shape[1] // lax.axis_size("narrow")
    odd = lax.axis_index("wide") % 2
    rows = PAIR * B
    partner = lambda w: w ^ 1

    places = jnp.mod(pattern - (lax.axis_index("wide") * CL - REACH), clusters)
    picks = column_band[:, None] == jnp.arange(occupation.shape[0], dtype=jnp.int32)[None, :]
    weight = jnp.sum(jnp.where(picks, occupation[None, :], jnp.float32(0.0)), axis=1)
    scaled = (slab.astype(jnp.float32) * weight[None, :]).astype(jnp.bfloat16)

    early = {0: slab}
    end_rows = take(slab, "end", jnp.zeros((8, 128), jnp.float32))
    middle_rows = take(slab, "middle", jnp.zeros((8, 128), jnp.float32))
    later_rows = take(slab, "near", end_rows)
    near_rows = take(slab, "near", later_rows, middle_rows)
    early[-6] = move(end_rows, "wide", partner)
    early[12] = move(later_rows, "wide", outward)
    early[-4] = move(middle_rows, "wide", partner)
    near = move(near_rows, "wide", partner)
    early[6] = move(early[-6], "wide", outward)
    early[8] = move(early[-4], "wide", outward)
    early[-2] = near
    late = {10: move(near, "wide", outward)}
    from_partner = move(end_blocks(weight, near, early[6]), "wide", partner)

    dense = pieces_blocks(scaled, early, LONG)
    chunks = ((0, 1), (2, 5))

    after = scaled
    sums = []
    for pieces, chunk, ends in (({}, chunks[0], True), (late, chunks[1], False)):
        dense, send, keep = choose_blocks(
            share, [(3, chunk), (2, chunk)], ends, places, scaled, from_partner, after, pieces, dense
        )
        after = move(send, "narrow", lambda n: n ^ 1)
        sums.append(move(add(keep, after), "narrow", lambda n: n ^ 2))
    everyone = (0, CL - 1)
    _, send, near = choose_blocks(
        share, [(1, everyone), (0, everyone)], False, places, scaled, from_partner, scaled, {}, dense
    )
    got_near = move(send, "narrow", lambda n: n ^ 1)
    return finish(chunks, total(chunks[0], near, sums[0]), near, got_near, sums[1])


def solution(mesh):
    placed = (P("wide", "narrow"), P(), P("narrow"), P("wide", None))
    return jax.shard_map(
        per_device,
        mesh=mesh,
        in_specs=placed,
        out_specs=P("wide", "narrow", None, None),
        check_vma=False,
    )
```

```python
import functools

import jax
import jax.numpy as jnp
from jax import lax
from jax.experimental import pallas as pl
from jax.experimental.pallas import tpu as pltpu
from jax.sharding import PartitionSpec as P

B = 128
REACH = 8
CL = 6
PAIR = 2
VMEM = pl.BlockSpec(memory_space=pltpu.VMEM)
SMEM = pl.BlockSpec(memory_space=pltpu.SMEM)
LIMIT = 40 * 1024 * 1024
LONG = pl.CostEstimate(flops=20 * 10**9, bytes_accessed=1, transcendentals=0)
SHORT = pl.CostEstimate(flops=1, bytes_accessed=1, transcendentals=0)


def move(value, axis, target):
    count = lax.axis_size(axis)
    return lax.ppermute(value, axis, [(s, target(s) % count) for s in range(count)])


def outward(w):
    return w + 2 if w % 2 == 0 else w - 2


def natural(low, high):
    odd = lax.rem(lax.axis_index("wide"), 2)
    return jnp.where(odd == 1, low, CL - 1 - high)


def multiply(left, right):
    product = lax.dot_general(left, right, (((1,), (1,)), ((), ())), preferred_element_type=jnp.float32)
    return product.astype(jnp.bfloat16)


def add_pieces(marks, pieces, left, dense):
    for piece, mark in zip(pieces, marks):
        count = piece.shape[0] // B
        for at in range(0, count, PAIR):
            low, high = mark + at, mark + at + PAIR - 1
            c0, c1 = max(0, low - REACH), min(CL - 1, high + REACH)
            offset, start, rows = natural(low, high), natural(c0, c1), (c1 - c0 + 1) * B
            row = pl.multiple_of((offset - natural(mark, mark + count - 1)) * B, PAIR * B)
            product = multiply(
                left[pl.ds(pl.multiple_of(start * B, B), rows), :], piece[pl.ds(row, PAIR * B), :]
            )
            for r in range(c1 - c0 + 1):
                for h in range(PAIR):
                    dense[start + r, offset + REACH + h] = product[r * B : (r + 1) * B, h * B : (h + 1) * B]


def pieces_kernel(marks, left, *refs):
    add_pieces(marks, refs[: len(marks)], left, refs[-1])


def pieces_blocks(left, pieces, cost, dense=None):
    held = [] if dense is None else [dense]
    return pl.pallas_call(
        functools.partial(pieces_kernel, list(pieces)),
        out_shape=jax.ShapeDtypeStruct((CL, CL + 2 * REACH, B, B), jnp.bfloat16),
        in_specs=[VMEM] * (1 + len(pieces) + len(held)),
        out_specs=VMEM,
        input_output_aliases={1 + len(pieces): 0} if held else {},
        compiler_params=pltpu.CompilerParams(vmem_limit_bytes=LIMIT),
        cost_estimate=cost,
        name="pieces_blocks",
    )(left, *pieces.values(), *held)


def ends_kernel(weight, near, far, out):
    odd = lax.rem(lax.axis_index("wide"), 2) == 1
    left = (near[...].astype(jnp.float32) * weight[...]).astype(jnp.bfloat16)
    product = multiply(left, far[...])
    for at, (c, m) in enumerate(((-1, 6), (-1, 7), (-2, 6))):
        here, there = ((c + 2) * B, (m - 6) * B), ((-1 - c) * B, (7 - m) * B)
        one, two = [product[row : row + B, column : column + B] for row, column in (here, there)]
        out[at] = jnp.where(odd, one, two)


def end_blocks(weight, near, far):
    return pl.pallas_call(
        ends_kernel,
        out_shape=jax.ShapeDtypeStruct((3, B, B), jnp.bfloat16),
        in_specs=[VMEM] * 3,
        out_specs=VMEM,
        compiler_params=pltpu.CompilerParams(vmem_limit_bytes=LIMIT),
        cost_estimate=SHORT,
        name="end_blocks",
    )(weight[None, :], near, far)


def choose_kernel(share, marks, shares, ends, all_places, left, from_partner, after, *refs):
    dense = refs[len(marks) + 1]
    outs = refs[len(marks) + 2 : -2]
    places, done = refs[-2:]
    fetch = pltpu.make_async_copy(all_places, places, done)
    fetch.start()
    add_pieces(marks, refs[: len(marks)], left, dense)
    if ends:
        for at, (c, m) in enumerate(((0, -7), (0, -8), (1, -7))):
            dense[natural(c, c), natural(m, m) + REACH] = from_partner[at]
    fetch.wait()
    me = lax.axis_index("narrow")
    for out, (mask, (first, last)) in zip(outs, shares):
        start, slot0 = natural(first, last), (me ^ mask) * share
        for c in range(last - first + 1):
            for s in range(share):
                out[c, s] = dense[start + c, places[start + c, slot0 + s]]


def choose_blocks(share, shares, ends, places, left, from_partner, after, pieces, dense):
    shapes = [jax.ShapeDtypeStruct(dense.shape, dense.dtype)]
    shapes += [jax.ShapeDtypeStruct((last - first + 1, share, B, B), jnp.bfloat16) for _, (first, last) in shares]
    return pl.pallas_call(
        functools.partial(choose_kernel, share, list(pieces), shares, ends),
        out_shape=shapes,
        in_specs=[VMEM] * (5 + len(pieces)),
        out_specs=[VMEM] * len(shapes),
        scratch_shapes=[pltpu.SMEM(places.shape, places.dtype), pltpu.SemaphoreType.DMA],
        input_output_aliases={4 + len(pieces): 0},
        compiler_params=pltpu.CompilerParams(vmem_limit_bytes=LIMIT),
        cost_estimate=SHORT,
        name="choose_blocks",
    )(places, left, from_partner, after, *pieces.values(), dense)


def add_kernel(x, y, out):
    out[...] = (x[...].astype(jnp.float32) + y[...].astype(jnp.float32)).astype(jnp.bfloat16)


def add(x, y):
    return pl.pallas_call(
        add_kernel,
        out_shape=jax.ShapeDtypeStruct(x.shape, x.dtype),
        in_specs=[VMEM] * 2,
        out_specs=VMEM,
        compiler_params=pltpu.CompilerParams(vmem_limit_bytes=LIMIT),
        cost_estimate=SHORT,
        name="add",
    )(x, y)


def total_kernel(chunk, near, got, out):
    start = natural(*chunk)
    for r in range(out.shape[0]):
        out[r] = near[start + r].astype(jnp.float32) + got[r].astype(jnp.float32)


def total(chunk, near, got):
    return pl.pallas_call(
        functools.partial(total_kernel, chunk),
        out_shape=jax.ShapeDtypeStruct(got.shape, jnp.float32),
        in_specs=[VMEM] * 2,
        out_specs=VMEM,
        compiler_params=pltpu.CompilerParams(vmem_limit_bytes=LIMIT),
        cost_estimate=LONG,
        name="total",
    )(near, got)


def complete_kernel(chunk, early, got_near, out):
    start = natural(*chunk)
    for r in range(early.shape[0]):
        out[r] = (early[r] + got_near[start + r].astype(jnp.float32)).astype(jnp.bfloat16)


def complete(chunk, early, got_near):
    return pl.pallas_call(
        functools.partial(complete_kernel, chunk),
        out_shape=jax.ShapeDtypeStruct(early.shape, got_near.dtype),
        in_specs=[VMEM] * 2,
        out_specs=VMEM,
        compiler_params=pltpu.CompilerParams(vmem_limit_bytes=LIMIT),
        cost_estimate=SHORT,
        name="complete",
    )(early, got_near)


def finish_kernel(chunks, early, near, got_near, got, out, rows, done):
    copies = []

    def write(row, rows_of):
        copies.append(pltpu.make_async_copy(rows_of, out.at[row], done.at[len(copies)]))
        copies[-1].start()

    start, later = [natural(*chunk) for chunk in chunks]
    for r in range(early.shape[0]):
        write(start + r, early.at[r])
    for r in range(got.shape[0]):
        total = near[later + r].astype(jnp.float32) + got_near[later + r].astype(jnp.float32)
        rows[r] = (total + got[r].astype(jnp.float32)).astype(jnp.bfloat16)
        write(later + r, rows.at[r])
    for copy in copies:
        copy.wait()


def finish(chunks, early, near, got_near, got):
    return pl.pallas_call(
        functools.partial(finish_kernel, chunks),
        out_shape=jax.ShapeDtypeStruct(near.shape, near.dtype),
        in_specs=[VMEM] * 4,
        out_specs=pl.BlockSpec(memory_space=pl.ANY),
        scratch_shapes=[pltpu.VMEM(near.shape, near.dtype), pltpu.SemaphoreType.DMA((CL,))],
        compiler_params=pltpu.CompilerParams(vmem_limit_bytes=LIMIT),
        cost_estimate=SHORT,
        name="finish",
    )(early, near, got_near, got)


def take_kernel(which, slab, *refs):
    out, done = refs[-2:]
    odd = lax.rem(lax.axis_index("wide"), 2)
    row = {"end": odd * 2, "middle": 1, "near": (1 - odd) * 2}[which] * PAIR * B
    copy = pltpu.make_async_copy(slab.at[pl.ds(pl.multiple_of(row, PAIR * B), PAIR * B), :], out, done)
    copy.start()
    copy.wait()


def take(slab, which, *after):
    return pl.pallas_call(
        functools.partial(take_kernel, which),
        out_shape=jax.ShapeDtypeStruct((PAIR * B, slab.shape[1]), slab.dtype),
        in_specs=[pl.BlockSpec(memory_space=pl.ANY)] + [VMEM] * len(after),
        out_specs=VMEM,
        scratch_shapes=[pltpu.SemaphoreType.DMA],
        compiler_params=pltpu.CompilerParams(vmem_limit_bytes=LIMIT),
        cost_estimate=SHORT,
        name=f"take_{which}",
    )(slab, *after)


def per_device(slab, occupation, column_band, pattern):
    clusters = CL * lax.axis_size("wide")
    share = pattern.shape[1] // lax.axis_size("narrow")
    odd = lax.axis_index("wide") % 2
    rows = PAIR * B
    partner = lambda w: w ^ 1

    places = jnp.mod(pattern - (lax.axis_index("wide") * CL - REACH), clusters)
    picks = column_band[:, None] == jnp.arange(occupation.shape[0], dtype=jnp.int32)[None, :]
    weight = jnp.sum(jnp.where(picks, occupation[None, :], jnp.float32(0.0)), axis=1)
    scaled = (slab.astype(jnp.float32) * weight[None, :]).astype(jnp.bfloat16)

    early = {0: slab}
    end_rows = take(slab, "end", jnp.zeros((8, 128), jnp.float32))
    middle_rows = take(slab, "middle", jnp.zeros((8, 128), jnp.float32))
    later_rows = take(slab, "near", end_rows)
    near_rows = take(slab, "near", later_rows, middle_rows)
    early[-6] = move(end_rows, "wide", partner)
    early[12] = move(later_rows, "wide", outward)
    early[-4] = move(middle_rows, "wide", partner)
    near = move(near_rows, "wide", partner)
    early[6] = move(early[-6], "wide", outward)
    early[8] = move(early[-4], "wide", outward)
    early[-2] = near
    late = {10: move(near, "wide", outward)}
    from_partner = move(end_blocks(weight, near, early[6]), "wide", partner)

    dense = pieces_blocks(scaled, early, LONG)
    chunks = ((0, 1), (2, 5))

    after = scaled
    sums = []
    for pieces, chunk, ends in (({}, chunks[0], True), (late, chunks[1], False)):
        dense, send, keep = choose_blocks(
            share, [(3, chunk), (2, chunk)], ends, places, scaled, from_partner, after, pieces, dense
        )
        after = move(send, "narrow", lambda n: n ^ 1)
        sums.append(move(add(keep, after), "narrow", lambda n: n ^ 2))
    everyone = (0, CL - 1)
    _, send, near = choose_blocks(
        share, [(1, everyone), (0, everyone)], False, places, scaled, from_partner, scaled, {}, dense
    )
    got_near = move(send, "narrow", lambda n: n ^ 1)
    early = complete(chunks[0], total(chunks[0], near, sums[0]), got_near)
    return finish(chunks, early, near, got_near, sums[1])


def solution(mesh):
    placed = (P("wide", "narrow"), P(), P("narrow"), P("wide", None))
    return jax.shard_map(
        per_device,
        mesh=mesh,
        in_specs=placed,
        out_specs=P("wide", "narrow", None, None),
        check_vma=False,
    )
```

```python
import functools

import jax
import jax.numpy as jnp
from jax import lax
from jax.experimental import pallas as pl
from jax.experimental.pallas import tpu as pltpu
from jax.sharding import PartitionSpec as P

B = 128
REACH = 8
CL = 6
PAIR = 2
VMEM = pl.BlockSpec(memory_space=pltpu.VMEM)
SMEM = pl.BlockSpec(memory_space=pltpu.SMEM)
LIMIT = 40 * 1024 * 1024
LONG = pl.CostEstimate(flops=20 * 10**9, bytes_accessed=1, transcendentals=0)
SHORT = pl.CostEstimate(flops=1, bytes_accessed=1, transcendentals=0)


def move(value, axis, target):
    count = lax.axis_size(axis)
    return lax.ppermute(value, axis, [(s, target(s) % count) for s in range(count)])


def outward(w):
    return w + 2 if w % 2 == 0 else w - 2


def natural(low, high):
    odd = lax.rem(lax.axis_index("wide"), 2)
    return jnp.where(odd == 1, low, CL - 1 - high)


def multiply(left, right):
    product = lax.dot_general(left, right, (((1,), (1,)), ((), ())), preferred_element_type=jnp.float32)
    return product.astype(jnp.bfloat16)


def add_pieces(marks, pieces, left, dense):
    for piece, mark in zip(pieces, marks):
        count = piece.shape[0] // B
        for at in range(0, count, PAIR):
            low, high = mark + at, mark + at + PAIR - 1
            c0, c1 = max(0, low - REACH), min(CL - 1, high + REACH)
            offset, start, rows = natural(low, high), natural(c0, c1), (c1 - c0 + 1) * B
            row = pl.multiple_of((offset - natural(mark, mark + count - 1)) * B, PAIR * B)
            product = multiply(
                left[pl.ds(pl.multiple_of(start * B, B), rows), :], piece[pl.ds(row, PAIR * B), :]
            )
            for r in range(c1 - c0 + 1):
                for h in range(PAIR):
                    dense[start + r, offset + REACH + h] = product[r * B : (r + 1) * B, h * B : (h + 1) * B]


def pieces_kernel(marks, left, *refs):
    add_pieces(marks, refs[: len(marks)], left, refs[-1])


def pieces_blocks(left, pieces, cost, dense=None):
    held = [] if dense is None else [dense]
    return pl.pallas_call(
        functools.partial(pieces_kernel, list(pieces)),
        out_shape=jax.ShapeDtypeStruct((CL, CL + 2 * REACH, B, B), jnp.bfloat16),
        in_specs=[VMEM] * (1 + len(pieces) + len(held)),
        out_specs=VMEM,
        input_output_aliases={1 + len(pieces): 0} if held else {},
        compiler_params=pltpu.CompilerParams(vmem_limit_bytes=LIMIT),
        cost_estimate=cost,
        name="pieces_blocks",
    )(left, *pieces.values(), *held)


def ends_kernel(weight, near, far, out):
    odd = lax.rem(lax.axis_index("wide"), 2) == 1
    left = (near[...].astype(jnp.float32) * weight[...]).astype(jnp.bfloat16)
    product = multiply(left, far[...])
    for at, (c, m) in enumerate(((-1, 6), (-1, 7), (-2, 6))):
        here, there = ((c + 2) * B, (m - 6) * B), ((-1 - c) * B, (7 - m) * B)
        one, two = [product[row : row + B, column : column + B] for row, column in (here, there)]
        out[at] = jnp.where(odd, one, two)


def end_blocks(weight, near, far):
    return pl.pallas_call(
        ends_kernel,
        out_shape=jax.ShapeDtypeStruct((3, B, B), jnp.bfloat16),
        in_specs=[VMEM] * 3,
        out_specs=VMEM,
        compiler_params=pltpu.CompilerParams(vmem_limit_bytes=LIMIT),
        cost_estimate=SHORT,
        name="end_blocks",
    )(weight[None, :], near, far)


def choose_kernel(share, marks, shares, ends, all_places, left, from_partner, after, *refs):
    dense = refs[len(marks) + 1]
    outs = refs[len(marks) + 2 : -2]
    places, done = refs[-2:]
    fetch = pltpu.make_async_copy(all_places, places, done)
    fetch.start()
    add_pieces(marks, refs[: len(marks)], left, dense)
    if ends:
        for at, (c, m) in enumerate(((0, -7), (0, -8), (1, -7))):
            dense[natural(c, c), natural(m, m) + REACH] = from_partner[at]
    fetch.wait()
    me = lax.axis_index("narrow")
    for out, (mask, (first, last)) in zip(outs, shares):
        start, slot0 = natural(first, last), (me ^ mask) * share
        for c in range(last - first + 1):
            for s in range(share):
                out[c, s] = dense[start + c, places[start + c, slot0 + s]]


def choose_blocks(share, shares, ends, places, left, from_partner, after, pieces, dense):
    shapes = [jax.ShapeDtypeStruct(dense.shape, dense.dtype)]
    shapes += [jax.ShapeDtypeStruct((last - first + 1, share, B, B), jnp.bfloat16) for _, (first, last) in shares]
    return pl.pallas_call(
        functools.partial(choose_kernel, share, list(pieces), shares, ends),
        out_shape=shapes,
        in_specs=[VMEM] * (5 + len(pieces)),
        out_specs=[VMEM] * len(shapes),
        scratch_shapes=[pltpu.SMEM(places.shape, places.dtype), pltpu.SemaphoreType.DMA],
        input_output_aliases={4 + len(pieces): 0},
        compiler_params=pltpu.CompilerParams(vmem_limit_bytes=LIMIT),
        cost_estimate=SHORT,
        name="choose_blocks",
    )(places, left, from_partner, after, *pieces.values(), dense)


def add_kernel(x, y, out):
    out[...] = (x[...].astype(jnp.float32) + y[...].astype(jnp.float32)).astype(jnp.bfloat16)


def add(x, y):
    return pl.pallas_call(
        add_kernel,
        out_shape=jax.ShapeDtypeStruct(x.shape, x.dtype),
        in_specs=[VMEM] * 2,
        out_specs=VMEM,
        compiler_params=pltpu.CompilerParams(vmem_limit_bytes=LIMIT),
        cost_estimate=SHORT,
        name="add",
    )(x, y)


def total_kernel(chunk, near, got, out):
    start = natural(*chunk)
    for r in range(out.shape[0]):
        out[r] = near[start + r].astype(jnp.float32) + got[r].astype(jnp.float32)


def total(chunk, near, got):
    return pl.pallas_call(
        functools.partial(total_kernel, chunk),
        out_shape=jax.ShapeDtypeStruct(got.shape, jnp.float32),
        in_specs=[VMEM] * 2,
        out_specs=VMEM,
        compiler_params=pltpu.CompilerParams(vmem_limit_bytes=LIMIT),
        cost_estimate=LONG,
        name="total",
    )(near, got)


def complete_kernel(chunk, early, got_near, out):
    start = natural(*chunk)
    for r in range(early.shape[0]):
        out[r] = (early[r] + got_near[start + r].astype(jnp.float32)).astype(jnp.bfloat16)


def complete(chunk, early, got_near):
    return pl.pallas_call(
        functools.partial(complete_kernel, chunk),
        out_shape=jax.ShapeDtypeStruct(early.shape, got_near.dtype),
        in_specs=[VMEM] * 2,
        out_specs=VMEM,
        compiler_params=pltpu.CompilerParams(vmem_limit_bytes=LIMIT),
        cost_estimate=SHORT,
        name="complete",
    )(early, got_near)


def finish_kernel(chunks, early, near, got_near, got, out, rows, done):
    copies = []

    def write(row, rows_of):
        copies.append(pltpu.make_async_copy(rows_of, out.at[row], done.at[len(copies)]))
        copies[-1].start()

    start, later = [natural(*chunk) for chunk in chunks]
    write(pl.ds(start, early.shape[0]), early)
    for r in range(got.shape[0]):
        total = near[later + r].astype(jnp.float32) + got_near[later + r].astype(jnp.float32)
        rows[r] = (total + got[r].astype(jnp.float32)).astype(jnp.bfloat16)
        if r % 2 == 1:
            write(pl.ds(later + r - 1, 2), rows.at[pl.ds(r - 1, 2)])
    for copy in copies:
        copy.wait()


def finish(chunks, early, near, got_near, got):
    return pl.pallas_call(
        functools.partial(finish_kernel, chunks),
        out_shape=jax.ShapeDtypeStruct(near.shape, near.dtype),
        in_specs=[VMEM] * 4,
        out_specs=pl.BlockSpec(memory_space=pl.ANY),
        scratch_shapes=[pltpu.VMEM(near.shape, near.dtype), pltpu.SemaphoreType.DMA((CL,))],
        compiler_params=pltpu.CompilerParams(vmem_limit_bytes=LIMIT),
        cost_estimate=SHORT,
        name="finish",
    )(early, near, got_near, got)


def take_kernel(which, slab, *refs):
    out, done = refs[-2:]
    odd = lax.rem(lax.axis_index("wide"), 2)
    row = {"end": odd * 2, "middle": 1, "near": (1 - odd) * 2}[which] * PAIR * B
    copy = pltpu.make_async_copy(slab.at[pl.ds(pl.multiple_of(row, PAIR * B), PAIR * B), :], out, done)
    copy.start()
    copy.wait()


def take(slab, which, *after):
    return pl.pallas_call(
        functools.partial(take_kernel, which),
        out_shape=jax.ShapeDtypeStruct((PAIR * B, slab.shape[1]), slab.dtype),
        in_specs=[pl.BlockSpec(memory_space=pl.ANY)] + [VMEM] * len(after),
        out_specs=VMEM,
        scratch_shapes=[pltpu.SemaphoreType.DMA],
        compiler_params=pltpu.CompilerParams(vmem_limit_bytes=LIMIT),
        cost_estimate=SHORT,
        name=f"take_{which}",
    )(slab, *after)


def per_device(slab, occupation, column_band, pattern):
    clusters = CL * lax.axis_size("wide")
    share = pattern.shape[1] // lax.axis_size("narrow")
    odd = lax.axis_index("wide") % 2
    rows = PAIR * B
    partner = lambda w: w ^ 1

    places = jnp.mod(pattern - (lax.axis_index("wide") * CL - REACH), clusters)
    picks = column_band[:, None] == jnp.arange(occupation.shape[0], dtype=jnp.int32)[None, :]
    weight = jnp.sum(jnp.where(picks, occupation[None, :], jnp.float32(0.0)), axis=1)
    scaled = (slab.astype(jnp.float32) * weight[None, :]).astype(jnp.bfloat16)

    early = {0: slab}
    end_rows = take(slab, "end", jnp.zeros((8, 128), jnp.float32))
    middle_rows = take(slab, "middle", jnp.zeros((8, 128), jnp.float32))
    later_rows = take(slab, "near", end_rows)
    near_rows = take(slab, "near", later_rows, middle_rows)
    early[-6] = move(end_rows, "wide", partner)
    early[12] = move(later_rows, "wide", outward)
    early[-4] = move(middle_rows, "wide", partner)
    near = move(near_rows, "wide", partner)
    early[6] = move(early[-6], "wide", outward)
    early[8] = move(early[-4], "wide", outward)
    early[-2] = near
    late = {10: move(near, "wide", outward)}
    from_partner = move(end_blocks(weight, near, early[6]), "wide", partner)

    dense = pieces_blocks(scaled, early, LONG)
    chunks = ((0, 1), (2, 5))

    after = scaled
    sums = []
    for pieces, chunk, ends in (({}, chunks[0], True), (late, chunks[1], False)):
        dense, send, keep = choose_blocks(
            share, [(3, chunk), (2, chunk)], ends, places, scaled, from_partner, after, pieces, dense
        )
        after = move(send, "narrow", lambda n: n ^ 1)
        sums.append(move(add(keep, after), "narrow", lambda n: n ^ 2))
    everyone = (0, CL - 1)
    _, send, near = choose_blocks(
        share, [(1, everyone), (0, everyone)], False, places, scaled, from_partner, scaled, {}, dense
    )
    got_near = move(send, "narrow", lambda n: n ^ 1)
    early = complete(chunks[0], total(chunks[0], near, sums[0]), got_near)
    return finish(chunks, early, near, got_near, sums[1])


def solution(mesh):
    placed = (P("wide", "narrow"), P(), P("narrow"), P("wide", None))
    return jax.shard_map(
        per_device,
        mesh=mesh,
        in_specs=placed,
        out_specs=P("wide", "narrow", None, None),
        check_vma=False,
    )
```
